32 devices in a mesh: dp: 2 (over y), row: 4 (over z), col: 4 (over x, core).
Axes of the slice: x: 2, y: 2, z: 4, core: 2. Of those that a mesh axis runs over, the one named last changes fastest.
Arguments:
- residual: bfloat16 [8192, 2048], P(('dp', 'col'), 'row'), may hold values from -6 to 6
- segments: int32 [8192], P(('dp', 'col')), may hold values from 0 to 127, never falling along the last dimension, each value on 1 to 512 neighbouring positions
- routes: int32 [8192, 8], P(('dp', 'col')), may hold values from 0 to 15, all different within a row; in each aligned block of 512 rows (0 to 511, 512 to 1023, ...) at most 320 rows name the same one
- norm_attention: float32 [2048], replicated, may hold values from 0.5 to 1.5
- query_weight: bfloat16 [2048, 4096], P('col', 'row'), may hold values from -0.125 to 0.125
- key_projection_matrix: bfloat16 [2048, 512], P('col'), may hold values from -0.125 to 0.125
- value_projection_matrix: bfloat16 [2048, 512], P('col'), may hold values from -0.125 to 0.125
- query_gain: float32 [128], replicated, may hold values from 0.5 to 1.5
- key_gain: float32 [128], replicated, may hold values from 0.5 to 1.5
- out_weight: bfloat16 [4096, 2048], P('row', 'col'), may hold values from -0.375 to 0.375
- norm_experts: float32 [2048], replicated, may hold values from 0.5 to 1.5
- router_weight: bfloat16 [2048, 16], replicated, may hold values from -0.0625 to 0.0625
- gate_weight: bfloat16 [16, 2048, 768], P(('row', 'col')), may hold values from -0.125 to 0.125
- up_weight: bfloat16 [16, 2048, 768], P(('row', 'col')), may hold values from -0.125 to 0.125
- down_weight: bfloat16 [16, 768, 2048], P(('row', 'col')), may hold values from -0.875 to 0.875
- grad_output: bfloat16 [8192, 2048], P(('dp', 'col'), 'row'), may hold values from -6 to 6
Outputs:
- output: bfloat16 [8192, 2048], P(('dp', 'col'), 'row')
- grad_residual: float32 [8192, 2048], P(('dp', 'col'), 'row')
- grad_norm_attention: float32 [2048], replicated
- grad_query: float32 [2048, 4096], P('col', 'row')
- grad_key: float32 [2048, 512], P('col')
- grad_value: float32 [2048, 512], P('col')
- grad_query_gain: float32 [128], replicated
- grad_key_gain: float32 [128], replicated
- grad_out_weight: float32 [4096, 2048], P('row', 'col')
- grad_norm_experts: float32 [2048], replicated
- grad_router: float32 [2048, 16], replicated
- grad_gate: float32 [16, 2048, 768], P(('row', 'col'))
- grad_up: float32 [16, 2048, 768], P(('row', 'col'))
- grad_down: float32 [16, 768, 2048], P(('row', 'col'))
The draws below stay inside these ranges and needn't reach their ends.
Inputs may be any that keep to these rules, and one draw needn't show every extreme that they name: `routes`: in each aligned block of 512 rows (the rows of one device's micro-batch) no expert is named by more than 320 rows; the 8 experts of a row differ. `segments`: document numbers never fall along the whole array; a document has 1 to 512 tokens.
All inputs are finite; a program needn't handle non-finite values.
Results may differ from the reference program's by a relative error of at most 0.017.
Values may be sent and summed in bfloat16 or wider, within the bound.
No kernel may reach another device: no remote copies, remote signals or barrier semaphores. Data moves between devices by JAX's collectives and lax.ppermute only.
A program may use at most 320 MiB of HBM per device.

```python
import math
import jax
import jax.numpy as jnp
import numpy as np
from jax import lax

MODEL_DIM = 2048
QUERY_HEADS = 32
KEY_VALUE_HEADS = 4
HEAD_DIM = 128
FF = 768
TOP = 8
SEQUENCE_TOKENS = 512
E = 16
MBT = 512
TOKENS = 8192
CAP = 320
DOCS = 128


def block_scale(stream_key, shape, cuts, smallest, top_value):
    loudness, own = 1.0, jax.random.fold_in(stream_key, 6)
    for dim, shards_of in cuts:
        steps = jnp.exp(jax.random.uniform(jax.random.fold_in(own, dim), (shards_of,), jnp.float32, smallest / len(cuts), top_value / len(cuts)))
        loudness = loudness * jnp.repeat(steps, shape[dim] // shards_of).reshape([-1 if axis == dim else 1 for axis in range(len(shape))])
    return loudness


def profile(count, total, limit, slope):
    portions = [(1 << 20) // math.isqrt(grade ** slope) + 1 for grade in range(2, count + 1)]
    surplus, counts = total - limit - (count - 1), [1] * (count - 1)
    while surplus > 0:
        free = [i for i in range(count - 1) if counts[i] < limit]
        pool, remaining = sum([portions[i] for i in free]), surplus
        for i in free:
            addition = min(limit - counts[i], max(1, remaining * portions[i] // pool), surplus)
            counts[i] = counts[i] + addition
            surplus = surplus - addition
    return np.array([limit] + counts)


def uneven_parts(own_key, count, total, limit, lean):
    if count == 2:
        one = jax.random.randint(own_key, (), max(1, total - limit), min(limit, total - 1) + 1)
        return jnp.stack([one, total - one])
    lengths = jnp.asarray(profile(count, total, limit, lean), jnp.int32)
    couples = (count - 1) // 2
    donor, receiver = lengths[1:1 + 2 * couples:2], lengths[2:2 + 2 * couples:2]
    slack = jnp.minimum(donor - 1, limit - receiver)
    moved = jax.random.randint(jax.random.fold_in(own_key, 1), (couples,), 0, 1 << 20) % (slack + 1)
    lengths = lengths.at[1:1 + 2 * couples:2].set(donor - moved).at[2:2 + 2 * couples:2].set(receiver + moved)
    return lengths[jax.random.permutation(jax.random.fold_in(own_key, 2), count)]


def assign_block(stream_key, own, number, rows, count, top, reach, slope):
    sequence = jax.random.permutation(stream_key, count)
    crowded, usual = load_shares(count, rows * top, reach, slope, True), load_shares(count, rows * top, reach, slope, False)
    places = jnp.arange(count)

    def named(tallies, turn):
        used = int((tallies > 0).sum())
        fixed = max(1, used // 4)
        shifted = fixed + (places - fixed + turn * (used - fixed)) % max(1, count - fixed)
        return jnp.zeros((count,), jnp.int32).at[sequence[jnp.where(places < fixed, places, shifted)]].set(jnp.asarray(tallies, jnp.int32))

    tallies = jnp.where(number % 4 == 0, named(crowded, number // 4), named(usual, number - number // 4 - 1))
    mixed = jax.random.permutation(jax.random.fold_in(own, 3), count)
    giver, receiver = mixed[0:count // 2 * 2:2], mixed[1:count // 2 * 2:2]
    room = jnp.minimum(tallies[giver] - 1, reach - tallies[receiver]) // 2
    room = jnp.where((giver == sequence[0]) | (receiver == sequence[0]) | (tallies[receiver] == 0), 0, jnp.maximum(room, 0))
    shifted = jax.random.randint(jax.random.fold_in(own, 4), (count // 2,), 0, 1 << 20) % (room + 1)
    tallies = tallies.at[giver].add(-shifted).at[receiver].add(shifted)
    items = jnp.searchsorted(jnp.cumsum(tallies), jnp.arange(rows * top), side="right").astype(jnp.int32)
    grid = items.reshape(top, rows).T
    grid = grid[jax.random.permutation(jax.random.fold_in(own, 1), rows)]
    turn = jax.random.randint(jax.random.fold_in(own, 2), (rows, 1), 0, top)
    return jnp.take_along_axis(grid, (jnp.arange(top)[None, :] + turn) % top, axis=1)


def load_shares(count, total, most, slope, full):
    loads = [(1 << 20) // math.isqrt(standing ** slope) + 1 for standing in range(1, count + 1)]
    largest = most if full else min(most, max(-(-total // count), total * loads[0] // sum(loads)))
    least = 1 if total - largest >= count - 1 else 0
    given, rest = [largest] + [least] * (count - 1), total - largest - least * (count - 1)
    while rest > 0:
        free = [i for i in range(1, count) if given[i] < largest] or [i for i in range(1, count) if given[i] < most]
        whole, remaining = sum([loads[i] for i in free]), rest
        for i in free:
            more = min(most - given[i], max(1, remaining * loads[i] // whole), rest)
            given[i] = given[i] + more
            rest = rest - more
    return np.array(given)


def gaussian(stream_key, extent, scale, most, cuts=(), kind=jnp.bfloat16):
    drawn = jax.random.normal(stream_key, extent, jnp.float32) * scale
    if len(cuts) > 0:
        drawn = block_scale(stream_key, extent, cuts, -0.22, 0.18) * drawn
    return jnp.clip(drawn, min=-most, max=most).astype(kind)


def setup_inputs(seed: int = 0) -> dict:
    seeds = jax.random.split(jax.random.key(seed), 17)
    residual = gaussian(seeds[0], (TOKENS, MODEL_DIM), 1.0, 6.0, ((0, 8), (1, 4)))
    segments = jnp.searchsorted(jnp.cumsum(uneven_parts(seeds[1], DOCS, TOKENS, SEQUENCE_TOKENS, 2)), jnp.arange(TOKENS), side="right").astype(jnp.int32)
    routes_keys = jax.random.split(jax.random.fold_in(seeds[2], 1), TOKENS // MBT)
    routes_turns = jax.random.permutation(jax.random.fold_in(seeds[2], 3), TOKENS // MBT)
    routes = jax.vmap(lambda own, number: assign_block(jax.random.fold_in(seeds[2], 2), own, number, MBT, E, TOP, CAP, 1))(routes_keys, routes_turns).reshape((TOKENS, TOP))
    norm_attention = jnp.clip(1.0 + 0.1 * jax.random.normal(seeds[3], (MODEL_DIM,), jnp.float32), 0.5, 1.5)
    query_weight = gaussian(seeds[4], (MODEL_DIM, QUERY_HEADS * HEAD_DIM), MODEL_DIM ** -0.5, 0.125, ((0, 4), (1, 4)))
    key_projection_matrix = gaussian(seeds[5], (MODEL_DIM, KEY_VALUE_HEADS * HEAD_DIM), MODEL_DIM ** -0.5, 0.125, ((0, 4),))
    value_projection_matrix = gaussian(seeds[6], (MODEL_DIM, KEY_VALUE_HEADS * HEAD_DIM), MODEL_DIM ** -0.5, 0.125, ((0, 4),))
    query_gain = jnp.clip(1.0 + 0.1 * jax.random.normal(seeds[7], (HEAD_DIM,), jnp.float32), 0.5, 1.5)
    key_gain = jnp.clip(1.0 + 0.1 * jax.random.normal(seeds[8], (HEAD_DIM,), jnp.float32), 0.5, 1.5)
    out_weight = gaussian(seeds[9], (QUERY_HEADS * HEAD_DIM, MODEL_DIM), (QUERY_HEADS * HEAD_DIM // 16) ** -0.5, 0.375, ((0, 4), (1, 4)))
    norm_experts = jnp.clip(1.0 + 0.1 * jax.random.normal(seeds[10], (MODEL_DIM,), jnp.float32), 0.5, 1.5)
    router_weight = gaussian(seeds[11], (MODEL_DIM, E), (4 * MODEL_DIM) ** -0.5, 0.0625)
    gate_weight = gaussian(seeds[12], (E, MODEL_DIM, FF), MODEL_DIM ** -0.5, 0.125, ((0, 16),))
    up_weight = gaussian(seeds[13], (E, MODEL_DIM, FF), MODEL_DIM ** -0.5, 0.125, ((0, 16),))
    down_weight = gaussian(seeds[14], (E, FF, MODEL_DIM), (FF // 16) ** -0.5, 0.875, ((0, 16),))
    grad_output = gaussian(seeds[15], (TOKENS, MODEL_DIM), 1.0, 6.0, ((0, 8), (1, 4)))
    return {"residual": residual, "segments": segments, "routes": routes, "norm_attention": norm_attention, "query_weight": query_weight, "key_projection_matrix": key_projection_matrix, "value_projection_matrix": value_projection_matrix, "query_gain": query_gain, "key_gain": key_gain, "out_weight": out_weight, "norm_experts": norm_experts, "router_weight": router_weight, "gate_weight": gate_weight, "up_weight": up_weight, "down_weight": down_weight, "grad_output": grad_output}


@jax.custom_vjp
def reduced_precision(v):
    return lax.optimization_barrier(v.astype(jnp.bfloat16)).astype(jnp.float32)

@jax.custom_vjp
def reduced_precision_backward(v):
    return v

def low_keep(v):
    return (reduced_precision(v), None)

def low_pass(kept, grad):
    return (grad,)

def back_keep(v):
    return (v, None)

def back_low(kept, grad):
    return (reduced_precision(grad),)
reduced_precision.defvjp(low_keep, low_pass)
reduced_precision_backward.defvjp(back_keep, back_low)
EPSILON = 1e-06
ROPE_BASE = 1000000.0
MASKED = -1e+30
HIGHEST = lax.Precision.HIGHEST

def matrix_product(operand, weights):
    return jnp.dot(operand, weights, precision=HIGHEST, preferred_element_type=jnp.float32)

def rms_scale(values, gain):
    return values * lax.rsqrt(lax.optimization_barrier(jnp.mean(values * values, axis=-1, keepdims=True)) + EPSILON) * gain

def positions(segment_ids):
    places = jnp.arange(segment_ids.shape[0], dtype=jnp.int32)
    earlier = jnp.concatenate([segment_ids[:1] - 1, segment_ids[:-1]])
    starts = jnp.logical_or(segment_ids != earlier, places % SEQUENCE_TOKENS == 0)
    opening = lax.cummax(jnp.where(starts, places, 0), axis=0)
    return places - opening

def rotary(places, head_size):
    halfway = head_size // 2
    frequency = ROPE_BASE ** (-2.0 * jnp.arange(halfway, dtype=jnp.float32) / head_size)
    angles = places.astype(jnp.float32)[:, None] * frequency[None, :]
    return (jnp.cos(angles), jnp.sin(angles))

def rotate(values, cos_table, sin_table):
    halfway = values.shape[-1] // 2
    front_part = values[..., :halfway]
    back_part = values[..., halfway:]
    cos_wide = cos_table[:, None, :]
    sin_wide = sin_table[:, None, :]
    return jnp.concatenate([front_part * cos_wide - back_part * sin_wide, back_part * cos_wide + front_part * sin_wide], axis=-1)

def slot_ranks(routes, experts):
    token_rows, chosen = routes.shape
    labels = jnp.arange(experts, dtype=jnp.int32)
    onehot = (routes.reshape(-1)[:, None] == labels[None, :]).astype(jnp.int32)
    before = jnp.cumsum(onehot, axis=0, dtype=jnp.int32) - onehot
    return lax.optimization_barrier(jnp.sum(before * onehot, axis=1, dtype=jnp.int32)).reshape(token_rows, chosen)

def attend_packed_sequence(pieces):
    query_rows_matrix, key_row_matrix, value_row_matrix, segment_ids = pieces
    query_group_width = QUERY_HEADS // KEY_VALUE_HEADS
    key_row_matrix = jnp.repeat(key_row_matrix, query_group_width, axis=1)
    value_row_matrix = jnp.repeat(value_row_matrix, query_group_width, axis=1)
    scores = reduced_precision_backward(jnp.einsum('qhd,khd->hqk', query_rows_matrix, key_row_matrix, precision=HIGHEST) * HEAD_DIM ** (-0.5))
    places = jnp.arange(SEQUENCE_TOKENS, dtype=jnp.int32)
    allowed = jnp.logical_and(segment_ids[:, None] == segment_ids[None, :], places[None, :] <= places[:, None])
    scores = jnp.where(allowed[None], scores, MASKED)
    top_score = lax.optimization_barrier(jnp.max(scores, axis=-1, keepdims=True))
    weights = jnp.exp(scores - top_score)
    probs = reduced_precision(weights / lax.optimization_barrier(jnp.sum(weights, axis=-1, keepdims=True)))
    return jnp.einsum('hqk,khd->qhd', probs, value_row_matrix, precision=HIGHEST)

def expert_block(pieces, gate_weight, up_weight, down_weight):
    normed, routes, gates = pieces
    experts = gate_weight.shape[0]
    ranks = slot_ranks(routes, experts)
    slots = routes * CAP + ranks
    token_ids = jnp.broadcast_to(jnp.arange(MBT, dtype=jnp.int32)[:, None], routes.shape)
    source = jnp.full((experts * CAP,), MBT, dtype=jnp.int32).at[slots.reshape(-1)].set(token_ids.reshape(-1))
    padded = jnp.concatenate([normed, jnp.zeros((1, normed.shape[1]), jnp.float32)], axis=0)
    slot_inputs = reduced_precision_backward(padded[source]).reshape(experts, CAP, normed.shape[1])
    gate_pre = reduced_precision_backward(jnp.einsum('esd,edf->esf', slot_inputs, gate_weight, precision=HIGHEST))
    up_pre = reduced_precision_backward(jnp.einsum('esd,edf->esf', slot_inputs, up_weight, precision=HIGHEST))
    hidden = reduced_precision_backward(reduced_precision(gate_pre * jax.nn.sigmoid(gate_pre) * up_pre))
    result = reduced_precision_backward(reduced_precision(jnp.einsum('esf,efd->esd', hidden, down_weight, precision=HIGHEST)))
    result = result.reshape(experts * CAP, normed.shape[1])
    return lax.optimization_barrier(jnp.sum(gates[:, :, None] * result[slots], axis=1))

def forward(residual, norm_attention, query_weight, key_projection_matrix, value_projection_matrix, query_gain, key_gain, out_weight, norm_experts, router_weight, gate_weight, up_weight, down_weight, routes, segments):
    total_token_count = residual.shape[0]
    model_width = residual.shape[1]
    first_normalized = reduced_precision(rms_scale(residual, norm_attention))
    query_rows_matrix = reduced_precision_backward(matrix_product(first_normalized, query_weight)).reshape(total_token_count, QUERY_HEADS, HEAD_DIM)
    key_row_matrix = reduced_precision_backward(matrix_product(first_normalized, key_projection_matrix)).reshape(total_token_count, KEY_VALUE_HEADS, HEAD_DIM)
    value_row_matrix = reduced_precision_backward(reduced_precision(matrix_product(first_normalized, value_projection_matrix))).reshape(total_token_count, KEY_VALUE_HEADS, HEAD_DIM)
    cos_table, sin_table = rotary(positions(segments), HEAD_DIM)
    query_rows_matrix = reduced_precision(rotate(rms_scale(query_rows_matrix, query_gain), cos_table, sin_table))
    key_row_matrix = reduced_precision(rotate(rms_scale(key_row_matrix, key_gain), cos_table, sin_table))
    sequence_count = total_token_count // SEQUENCE_TOKENS
    expert_mixture_output = lax.map(jax.checkpoint(attend_packed_sequence), (query_rows_matrix.reshape(sequence_count, SEQUENCE_TOKENS, QUERY_HEADS, HEAD_DIM), key_row_matrix.reshape(sequence_count, SEQUENCE_TOKENS, KEY_VALUE_HEADS, HEAD_DIM), value_row_matrix.reshape(sequence_count, SEQUENCE_TOKENS, KEY_VALUE_HEADS, HEAD_DIM), segments.reshape(sequence_count, SEQUENCE_TOKENS)))
    expert_mixture_output = reduced_precision_backward(reduced_precision(expert_mixture_output.reshape(total_token_count, QUERY_HEADS * HEAD_DIM)))
    hidden = residual + reduced_precision_backward(matrix_product(expert_mixture_output, out_weight))
    normed_two = reduced_precision(rms_scale(hidden, norm_experts))
    logits = reduced_precision_backward(matrix_product(normed_two, router_weight))
    picked = jnp.take_along_axis(logits, routes, axis=1)
    picked = jnp.exp(picked - lax.optimization_barrier(jnp.max(picked, axis=1, keepdims=True)))
    gates = picked / lax.optimization_barrier(jnp.sum(picked, axis=1, keepdims=True))
    block_count = total_token_count // MBT

    def run_block(pieces):
        return expert_block(pieces, gate_weight, up_weight, down_weight)
    mixture = lax.map(jax.checkpoint(run_block), (normed_two.reshape(block_count, MBT, model_width), routes.reshape(block_count, MBT, TOP), gates.reshape(block_count, MBT, TOP)))
    return hidden + mixture.reshape(total_token_count, model_width)

def reference(residual, segments, routes, norm_attention, query_weight, key_projection_matrix, value_projection_matrix, query_gain, key_gain, out_weight, norm_experts, router_weight, gate_weight, up_weight, down_weight, grad_output):
    floats = (residual.astype(jnp.float32), norm_attention.astype(jnp.float32), query_weight.astype(jnp.float32), key_projection_matrix.astype(jnp.float32), value_projection_matrix.astype(jnp.float32), query_gain.astype(jnp.float32), key_gain.astype(jnp.float32), out_weight.astype(jnp.float32), norm_experts.astype(jnp.float32), router_weight.astype(jnp.float32), gate_weight.astype(jnp.float32), up_weight.astype(jnp.float32), down_weight.astype(jnp.float32))

    def closed(*params):
        return forward(*params, routes, segments)
    result, pullback = jax.vjp(closed, *floats)
    gradients = pullback(grad_output.astype(jnp.float32))
    return (result.astype(jnp.bfloat16), gradients[0], gradients[1], gradients[2], gradients[3], gradients[4], gradients[5], gradients[6], gradients[7], gradients[8], gradients[9], gradients[10], gradients[11], gradients[12])
```

```python
import jax
import jax.numpy as jnp
from jax import lax
from jax.sharding import PartitionSpec as P

SEQUENCE_TOKENS = 512
EPSILON = 1e-06
ROPE_BASE = 1000000.0
MASKED = -1e30
BF16 = jnp.bfloat16
F32 = jnp.float32


def dot(left, right):
    return jnp.dot(left, right, preferred_element_type=F32)


def moved(block, axis, by):
    count = lax.axis_size(axis)
    return lax.ppermute(block, axis, [(i, (i + by) % count) for i in range(count)])


def swapped(block, axis, bit):
    count = lax.axis_size(axis)
    return lax.ppermute(block, axis, [(i, i ^ (1 << bit)) for i in range(count)])


def butterfly(values, axis):
    for bit in range(lax.axis_size(axis).bit_length() - 1):
        values = values + swapped(values, axis, bit)
    return values


def ring_pieces(block):
    count = lax.axis_size("row")
    pieces = [block] + [None] * (count - 1)
    from_left = from_right = block
    half = block.shape[0] // 2
    for step in range(1, count // 2):
        from_left = moved(from_left, "row", 1)
        from_right = moved(from_right, "row", -1)
        pieces[count - step] = from_left
        pieces[step] = from_right
    if count > 1:
        pieces[count // 2] = jnp.concatenate(
            [moved(from_left[:half], "row", 1), moved(from_right[half:], "row", -1)], axis=0
        )
    return pieces


def ring_gather(block):
    count = lax.axis_size("row")
    place = lax.axis_index("row")
    width = block.shape[-1]
    whole = jnp.zeros(block.shape[:-1] + (width * count,), block.dtype)
    for distance, piece in enumerate(ring_pieces(block)):
        start = (place + distance) % count * width
        whole = lax.dynamic_update_slice_in_dim(whole, piece, start, block.ndim - 1)
    return whole


def ring_scatter(partial):
    count = lax.axis_size("row")
    place = lax.axis_index("row")
    width = partial.shape[1] // count
    half = partial.shape[0] // 2

    def piece(distance):
        start = (place + distance) % count * width
        return lax.dynamic_slice_in_dim(partial, start, width, 1)

    total = piece(0).astype(F32)
    if count == 1:
        return total
    middle = piece(count // 2)
    to_right = moved(middle[:half], "row", 1)
    to_left = moved(middle[half:], "row", -1)
    for step in range(count // 2 - 1, 0, -1):
        right, left = piece(step), piece(count - step)
        if step == count // 2 - 1:
            right = jnp.concatenate([right[:half] + to_right, right[half:]], axis=0)
            left = jnp.concatenate([left[:half], left[half:] + to_left], axis=0)
        else:
            right = right + to_right
            left = left + to_left
        to_right = moved(right, "row", 1)
        to_left = moved(left, "row", -1)
    if count == 2:
        return total + jnp.concatenate([to_right, to_left], axis=0).astype(F32)
    return total + to_right.astype(F32) + to_left.astype(F32)


def col_gather(block):
    count = lax.axis_size("col")
    pieces = []
    for step in range(count // 2):
        same = block if step == 0 else moved(block, "col", 2 * step)
        pieces += [same, swapped(same, "col", 0)]
    return pieces


def col_scatter(pieces):
    count = lax.axis_size("col")
    total = None
    for step in range(count // 2 - 1, -1, -1):
        here = pieces[2 * step].astype(F32) + swapped(pieces[2 * step + 1], "col", 0).astype(F32)
        if step > 0:
            here = moved(here.astype(pieces[0].dtype), "col", -2 * step).astype(F32)
        total = here if total is None else total + here
    return total


def col_order():
    count = lax.axis_size("col")
    place = lax.axis_index("col")
    chip, core = place // 2, place % 2
    order = []
    for step in range(count // 2):
        back = (chip - step) % (count // 2) * 2
        order += [back + core, back + 1 - core]
    return order


def col_assemble(block, axis):
    count = lax.axis_size("col")
    width = block.shape[axis]
    shape = list(block.shape)
    shape[axis] = width * count
    whole = jnp.zeros(shape, block.dtype)
    for piece, place in zip(col_gather(block), col_order()):
        whole = lax.dynamic_update_slice_in_dim(whole, piece, place * width, axis)
    return whole


def col_share(partial, axis):
    width = partial.shape[axis] // lax.axis_size("col")
    return col_scatter(
        [lax.dynamic_slice_in_dim(partial, place * width, width, axis) for place in col_order()]
    )


def pair_total(values):
    low = values.astype(BF16)
    total = low.astype(F32)
    for bit in range(lax.axis_size("dp").bit_length() - 1):
        total = total + swapped(low, "dp", bit).astype(F32)
        low = total.astype(BF16)
    return total


def rms_factor(values):
    return lax.rsqrt(jnp.mean(values * values, axis=-1, keepdims=True) + EPSILON)


def rms_back(values, gain, upstream):
    factor = rms_factor(values)
    weighted = upstream * gain
    inner_sum = jnp.mean(weighted * values, axis=-1, keepdims=True)
    return (
        weighted * factor - values * (factor * factor * factor * inner_sum),
        upstream * values * factor,
    )


def positions(segment_ids):
    places = jnp.arange(segment_ids.shape[0], dtype=jnp.int32)
    earlier = jnp.concatenate([segment_ids[:1] - 1, segment_ids[:-1]])
    starts = jnp.logical_or(segment_ids != earlier, places % SEQUENCE_TOKENS == 0)
    opening = lax.cummax(jnp.where(starts, places, 0), axis=0)
    return places - opening


def rotary(places, head_size):
    halfway = head_size // 2
    frequency = ROPE_BASE ** (-2.0 * jnp.arange(halfway, dtype=F32) / head_size)
    angles = places.astype(F32)[:, None] * frequency[None, :]
    return (jnp.cos(angles), jnp.sin(angles))


def rotate(values, cos_table, sin_table):
    halfway = values.shape[-1] // 2
    front, back = values[..., :halfway], values[..., halfway:]
    cos_wide, sin_wide = cos_table[:, None, :], sin_table[:, None, :]
    return jnp.concatenate(
        [front * cos_wide - back * sin_wide, back * cos_wide + front * sin_wide], axis=-1
    )


def unrotate(upstream, cos_table, sin_table):
    return rotate(upstream, cos_table, -sin_table)


def sequence_scores(query_low, key_low, segment_ids, score_scale):
    scores = jnp.einsum("qhd,kd->hqk", query_low, key_low, preferred_element_type=F32) * score_scale
    places = jnp.arange(segment_ids.shape[0], dtype=jnp.int32)
    allowed = jnp.logical_and(
        segment_ids[:, None] == segment_ids[None, :], places[None, :] <= places[:, None]
    )
    return jnp.where(allowed[None], scores, MASKED)


def attention_forward(query_low, key_low, value_low, segment_ids, score_scale):
    scores = sequence_scores(query_low, key_low, segment_ids, score_scale)
    top_score = jnp.max(scores, axis=-1, keepdims=True)
    weights = jnp.exp(scores - top_score)
    denominator = jnp.sum(weights, axis=-1, keepdims=True)
    probs_low = (weights / denominator).astype(BF16)
    mixed = jnp.einsum("hqk,kd->qhd", probs_low, value_low, preferred_element_type=F32)
    return mixed, (top_score + jnp.log(denominator))[..., 0]


def attention_backward(
    query_low, key_low, value_low, segment_ids, log_totals, mixed_grad, score_scale
):
    scores = sequence_scores(query_low, key_low, segment_ids, score_scale)
    probs = jnp.exp(scores - log_totals[:, :, None])
    probs_low = probs.astype(BF16)
    prob_grad = jnp.einsum("qhd,kd->hqk", mixed_grad, value_low, preferred_element_type=F32)
    score_grad = (
        probs * (prob_grad - jnp.sum(probs * prob_grad, axis=-1, keepdims=True))
    ).astype(BF16)
    query_grad = (
        jnp.einsum("hqk,kd->qhd", score_grad, key_low, preferred_element_type=F32) * score_scale
    )
    key_grad = (
        jnp.einsum("hqk,qhd->kd", score_grad, query_low, preferred_element_type=F32) * score_scale
    )
    value_grad = jnp.einsum("hqk,qhd->kd", probs_low, mixed_grad, preferred_element_type=F32)
    return query_grad, key_grad, value_grad


def per_device(
    residual,
    segments,
    routes,
    norm_attention,
    query_weight,
    key_projection_matrix,
    value_projection_matrix,
    query_gain,
    key_gain,
    out_weight,
    norm_experts,
    router_weight,
    gate_weight,
    up_weight,
    down_weight,
    grad_output,
):
    row_count = lax.axis_size("row")
    col_count = lax.axis_size("col")
    row_place = lax.axis_index("row")
    col_place = lax.axis_index("col")
    model_width = norm_attention.shape[0]
    feature_width = model_width // row_count
    head_size = query_gain.shape[0]
    heads_here = query_weight.shape[1] // head_size
    query_width = heads_here * head_size
    kv_heads = key_projection_matrix.shape[1] // head_size
    query_group_width = heads_here * row_count // kv_heads
    members = query_group_width // heads_here
    kv_index = row_place * heads_here // query_group_width
    member_place = row_place % members
    share_width = head_size // members
    column_mask = (jnp.arange(head_size, dtype=jnp.int32) // share_width == member_place).astype(
        F32
    )
    experts = gate_weight.shape[0] * row_count * col_count
    expert = row_place * col_count + col_place
    gate_here, up_here, down_here = gate_weight[0], up_weight[0], down_weight[0]
    token_rows = residual.shape[0]
    chunks = token_rows // SEQUENCE_TOKENS
    rows = SEQUENCE_TOKENS
    top_count = routes.shape[1]
    capacity = max(2, 5 * rows * top_count // (4 * experts))
    score_scale = head_size ** (-0.5)
    row_start = row_place * feature_width
    gain_one = lax.dynamic_slice_in_dim(norm_attention, row_start, feature_width)
    gain_two = lax.dynamic_slice_in_dim(norm_experts, row_start, feature_width)
    router_rows = lax.dynamic_slice_in_dim(router_weight, row_start, feature_width, 0)
    labels = jnp.arange(experts, dtype=jnp.int32)
    key_part = lax.dynamic_slice_in_dim(key_projection_matrix, kv_index * head_size, head_size, 1)
    value_part = lax.dynamic_slice_in_dim(
        value_projection_matrix, kv_index * head_size, head_size, 1
    )

    def chunk(array, number):
        return array[number * rows : (number + 1) * rows]

    blocks = [chunk(residual, n) for n in range(chunks)]
    grads = [chunk(grad_output, n) for n in range(chunks)]
    segs = [chunk(segments, n) for n in range(chunks)]
    picks = [chunk(routes, n) for n in range(chunks)]

    inputs_full = [ring_gather(block) for block in blocks]
    projection = col_assemble(jnp.concatenate([query_weight, key_part, value_part], axis=1), 0)
    out_full = col_assemble(out_weight, 1)
    picks_all = [jnp.stack(col_gather(pick)) for pick in picks]
    grads_cols = [jnp.stack(col_gather(grad)) for grad in grads]

    state = [{} for _ in range(chunks)]

    for n in range(chunks):
        s = state[n]
        wide = inputs_full[n].astype(F32)
        s["scale_one"] = rms_factor(wide)
        s["normed_full"] = (wide * s["scale_one"] * norm_attention).astype(BF16)
        projected = dot(s["normed_full"], projection)
        s["query_pre"] = projected[:, :query_width].reshape(rows, heads_here, head_size)
        s["key_pre"] = projected[:, None, query_width : query_width + head_size]
        s["value_pre"] = projected[:, query_width + head_size :]
        s["value_low"] = s["value_pre"].astype(BF16)
        s["tables"] = rotary(positions(segs[n]), head_size)
        s["query_low"] = rotate(
            s["query_pre"] * rms_factor(s["query_pre"]) * query_gain, *s["tables"]
        ).astype(BF16)
        s["key_low"] = rotate(s["key_pre"] * rms_factor(s["key_pre"]) * key_gain, *s["tables"])[
            :, 0, :
        ].astype(BF16)
        mixed, s["log_totals"] = attention_forward(
            s["query_low"], s["key_low"], s["value_low"], segs[n], score_scale
        )
        s["mixed_low"] = mixed.reshape(rows, query_width).astype(BF16)
        partial = dot(s["mixed_low"], out_full).astype(BF16)
        s["hidden"] = blocks[n].astype(F32) + ring_scatter(partial)

    for n in range(chunks):
        s = state[n]
        wide = ring_gather(s["hidden"].astype(BF16)).astype(F32)
        s["scale_two"] = rms_factor(wide)
        normed_full = (wide * s["scale_two"] * norm_experts).astype(BF16)
        s["normed_two"] = lax.dynamic_slice_in_dim(normed_full, row_start, feature_width, 1)
        s["tokens"] = jnp.stack(col_gather(normed_full))

    grads_full = [ring_gather(g) for g in grads_cols]

    acc_gate = acc_up = acc_down = None
    for n in range(chunks):
        s = state[n]
        chosen = jnp.any(picks_all[n][:, :, :, None] == labels, axis=2)
        s["chosen"] = chosen[0]
        logits = jnp.einsum("gtd,de->gte", s["tokens"], router_weight, preferred_element_type=F32)
        shifted = jnp.where(chosen, logits, MASKED)
        weights = jnp.exp(shifted - jnp.max(shifted, axis=-1, keepdims=True))
        gates = weights / jnp.sum(weights, axis=-1, keepdims=True)
        s["logits"], s["gates"] = logits[0], gates[0]
        mine = jnp.any(picks_all[n] == expert, axis=2)
        ranks = jnp.cumsum(mine.astype(jnp.int32), axis=1) - 1
        slots = jnp.arange(capacity, dtype=jnp.int32)
        onehot = jnp.logical_and(ranks[:, None, :] == slots[None, :, None], mine[:, None, :])
        gates_here = lax.dynamic_index_in_dim(gates, expert, 2, keepdims=False)
        slot_gates = jnp.sum(jnp.where(onehot, gates_here[:, None, :], 0.0), axis=2).reshape(-1, 1)
        choose = onehot.astype(BF16)

        def gather(values):
            found = jnp.einsum("gst,gtd->gsd", choose, values, preferred_element_type=F32)
            return found.astype(BF16).reshape(-1, model_width)

        def scatter(values):
            values = values.reshape(col_count, capacity, model_width)
            spread = jnp.einsum("gst,gsd->gtd", choose, values, preferred_element_type=F32)
            spread = spread.astype(BF16)
            return ring_scatter(
                col_scatter([spread[g] for g in range(col_count)]).astype(BF16)
            )

        expert_in = gather(s["tokens"])
        gate_pre = dot(expert_in, gate_here)
        up_pre = dot(expert_in, up_here)
        sigmoid_gate = jax.nn.sigmoid(gate_pre)
        silu_gate = gate_pre * sigmoid_gate
        hidden_low = (silu_gate * up_pre).astype(BF16)
        expert_out = dot(hidden_low, down_here).astype(BF16).astype(F32)
        s["mixture"] = scatter((slot_gates * expert_out).astype(BF16))

        out_grad = gather(grads_full[n]).astype(F32)
        gate_dots = jnp.sum(out_grad * expert_out, axis=1)
        expert_grad = (slot_gates * out_grad).astype(BF16)
        hidden_grad = dot(expert_grad, down_here.T).astype(BF16).astype(F32)
        gate_grad = (
            hidden_grad * up_pre * sigmoid_gate * (1.0 + gate_pre * (1.0 - sigmoid_gate))
        ).astype(BF16)
        up_grad = (hidden_grad * silu_gate).astype(BF16)
        slot_grad = dot(gate_grad, gate_here.T) + dot(up_grad, up_here.T)
        slot_low = slot_grad.astype(BF16)
        slot_inner = jnp.sum(slot_grad * expert_in.astype(F32), axis=1)
        s["spread_grad"] = scatter(slot_low)

        def by_token(values):
            values = values.reshape(col_count, capacity, 1)
            return jnp.sum(jnp.where(onehot, values, 0.0), axis=1)

        dots_here = by_token(gate_dots)
        inner_here = by_token(slot_inner)
        small = jnp.concatenate(
            [
                jnp.where((labels == expert)[None, :, None], dots_here[:, None, :], 0.0),
                inner_here[:, None, :],
            ],
            axis=1,
        )
        s["small"] = butterfly(col_scatter([small[g] for g in range(col_count)]), "row")
        here = (
            dot(expert_in.T, gate_grad),
            dot(expert_in.T, up_grad),
            dot(hidden_low.T, expert_grad),
        )
        if n == 0:
            acc_gate, acc_up, acc_down = here
        else:
            acc_gate, acc_up, acc_down = acc_gate + here[0], acc_up + here[1], acc_down + here[2]
    grad_gate, grad_up, grad_down = pair_total(acc_gate), pair_total(acc_up), pair_total(acc_down)

    acc_projection = acc_out = None
    acc_router = jnp.zeros((feature_width, experts), F32)
    acc_gain_one = jnp.zeros((model_width,), F32)
    acc_gain_two = jnp.zeros((feature_width,), F32)
    acc_query_gain = jnp.zeros((head_size,), F32)
    acc_key_gain = jnp.zeros((head_size,), F32)
    output_blocks, input_blocks = [], []
    for n in range(chunks):
        s = state[n]
        output_blocks.append((s["hidden"] + s["mixture"]).astype(BF16))
        block_grad = grads[n].astype(F32)
        gate_dots = s["small"][:experts].T
        slot_inner = s["small"][experts]
        pick_grad = s["gates"] * (
            gate_dots - jnp.sum(s["gates"] * gate_dots, axis=1, keepdims=True)
        )
        logit_grad = pick_grad.astype(BF16)
        acc_router = acc_router + dot(s["normed_two"].T, logit_grad)
        normed_two_grad = s["spread_grad"] + dot(logit_grad, router_rows.T)
        inner_two = slot_inner[:, None] + jnp.sum(
            logit_grad.astype(F32) * s["logits"], axis=1, keepdims=True
        )
        scale_two = s["scale_two"]
        hidden_total = (
            block_grad
            + normed_two_grad * gain_two * scale_two
            - s["hidden"] * (scale_two * scale_two * inner_two / model_width)
        )
        acc_gain_two = acc_gain_two + jnp.sum(normed_two_grad * s["hidden"] * scale_two, axis=0)
        branch_full = ring_gather(hidden_total.astype(BF16))
        out_here = dot(s["mixed_low"].T, branch_full)
        acc_out = out_here if n == 0 else acc_out + out_here
        mixed_grad = dot(branch_full, out_full.T).astype(BF16)
        mixed_grad = mixed_grad.reshape(rows, heads_here, head_size)
        query_grad, key_grad, value_grad = attention_backward(
            s["query_low"],
            s["key_low"],
            s["value_low"],
            segs[n],
            s["log_totals"],
            mixed_grad,
            score_scale,
        )
        for bit in range(members.bit_length() - 1):
            key_grad = key_grad + swapped(key_grad, "row", bit)
            value_grad = value_grad + swapped(value_grad, "row", bit)
        query_pre_grad, query_terms = rms_back(
            s["query_pre"], query_gain, unrotate(query_grad, *s["tables"])
        )
        acc_query_gain = acc_query_gain + jnp.sum(query_terms, axis=(0, 1))
        key_pre_grad, key_terms = rms_back(
            s["key_pre"], key_gain, unrotate(key_grad[:, None, :], *s["tables"])
        )
        acc_key_gain = acc_key_gain + column_mask * jnp.sum(key_terms, axis=(0, 1))
        projected_grad = jnp.concatenate(
            [
                query_pre_grad.reshape(rows, query_width).astype(BF16),
                (column_mask * key_pre_grad[:, 0, :]).astype(BF16),
                (column_mask * value_grad).astype(BF16),
            ],
            axis=1,
        )
        projected = jnp.concatenate(
            [s["query_pre"].reshape(rows, query_width), s["key_pre"][:, 0, :], s["value_pre"]],
            axis=1,
        )
        inner_one = butterfly(
            jnp.sum(projected_grad.astype(F32) * projected, axis=1), "row"
        )[:, None]
        partial = dot(projected_grad, projection.T)
        acc_gain_one = acc_gain_one + jnp.sum(
            partial * inputs_full[n].astype(F32) * s["scale_one"], axis=0
        )
        projection_here = dot(s["normed_full"].T, projected_grad)
        acc_projection = projection_here if n == 0 else acc_projection + projection_here
        normed_one_grad = ring_scatter(partial.astype(BF16))
        scale_one = s["scale_one"]
        input_blocks.append(
            hidden_total
            + normed_one_grad * gain_one * scale_one
            - blocks[n].astype(F32) * (scale_one * scale_one * inner_one / model_width)
        )

    grad_out_weight = pair_total(col_share(acc_out.astype(BF16), 1))
    projection_share = pair_total(col_share(acc_projection.astype(BF16), 0))
    grad_query = projection_share[:, :query_width]
    shares = ring_gather(projection_share[:, query_width:].astype(BF16))
    shares = shares.astype(F32).reshape(-1, kv_heads, members, 2, head_size).sum(axis=2)
    grad_key = shares[:, :, 0].reshape(-1, kv_heads * head_size)
    grad_value = shares[:, :, 1].reshape(-1, kv_heads * head_size)

    gain_two_full = lax.dynamic_update_slice_in_dim(
        jnp.zeros((model_width,), F32), acc_gain_two, row_start, 0
    )
    router_full = lax.dynamic_update_slice_in_dim(
        jnp.zeros((model_width, experts), F32), acc_router, row_start, 0
    )
    sizes = (model_width, model_width, head_size, head_size, model_width * experts)
    flat = jnp.concatenate(
        [acc_gain_one, gain_two_full, acc_query_gain, acc_key_gain, router_full.reshape(-1)]
    )
    for axis in ("dp", "col", "row"):
        flat = butterfly(flat, axis)
    totals, start = [], 0
    for size in sizes:
        totals.append(flat[start : start + size])
        start += size
    return (
        jnp.concatenate(output_blocks, axis=0),
        jnp.concatenate(input_blocks, axis=0),
        totals[0],
        grad_query,
        grad_key,
        grad_value,
        totals[2],
        totals[3],
        grad_out_weight,
        totals[1],
        totals[4].reshape(model_width, experts),
        grad_gate[None],
        grad_up[None],
        grad_down[None],
    )


def solution(mesh):
    in_specs = (
        P(("dp", "col"), "row"),
        P(("dp", "col")),
        P(("dp", "col"), None),
        P(),
        P("col", "row"),
        P("col", None),
        P("col", None),
        P(),
        P(),
        P("row", "col"),
        P(),
        P(),
        P(("row", "col"), None, None),
        P(("row", "col"), None, None),
        P(("row", "col"), None, None),
        P(("dp", "col"), "row"),
    )
    out_specs = (
        P(("dp", "col"), "row"),
        P(("dp", "col"), "row"),
        P(),
        P("col", "row"),
        P("col", None),
        P("col", None),
        P(),
        P(),
        P("row", "col"),
        P(),
        P(),
        P(("row", "col"), None, None),
        P(("row", "col"), None, None),
        P(("row", "col"), None, None),
    )
    return jax.shard_map(
        per_device, mesh=mesh, in_specs=in_specs, out_specs=out_specs, check_vma=False
    )
```

```python
import functools

import jax
import jax.numpy as jnp
from jax import lax
from jax.experimental import pallas as pl
from jax.experimental.pallas import tpu as pltpu
from jax.sharding import PartitionSpec as P

SEQUENCE_TOKENS = 512
EPSILON = 1e-06
ROPE_BASE = 1000000.0
MASKED = -1e30
LANES = 128
BF16 = jnp.bfloat16
F32 = jnp.float32
NT = (((1,), (1,)), ((), ()))
TN = (((0,), (0,)), ((), ()))

def mm(left, right):
    return jnp.dot(left, right, preferred_element_type=F32)

def mm_nt(left, right):
    return lax.dot_general(left, right, NT, preferred_element_type=F32)

def mm_tn(left, right):
    return lax.dot_general(left, right, (((0,), (0,)), ((), ())), preferred_element_type=F32)

def turn(values, cos_wide, sin_wide):
    return values * cos_wide + pltpu.roll(values, values.shape[1] // 2, 1) * sin_wide

def unit(values):
    return lax.rsqrt(jnp.mean(values * values, axis=1, keepdims=True) + EPSILON)

def sequence_bias(segs_ref, segs_t_ref):
    rows = segs_ref.shape[1]
    before = lax.broadcasted_iota(jnp.int32, (rows, rows), 1) <= lax.broadcasted_iota(jnp.int32, (rows, rows), 0)
    same = segs_t_ref[...] == segs_ref[...]
    return jnp.where(jnp.logical_and(same, before), 0.0, MASKED)

def block_probs(query, key, bias, scale):
    scores = mm_nt(query, key) * scale + bias
    weights = jnp.exp(scores - jnp.max(scores, axis=1, keepdims=True))
    return weights * (1.0 / jnp.sum(weights, axis=1, keepdims=True))

def attention_forward_kernel(scale, q_ref, k_ref, v_ref, segs_ref, segs_t_ref, cos_ref, sin_ref, q_gain_ref, k_gain_ref, out_ref, bias, key, value):
    head = k_ref.shape[1]
    rows = q_ref.shape[0]
    half = rows // 2
    cos_wide, sin_wide = cos_ref[...], sin_ref[...]

    @pl.when(pl.program_id(0) == 0)
    def _():
        bias[...] = sequence_bias(segs_ref, segs_t_ref)
        k_pre = k_ref[...]
        key[...] = turn(k_pre * unit(k_pre) * k_gain_ref[...], cos_wide, sin_wide).astype(BF16)
        value[...] = v_ref[...].astype(BF16)

    for h in range(q_ref.shape[1] // head):
        lanes = slice(h * head, (h + 1) * head)
        q_pre = q_ref[:, lanes]
        query = turn(q_pre * unit(q_pre) * q_gain_ref[...], cos_wide, sin_wide).astype(BF16)
        for part in range(2):
            at, keys = slice(part * half, (part + 1) * half), slice(0, (part + 1) * half)
            probs = block_probs(query[at], key[keys, :], bias[at, keys], scale)
            out_ref[at, lanes] = mm(probs.astype(BF16), value[keys, :]).astype(BF16)

def attention_forward(projected, heads, segs, segs_t, cos_wide, sin_wide, q_gain, k_gain):
    rows = projected.shape[0]
    head = q_gain.shape[1]
    pair = 2 if heads % 2 == 0 else 1
    fixed = lambda *shape: pl.BlockSpec(shape, lambda i: (0,) * len(shape))
    return pl.pallas_call(
        functools.partial(attention_forward_kernel, head ** -0.5),
        grid=(heads // pair,),
        out_shape=jax.ShapeDtypeStruct((rows, heads * head), BF16),
        in_specs=[
            pl.BlockSpec((rows, pair * head), lambda i: (0, i)),
            pl.BlockSpec((rows, head), lambda i: (0, heads)),
            pl.BlockSpec((rows, head), lambda i: (0, heads + 1)),
            fixed(1, rows), fixed(rows, 1), fixed(rows, head), fixed(rows, head), fixed(1, head), fixed(1, head),
        ],
        out_specs=pl.BlockSpec((rows, pair * head), lambda i: (0, i)),
        scratch_shapes=[pltpu.VMEM((rows, rows), F32), pltpu.VMEM((rows, head), BF16), pltpu.VMEM((rows, head), BF16)],
        compiler_params=pltpu.CompilerParams(vmem_limit_bytes=48 << 20),
        cost_estimate=pl.CostEstimate(flops=10**10, bytes_accessed=10**7, transcendentals=0),
        name="attention_forward",
    )(projected, projected, projected, segs, segs_t, cos_wide, sin_wide, q_gain, k_gain)

def norm_back(values, gain, upstream):
    factor = unit(values)
    weighted = upstream * gain
    inner = jnp.mean(weighted * values, axis=1, keepdims=True)
    return weighted * factor - values * (factor * factor * factor * inner), upstream * values * factor

def attention_backward_kernel(scale, finish, q_ref, k_ref, v_ref, g_ref, segs_ref, segs_t_ref, cos_ref, sin_ref, q_gain_ref, k_gain_ref,
                              out_ref, key_ref, value_ref, inner_ref, gains_ref, bias, key, value, inner):
    head = k_ref.shape[1]
    rows = q_ref.shape[0]
    half = rows // 2
    cos_wide, sin_wide = cos_ref[...], sin_ref[...]
    step, steps = pl.program_id(0), pl.num_programs(0)
    pair = q_ref.shape[1] // head

    @pl.when(step == 0)
    def _():
        bias[...] = sequence_bias(segs_ref, segs_t_ref)
        k_pre = k_ref[...]
        key[...] = turn(k_pre * unit(k_pre) * k_gain_ref[...], cos_wide, sin_wide).astype(BF16)
        value[...] = v_ref[...].astype(BF16)
        key_ref[...] = jnp.zeros_like(key_ref)
        value_ref[...] = jnp.zeros_like(value_ref)
        inner[...] = jnp.zeros_like(inner)
        gains_ref[...] = jnp.zeros_like(gains_ref)

    for h in range(pair):
        lanes = slice(h * head, (h + 1) * head)
        q_pre = q_ref[:, lanes]
        query = turn(q_pre * unit(q_pre) * q_gain_ref[...], cos_wide, sin_wide).astype(BF16)
        grads = []
        for part in range(2):
            at, keys = slice(part * half, (part + 1) * half), slice(0, (part + 1) * half)
            probs = block_probs(query[at], key[keys, :], bias[at, keys], scale)
            upstream = g_ref[at, lanes]
            prob_grad = mm_nt(upstream, value[keys, :])
            score_grad = (probs * (prob_grad - jnp.sum(probs * prob_grad, axis=1, keepdims=True))).astype(BF16)
            grads.append(mm(score_grad, key[keys, :]) * scale)
            key_ref[keys, :] += mm_tn(score_grad, query[at]) * scale
            value_ref[keys, :] += mm_tn(probs.astype(BF16), upstream)
        query_grad = turn(jnp.concatenate(grads, axis=0), cos_wide, -sin_wide)
        q_grad, terms = norm_back(q_pre, q_gain_ref[...], query_grad)
        low = q_grad.astype(BF16)
        out_ref[:, pl.ds(pl.multiple_of((step * pair + h) * head, head), head)] = low
        inner[...] += low.astype(F32) * q_pre
        gains_ref[0:1, :] += jnp.sum(terms, axis=0, keepdims=True)

    @pl.when(step == steps - 1)
    def _():
        total = jnp.sum(inner[...], axis=1, keepdims=True)
        if finish:
            k_pre, v_pre = k_ref[...], v_ref[...]
            k_grad, terms = norm_back(k_pre, k_gain_ref[...], turn(key_ref[...], cos_wide, -sin_wide))
            k_low, v_low = k_grad.astype(BF16), value_ref[...].astype(BF16)
            width = steps * pair * head
            out_ref[:, pl.ds(out_ref.shape[1] - 2 * head, head)] = k_low
            out_ref[:, pl.ds(out_ref.shape[1] - head, head)] = v_low
            gains_ref[1:2, :] = jnp.sum(terms, axis=0, keepdims=True)
            total = total + jnp.sum(k_low.astype(F32) * k_pre + v_low.astype(F32) * v_pre, axis=1, keepdims=True)
        inner_ref[...] = total

def attention_backward(finish, projected, upstream, heads, segs, segs_t, cos_wide, sin_wide, q_gain, k_gain):
    rows = projected.shape[0]
    head = q_gain.shape[1]
    pair = 2 if heads % 2 == 0 else 1
    fixed = lambda *shape: pl.BlockSpec(shape, lambda i: (0,) * len(shape))
    return pl.pallas_call(
        functools.partial(attention_backward_kernel, head ** -0.5, finish),
        grid=(heads // pair,),
        out_shape=[
            jax.ShapeDtypeStruct((rows, (heads + 2) * head), BF16),
            jax.ShapeDtypeStruct((rows, head), F32),
            jax.ShapeDtypeStruct((rows, head), F32),
            jax.ShapeDtypeStruct((rows, 1), F32),
            jax.ShapeDtypeStruct((2, head), F32),
        ],
        in_specs=[
            pl.BlockSpec((rows, pair * head), lambda i: (0, i)),
            pl.BlockSpec((rows, head), lambda i: (0, heads)),
            pl.BlockSpec((rows, head), lambda i: (0, heads + 1)),
            pl.BlockSpec((rows, pair * head), lambda i: (0, i)),
            fixed(1, rows), fixed(rows, 1), fixed(rows, head), fixed(rows, head), fixed(1, head), fixed(1, head),
        ],
        out_specs=[fixed(rows, (heads + 2) * head), fixed(rows, head), fixed(rows, head), fixed(rows, 1), fixed(2, head)],
        scratch_shapes=[pltpu.VMEM((rows, rows), F32), pltpu.VMEM((rows, head), BF16), pltpu.VMEM((rows, head), BF16), pltpu.VMEM((rows, head), F32)],
        compiler_params=pltpu.CompilerParams(vmem_limit_bytes=48 << 20),
        cost_estimate=pl.CostEstimate(flops=2 * 10**10, bytes_accessed=10**7, transcendentals=0),
        name="attention_backward",
    )(projected, projected, projected, upstream, segs, segs_t, cos_wide, sin_wide, q_gain, k_gain)

def norm_kernel(count, *refs):
    pieces, gain_ref, out_ref, scale_ref = refs[:count], refs[count], refs[count + 1], refs[count + 2]
    width = pieces[0].shape[1]
    total = None
    for piece in pieces:
        wide = piece[...].astype(F32)
        part = jnp.sum(wide * wide, axis=1, keepdims=True)
        total = part if total is None else total + part
    scale = lax.rsqrt(total / (width * count) + EPSILON)
    scale_ref[...] = scale
    for i, piece in enumerate(pieces):
        at = slice(i * width, (i + 1) * width)
        out_ref[:, at] = (piece[...].astype(F32) * scale * gain_ref[:, at]).astype(BF16)

def assemble_norm(pieces, offsets, rows, gain):
    count = len(pieces)
    width = pieces[0].shape[1]
    block = min(128, rows)
    return pl.pallas_call(
        functools.partial(norm_kernel, count),
        grid=(rows // block,),
        out_shape=[jax.ShapeDtypeStruct((rows, width * count), BF16), jax.ShapeDtypeStruct((rows, 1), F32)],
        in_specs=[pl.BlockSpec((block, width), lambda i, o=o: (o // block + i, 0)) for o in offsets]
        + [pl.BlockSpec((1, width * count), lambda i: (0, 0))],
        out_specs=[pl.BlockSpec((block, width * count), lambda i: (i, 0)), pl.BlockSpec((block, 1), lambda i: (i, 0))],
        compiler_params=pltpu.CompilerParams(vmem_limit_bytes=32 << 20),
        cost_estimate=pl.CostEstimate(flops=2 * 10**9, bytes_accessed=8 * 10**6, transcendentals=0),
        name="assemble_norm",
    )(*pieces, gain)


def pair_kernel(first, place, scalars_ref, slots_ref, slots_t_ref, mask_ref, router_ref, *refs):
    refs = list(refs)
    token_in, grad_in = refs[0:2], refs[2:4]
    weights_in = refs[4:7]
    del refs[:7]
    if not first:
        del refs[:5]
    y_out, x_out = refs[0:2], refs[2:4]
    small_out, logits_out, gates_out = refs[4:7]
    kept_out = refs[7:12]
    (token, grad, gate_w, up_w, down_w, y_buf, x_buf, rows_in, rows_grad, rows_dy, rows_u, rows_da, rows_db, in_sem, w_sem, out_sem, kept_sem) = refs[12:]
    capacity = rows_in.shape[0] // 2
    tokens, width = token.shape[1:]
    hidden = gate_w.shape[1]
    load_tok = [pltpu.make_async_copy(token_in[g], token.at[g], in_sem.at[0, g]) for g in range(2)]
    load_grad = [pltpu.make_async_copy(grad_in[g], grad.at[g], in_sem.at[1, g]) for g in range(2)]
    parts = w_sem.shape[1]
    strip = width // parts
    load_w = []
    for d in range(parts):
        there = pl.multiple_of((scalars_ref[1] + d) % parts * strip, strip)
        here = slice(d * strip, (d + 1) * strip)
        for i, (src, dst) in enumerate(zip(weights_in, (gate_w, up_w, down_w))):
            if i < 2:
                src, dst = src.at[pl.ds(there, strip), :], dst.at[here, :]
            else:
                src, dst = src.at[:, pl.ds(there, strip)], dst.at[:, here]
            load_w.append(pltpu.make_async_copy(src, dst, w_sem.at[i, d]))
    load_tok[0].start()
    load_grad[0].start()
    for load in load_w:
        load.start()
    load_tok[1].start()
    load_grad[1].start()
    expert = scalars_ref[0]
    stores = []
    wide = min(512, width)
    step = 256 if hidden % 256 == 0 else hidden
    chosen_rows, spreads, gate_cols = [], [], []
    for g in range(2):
        load_tok[g].wait()
        logits = mm(token[g], router_ref[...])
        shifted = logits + mask_ref[g].astype(F32)
        weights = jnp.exp(shifted - jnp.max(shifted, axis=1, keepdims=True))
        gates = weights / jnp.sum(weights, axis=1, keepdims=True)
        if g == 0:
            logits_out[...] = logits
            gates_out[...] = gates
        gates_t = gates.T
        lane = lax.broadcasted_iota(jnp.int32, gates_t.shape, 0)
        gate_row = jnp.sum(jnp.where(lane == expert, gates_t, 0.0), axis=0, keepdims=True)
        chosen = lax.broadcasted_iota(jnp.int32, (capacity, tokens), 0) == slots_ref[g]
        slot_gates = jnp.sum(jnp.where(chosen, gate_row, 0.0), axis=1, keepdims=True)
        pick = jnp.where(chosen, 1.0, 0.0).astype(BF16)
        here = slice(g * capacity, (g + 1) * capacity)
        gate_cols.append(slot_gates)
        load_grad[g].wait()

        def gather(j, _):
            at = pl.ds(pl.multiple_of(j * wide, wide), wide)
            rows_in[here, at] = mm(pick, token[g, :, at]).astype(BF16)
            found = mm(pick, grad[g, :, at])
            rows_grad[here, at] = found.astype(BF16)
            rows_dy[here, at] = (slot_gates * found).astype(BF16)
            return 0

        lax.fori_loop(0, width // wide, gather, 0)
    for load in load_w:
        load.wait()
    slot_gates = jnp.concatenate(gate_cols, axis=0)

    def middle(j, _):
        at = pl.ds(pl.multiple_of(j * step, step), step)
        a = mm(rows_in[...], gate_w[:, at])
        b = mm(rows_in[...], up_w[:, at])
        du = mm_nt(rows_dy[...], down_w[at, :]).astype(BF16).astype(F32)
        sig = 1.0 / (1.0 + jnp.exp(-a))
        silu = a * sig
        rows_u[:, at] = (silu * b).astype(BF16)
        rows_da[:, at] = (du * b * sig * (1.0 + a * (1.0 - sig))).astype(BF16)
        rows_db[:, at] = (du * silu).astype(BF16)
        return 0

    lax.fori_loop(0, hidden // step, middle, 0)
    kept_here = pl.ds(place * 2 * capacity, 2 * capacity)
    for i, kept_rows in enumerate((rows_in, rows_dy, rows_u, rows_da, rows_db)):
        store = pltpu.make_async_copy(kept_rows, kept_out[i].at[kept_here, :], kept_sem.at[i])
        store.start()
        stores.append(store)
    spreads = [
        jnp.where(
            lax.broadcasted_iota(jnp.int32, (tokens, capacity), 1) == slots_t_ref[g], 1.0, 0.0
        ).astype(BF16)
        for g in range(2)
    ]

    def back(j, carry):
        dots, inner = carry
        at = pl.ds(pl.multiple_of(j * wide, wide), wide)
        y = mm(rows_u[...], down_w[:, at]).astype(BF16).astype(F32)
        dots = dots + jnp.sum(rows_grad[:, at].astype(F32) * y, axis=1, keepdims=True)
        low = (slot_gates * y).astype(BF16)
        dx = mm_nt(rows_da[...], gate_w[at, :]) + mm_nt(rows_db[...], up_w[at, :])
        inner = inner + jnp.sum(rows_in[:, at].astype(F32) * dx, axis=1, keepdims=True)
        dx_low = dx.astype(BF16)
        for g in range(2):
            here = slice(g * capacity, (g + 1) * capacity)
            y_buf[g, :, at] = mm(spreads[g], low[here]).astype(BF16)
            x_buf[g, :, at] = mm(spreads[g], dx_low[here]).astype(BF16)
        return dots, inner

    nothing = jnp.zeros((2 * capacity, 1), F32)
    dots, inner = lax.fori_loop(0, width // wide, back, (nothing, nothing))
    for g in range(2):
        here = slice(g * capacity, (g + 1) * capacity)
        chosen = lax.broadcasted_iota(jnp.int32, (capacity, tokens), 0) == slots_ref[g]
        small_out[g, 0:1, :] = jnp.sum(jnp.where(chosen, dots[here], 0.0), axis=0, keepdims=True)
        small_out[g, 1:2, :] = jnp.sum(jnp.where(chosen, inner[here], 0.0), axis=0, keepdims=True)
        for i, (buf, out) in enumerate(((x_buf, x_out), (y_buf, y_out))):
            store = pltpu.make_async_copy(buf.at[g], out[g], out_sem.at[i, g])
            store.start()
            stores.append(store)
    for store in stores:
        store.wait()


def expert_pair(
    place, places, capacity, scalars, slots, slots_t, mask, router, tokens, grads, weights, kept
):
    rows, width = tokens[0].shape
    hidden = weights[0].shape[1]
    parts = lax.axis_size("row")
    total = places * 2 * capacity
    anywhere = pl.BlockSpec(memory_space=pl.ANY)
    inside = pl.BlockSpec(memory_space=pltpu.VMEM)
    first = kept is None
    dense = jax.ShapeDtypeStruct((rows, width), BF16)
    kept_shapes = [jax.ShapeDtypeStruct((total, w), BF16) for w in (width, width, hidden, hidden, hidden)]
    flat = jax.ShapeDtypeStruct((rows, router.shape[1]), F32)
    out = pl.pallas_call(
        functools.partial(pair_kernel, first, place),
        out_shape=[dense] * 4 + [jax.ShapeDtypeStruct((2, 2, rows), F32), flat, flat] + kept_shapes,
        in_specs=[pl.BlockSpec(memory_space=pltpu.SMEM)] + [inside] * 4 + [anywhere] * (7 if first else 12),
        out_specs=[anywhere] * 4 + [inside] * 3 + [anywhere] * 5,
        input_output_aliases={} if first else {12 + i: 7 + i for i in range(5)},
        scratch_shapes=[
            pltpu.VMEM((2, rows, width), BF16),
            pltpu.VMEM((2, rows, width), BF16),
            pltpu.VMEM((width, hidden), BF16),
            pltpu.VMEM((width, hidden), BF16),
            pltpu.VMEM((hidden, width), BF16),
            pltpu.VMEM((2, rows, width), BF16),
            pltpu.VMEM((2, rows, width), BF16),
            pltpu.VMEM((2 * capacity, width), BF16),
            pltpu.VMEM((2 * capacity, width), BF16),
            pltpu.VMEM((2 * capacity, width), BF16),
            pltpu.VMEM((2 * capacity, hidden), BF16),
            pltpu.VMEM((2 * capacity, hidden), BF16),
            pltpu.VMEM((2 * capacity, hidden), BF16),
            pltpu.SemaphoreType.DMA((2, 2)),
            pltpu.SemaphoreType.DMA((3, parts)),
            pltpu.SemaphoreType.DMA((2, 2)),
            pltpu.SemaphoreType.DMA((5,)),
        ],
        compiler_params=pltpu.CompilerParams(vmem_limit_bytes=56 << 20),
        cost_estimate=pl.CostEstimate(flops=36 * 10**9, bytes_accessed=10**7, transcendentals=0),
        name="expert_pair",
    )(scalars, slots, slots_t, mask, router, *tokens, *grads, *weights, *([] if first else kept))
    return out


def route_kernel(expert_ref, routes_ref, mask_ref, slots_ref, slots_t_ref):
    rows, top_count = routes_ref.shape[1:]
    routes = routes_ref[0]
    lanes = lax.broadcasted_iota(jnp.int32, (rows, LANES), 1)
    chosen = routes[:, 0:1] == lanes
    for k in range(1, top_count):
        chosen = jnp.logical_or(chosen, routes[:, k : k + 1] == lanes)
    mask_ref[0] = jnp.where(chosen, 0.0, MASKED).astype(BF16)
    below = lax.broadcasted_iota(jnp.int32, (rows, rows), 1) <= lax.broadcasted_iota(
        jnp.int32, (rows, rows), 0
    )
    ones = jnp.where(chosen, 1.0, 0.0)
    ranks = mm(jnp.where(below, 1.0, 0.0).astype(BF16), ones.astype(BF16))
    slots = jnp.where(chosen, ranks - 1.0, -1.0)
    here = lanes == expert_ref[0]
    slots_t_ref[0] = jnp.max(jnp.where(here, slots, -1.0), axis=1, keepdims=True).astype(jnp.int32)
    lane_first = lax.broadcasted_iota(jnp.int32, (LANES, rows), 0)
    slots_ref[0] = jnp.max(
        jnp.where(lane_first == expert_ref[0], slots.T, -1.0), axis=0, keepdims=True
    ).astype(jnp.int32)


def route_tables(scalars, routes):
    blocks, rows, top_count = routes.shape
    return pl.pallas_call(
        route_kernel,
        grid=(blocks,),
        out_shape=[
            jax.ShapeDtypeStruct((blocks, rows, LANES), BF16),
            jax.ShapeDtypeStruct((blocks, 1, rows), jnp.int32),
            jax.ShapeDtypeStruct((blocks, rows, 1), jnp.int32),
        ],
        in_specs=[
            pl.BlockSpec(memory_space=pltpu.SMEM),
            pl.BlockSpec((1, rows, top_count), lambda i: (i, 0, 0)),
        ],
        out_specs=[
            pl.BlockSpec((1, rows, LANES), lambda i: (i, 0, 0)),
            pl.BlockSpec((1, 1, rows), lambda i: (i, 0, 0)),
            pl.BlockSpec((1, rows, 1), lambda i: (i, 0, 0)),
        ],
        compiler_params=pltpu.CompilerParams(vmem_limit_bytes=32 << 20),
        cost_estimate=pl.CostEstimate(flops=10**9, bytes_accessed=10**6, transcendentals=0),
        name="route_tables",
    )(scalars, routes)


def place_kernel(axis, starts_ref, *refs):
    out = refs[-1]
    for i, piece in enumerate(refs[:-1]):
        width = piece.shape[axis]
        at = pl.ds(pl.multiple_of(starts_ref[i] * width, width), width)
        if axis == 0:
            out[at, :] = piece[...]
        else:
            out[:, at] = piece[...]


def placed(pieces, starts, axis):
    shape = list(pieces[0].shape)
    shape[axis] *= len(pieces)
    inside = pl.BlockSpec(memory_space=pltpu.VMEM)
    return pl.pallas_call(
        functools.partial(place_kernel, axis),
        out_shape=jax.ShapeDtypeStruct(tuple(shape), pieces[0].dtype),
        in_specs=[pl.BlockSpec(memory_space=pltpu.SMEM)] + [inside] * len(pieces),
        out_specs=inside,
        compiler_params=pltpu.CompilerParams(vmem_limit_bytes=32 << 20),
        cost_estimate=pl.CostEstimate(flops=10**6, bytes_accessed=10**7, transcendentals=0),
        name="placed",
    )(starts, *pieces)


def add_kernel(place_ref, one_ref, two_ref, out_ref):
    out_ref[...] = one_ref[...].astype(F32) + two_ref[...].astype(F32)


def unrolled_sum(one, two, place, parts, axis):
    shape = one.shape
    block = tuple(s // parts if d == axis else s for d, s in enumerate(shape))
    if axis == 0:
        at_in, at_out = lambda i, p: (i, 0), lambda i, p: ((i + p[0]) % parts, 0)
    else:
        at_in, at_out = lambda i, p: (0, i), lambda i, p: (0, (i + p[0]) % parts)
    return pl.pallas_call(
        add_kernel,
        grid_spec=pltpu.PrefetchScalarGridSpec(
            num_scalar_prefetch=1,
            grid=(parts,),
            in_specs=[pl.BlockSpec(block, at_in)] * 2,
            out_specs=pl.BlockSpec(block, at_out),
        ),
        out_shape=jax.ShapeDtypeStruct(shape, F32),
        compiler_params=pltpu.CompilerParams(vmem_limit_bytes=40 << 20),
        cost_estimate=pl.CostEstimate(flops=10**6, bytes_accessed=10**6, transcendentals=0),
        name="unrolled_sum",
    )(place, one, two)


def moved(block, axis, by):
    count = lax.axis_size(axis)
    return lax.ppermute(block, axis, [(i, (i + by) % count) for i in range(count)])


def swapped(block, axis, bit):
    count = lax.axis_size(axis)
    return lax.ppermute(block, axis, [(i, i ^ (1 << bit)) for i in range(count)])


def butterfly(values, axis):
    for bit in range(lax.axis_size(axis).bit_length() - 1):
        values = values + swapped(values, axis, bit)
    return values


def ring_pieces(block):
    count = lax.axis_size("row")
    pieces = [[block]] + [None] * (count - 1)
    from_left = from_right = block
    half = block.shape[0] // 2
    for step in range(1, count // 2):
        from_left = moved(from_left, "row", 1)
        from_right = moved(from_right, "row", -1)
        pieces[count - step] = [from_left]
        pieces[step] = [from_right]
    if count > 1:
        pieces[count // 2] = [
            moved(from_left[:half], "row", 1),
            moved(from_right[half:], "row", -1),
        ]
    return pieces


def chunk_pieces(pieces, number, rows):
    blocks, offsets = [], []
    for piece in pieces:
        tall = piece[0].shape[0]
        if len(piece) == 1:
            blocks.append(piece[0])
            offsets.append(number * rows)
        elif tall >= rows:
            blocks.append(piece[number * rows // tall])
            offsets.append(number * rows % tall)
        else:
            blocks.append(jnp.concatenate(piece, axis=0))
            offsets.append(number * rows)
    return blocks, offsets


def joined(pieces, number, rows):
    blocks, offsets = chunk_pieces(pieces, number, rows)
    return jnp.concatenate([b[o : o + rows] for b, o in zip(blocks, offsets)], axis=1)


def ring_scatter(partial):
    count = lax.axis_size("row")
    width = partial.shape[1] // count
    half = partial.shape[0] // 2

    def piece(distance):
        return partial[:, distance * width : (distance + 1) * width]

    total = piece(0).astype(F32)
    if count == 1:
        return total
    middle = piece(count // 2)
    to_right = moved(middle[:half], "row", 1)
    to_left = moved(middle[half:], "row", -1)
    for step in range(count // 2 - 1, 0, -1):
        right, left = piece(step), piece(count - step)
        if step == count // 2 - 1:
            right = jnp.concatenate([right[:half] + to_right, right[half:]], axis=0)
            left = jnp.concatenate([left[:half], left[half:] + to_left], axis=0)
        else:
            right = right + to_right
            left = left + to_left
        to_right = moved(right, "row", 1)
        to_left = moved(left, "row", -1)
    if count == 2:
        return total + jnp.concatenate([to_right, to_left], axis=0).astype(F32)
    return total + to_right.astype(F32) + to_left.astype(F32)


def after(value, *others):
    return lax.optimization_barrier((value,) + others)[0]


class Link:
    def __init__(self):
        self.last = ()

    def moved(self, block, by):
        block = moved(after(block, *self.last), "col", by)
        self.last = (block,)
        return block


def col_gather(block, link):
    count = lax.axis_size("col")
    pieces = []
    for step in range(count // 2):
        same = block if step == 0 else link.moved(block, 2 * step)
        pieces += [same, swapped(same, "col", 0)]
    return pieces


def chip_total(same, other):
    return (same.astype(F32) + swapped(other, "col", 0).astype(F32)).astype(same.dtype)


def chips_total(totals, link):
    total = totals[0].astype(F32)
    for step in range(1, len(totals)):
        total = total + link.moved(totals[step], -2 * step).astype(F32)
    return total


def col_order():
    count = lax.axis_size("col")
    place = lax.axis_index("col")
    chip, core = place // 2, place % 2
    order = []
    for step in range(count // 2):
        back = (chip - step) % (count // 2) * 2
        order += [back + core, back + 1 - core]
    return order


def col_assemble(block, axis, shift, link):
    count = lax.axis_size("col")
    width = block.shape[axis]
    starts = [(place - shift // width) % count for place in col_order()]
    return placed(col_gather(block, link), jnp.stack(starts).astype(jnp.int32), axis)


def col_share(partial, axis, shift, link):
    count = lax.axis_size("col")
    width = partial.shape[axis] // count
    pieces = [
        lax.dynamic_slice_in_dim(
            partial, (place * width - shift) % (width * count), width, axis
        )
        for place in col_order()
    ]
    return chips_total(
        [chip_total(pieces[2 * s], pieces[2 * s + 1]) for s in range(count // 2)], link
    )


def pair_total(values):
    low = values.astype(BF16)
    total = low.astype(F32)
    for bit in range(lax.axis_size("dp").bit_length() - 1):
        total = total + swapped(low, "dp", bit).astype(F32)
        low = total.astype(BF16)
    return total


def rolled(values, shift, axis=0):
    size = values.shape[axis]
    twice = jnp.concatenate([values, values], axis=axis)
    return lax.dynamic_slice_in_dim(twice, shift % size, size, axis)


def positions(segment_ids):
    places = jnp.arange(segment_ids.shape[0], dtype=jnp.int32)
    earlier = jnp.concatenate([segment_ids[:1] - 1, segment_ids[:-1]])
    starts = jnp.logical_or(segment_ids != earlier, places % SEQUENCE_TOKENS == 0)
    opening = lax.cummax(jnp.where(starts, places, 0), axis=0)
    return places - opening


def rotary(places, head_size):
    halfway = head_size // 2
    frequency = ROPE_BASE ** (-2.0 * jnp.arange(halfway, dtype=F32) / head_size)
    angles = places.astype(F32)[:, None] * frequency[None, :]
    cos_part, sin_part = jnp.cos(angles), jnp.sin(angles)
    return (
        jnp.concatenate([cos_part, cos_part], axis=1),
        jnp.concatenate([-sin_part, sin_part], axis=1),
    )


def turn_plain(values, cos_wide, sin_wide):
    return values * cos_wide + jnp.roll(values, values.shape[1] // 2, 1) * sin_wide


def per_device(
    residual,
    segments,
    routes,
    norm_attention,
    query_weight,
    key_projection_matrix,
    value_projection_matrix,
    query_gain,
    key_gain,
    out_weight,
    norm_experts,
    router_weight,
    gate_weight,
    up_weight,
    down_weight,
    grad_output,
):
    row_count = lax.axis_size("row")
    col_count = lax.axis_size("col")
    row_place = lax.axis_index("row")
    col_place = lax.axis_index("col")
    model_width = norm_attention.shape[0]
    feature_width = model_width // row_count
    head_size = query_gain.shape[0]
    heads_here = query_weight.shape[1] // head_size
    query_width = heads_here * head_size
    kv_heads = key_projection_matrix.shape[1] // head_size
    query_group_width = heads_here * row_count // kv_heads
    members = query_group_width // heads_here
    kv_index = row_place * heads_here // query_group_width
    member_place = row_place % members
    share_width = head_size // members
    column_mask = (jnp.arange(head_size, dtype=jnp.int32) // share_width == member_place).astype(
        F32
    )
    experts = gate_weight.shape[0] * row_count * col_count
    expert = row_place * col_count + col_place
    chips = col_count // 2
    token_rows = residual.shape[0]
    rows = SEQUENCE_TOKENS
    chunks = token_rows // rows
    top_count = routes.shape[1]
    capacity = max(2, 5 * rows * top_count // (4 * experts))
    row_start = row_place * feature_width
    labels = jnp.arange(experts, dtype=jnp.int32)
    scalars = jnp.stack([expert, row_place]).astype(jnp.int32)
    row_scalar = row_place.astype(jnp.int32).reshape(1)
    key_part = lax.dynamic_slice_in_dim(key_projection_matrix, kv_index * head_size, head_size, 1)
    value_part = lax.dynamic_slice_in_dim(
        value_projection_matrix, kv_index * head_size, head_size, 1
    )

    def chunk(array, number):
        return array[number * rows : (number + 1) * rows]

    link = Link()
    input_pieces = ring_pieces(residual)
    projection = col_assemble(
        jnp.concatenate([query_weight, key_part, value_part], axis=1), 0, row_start, link
    )
    routes_all = jnp.stack(col_gather(routes, link)).reshape(col_count * chunks, rows, top_count)
    out_full = col_assemble(out_weight, 1, row_start, link)
    arrived = [block for piece in input_pieces[1:] for block in piece]
    grad_pieces = ring_pieces(after(grad_output, *arrived))
    grads_cols = [col_gather(joined(grad_pieces, n, rows), link) for n in range(chunks)]

    gain_one = rolled(norm_attention, row_start)
    gain_two = rolled(norm_experts, row_start)
    router = rolled(router_weight, row_start)
    router = jnp.pad(router, ((0, 0), (0, LANES - experts)))
    cos_all, sin_all = rotary(positions(segments), head_size)
    tables = [(chunk(cos_all, n), chunk(sin_all, n)) for n in range(chunks)]
    segs = [(chunk(segments, n)[None, :], chunk(segments, n)[:, None]) for n in range(chunks)]
    head_gains = (query_gain[None, :], key_gain[None, :])
    masks, slots, slots_t = (
        table.reshape(col_count, chunks, *table.shape[1:])
        for table in route_tables(scalars, routes_all)
    )

    state = [{} for _ in range(chunks)]

    for n in range(chunks):
        s = state[n]
        s["normed_full"], s["scale_one"] = assemble_norm(
            *chunk_pieces(input_pieces, n, rows), rows, gain_one[None, :]
        )
        s["projected"] = mm(s["normed_full"], projection)
        s["mixed"] = attention_forward(
            s["projected"], heads_here, *segs[n], *tables[n], *head_gains
        )
        partial = mm(s["mixed"], out_full).astype(BF16)
        s["hidden"] = chunk(residual, n).astype(F32) + ring_scatter(partial)

    for n in range(chunks):
        s = state[n]
        pieces = ring_pieces(s["hidden"].astype(BF16))
        s["normed_two"], s["scale_two"] = assemble_norm(
            *chunk_pieces(pieces, 0, rows), rows, gain_two[None, :]
        )
        s["tokens"] = col_gather(s["normed_two"], link)

    kept = None
    for place in range(chips):
        for n in range(chunks):
            s = state[n]
            two = slice(2 * place, 2 * place + 2)
            found = expert_pair(
                n * chips + place,
                chunks * chips,
                capacity,
                scalars,
                slots[two, n],
                slots_t[two, n],
                masks[two, n],
                router,
                s["tokens"][two],
                grads_cols[n][two],
                (gate_weight[0], up_weight[0], down_weight[0]),
                kept,
            )
            kept = found[7:]
            s.setdefault("y", []).append(chip_total(found[0], found[1]))
            s.setdefault("x", []).append(chip_total(found[2], found[3]))
            s.setdefault("small", []).append(found[4])
            if place == 0:
                s["logits"], s["gates"] = found[5][:, :experts], found[6][:, :experts]
    grad_gate = lax.dot_general(kept[0], kept[3], TN, preferred_element_type=F32).astype(BF16)
    grad_up = lax.dot_general(kept[0], kept[4], TN, preferred_element_type=F32).astype(BF16)
    grad_down = lax.dot_general(kept[2], kept[1], TN, preferred_element_type=F32).astype(BF16)
    own_grads = (grad_gate, grad_up, grad_down)
    other_grads = []
    for own in own_grads:
        other_grads.append(swapped(after(own, *other_grads[-1:]), "dp", 0))

    for n in range(chunks):
        s = state[n]
        small = jnp.stack(s["small"])
        small = jnp.concatenate(
            [
                jnp.where((labels == expert)[:, None], small[:, :, 0, None, :], 0.0),
                small[:, :, 1, None, :],
            ],
            axis=2,
        )
        small = small[:, 0] + swapped(small[:, 1], "col", 0)
        total = chips_total(s["x"], link).astype(BF16)
        s["small"] = butterfly(chips_total([small[p] for p in range(chips)], link), "row")
        if n == chunks - 1:
            total = after(total, *own_grads)
        s["normed_two_grad"] = ring_scatter(total)
    for n in range(chunks):
        s = state[n]
        s["mixture"] = ring_scatter(chips_total(s["y"], link).astype(BF16))

    acc_projection = acc_out = None
    acc_router = jnp.zeros((feature_width, experts), F32)
    acc_gain_one = jnp.zeros((model_width,), F32)
    acc_gain_two = jnp.zeros((feature_width,), F32)
    acc_query_gain = jnp.zeros((head_size,), F32)
    acc_key_gain = jnp.zeros((head_size,), F32)
    output_blocks, input_blocks = [], []
    for n in range(chunks):
        s = state[n]
        hidden = s["hidden"]
        output_blocks.append((hidden + s["mixture"]).astype(BF16))
        gate_dots = s["small"][:experts].T
        slot_inner = s["small"][experts]
        pick_grad = s["gates"] * (
            gate_dots - jnp.sum(s["gates"] * gate_dots, axis=1, keepdims=True)
        )
        logit_grad = pick_grad.astype(BF16)
        acc_router = acc_router + lax.dot_general(
            s["normed_two"][:, :feature_width], logit_grad, TN, preferred_element_type=F32
        )
        normed_two_grad = s["normed_two_grad"] + lax.dot_general(
            logit_grad, router[:feature_width, :experts], NT, preferred_element_type=F32
        )
        inner_two = slot_inner[:, None] + jnp.sum(
            logit_grad.astype(F32) * s["logits"], axis=1, keepdims=True
        )
        scale_two = s["scale_two"]
        hidden_total = (
            chunk(grad_output, n).astype(F32)
            + normed_two_grad * gain_two[:feature_width] * scale_two
            - hidden * (scale_two * scale_two * inner_two / model_width)
        )
        acc_gain_two = acc_gain_two + jnp.sum(normed_two_grad * hidden * scale_two, axis=0)
        branch_full = joined(ring_pieces(hidden_total.astype(BF16)), 0, rows)
        if n == chunks - 1:
            branch_full = after(branch_full, other_grads[0])
        mixed_grad = lax.dot_general(
            branch_full, out_full, NT, preferred_element_type=F32
        ).astype(BF16)
        projected_grad, key_grad, value_grad, inner_one, head_terms = attention_backward(
            members == 1, s["projected"], mixed_grad, heads_here, *segs[n], *tables[n], *head_gains
        )
        acc_query_gain = acc_query_gain + head_terms[0]
        if members == 1:
            acc_key_gain = acc_key_gain + head_terms[1]
        else:
            for bit in range(members.bit_length() - 1):
                key_grad = key_grad + swapped(key_grad, "row", bit)
                value_grad = value_grad + swapped(value_grad, "row", bit)
            key_pre = s["projected"][:, query_width : query_width + head_size]
            value_pre = s["projected"][:, query_width + head_size :]
            key_grad, key_terms = norm_back(
                key_pre, head_gains[1], turn_plain(key_grad, tables[n][0], -tables[n][1])
            )
            acc_key_gain = acc_key_gain + column_mask * jnp.sum(key_terms, axis=0)
            key_low = (column_mask * key_grad).astype(BF16)
            value_low = (column_mask * value_grad).astype(BF16)
            projected_grad = jnp.concatenate(
                [projected_grad[:, :query_width], key_low, value_low], axis=1
            )
            inner_one = inner_one + jnp.sum(
                key_low.astype(F32) * key_pre + value_low.astype(F32) * value_pre,
                axis=1,
                keepdims=True,
            )
        partial = lax.dot_general(
            projected_grad, projection, NT, preferred_element_type=F32
        ).astype(BF16)
        normed_one_grad = ring_scatter(partial)
        inner_one = butterfly(inner_one[:, 0], "row")[:, None]
        out_here = lax.dot_general(s["mixed"], branch_full, TN, preferred_element_type=F32)
        acc_out = out_here if n == 0 else acc_out + out_here
        acc_gain_one = acc_gain_one + jnp.sum(
            partial.astype(F32) * s["normed_full"].astype(F32), axis=0
        )
        if n == chunks - 1:
            projected_grad = after(projected_grad, other_grads[1])
        projection_here = lax.dot_general(
            s["normed_full"], projected_grad, TN, preferred_element_type=F32
        )
        acc_projection = projection_here if n == 0 else acc_projection + projection_here
        scale_one = s["scale_one"]
        input_blocks.append(
            hidden_total
            + normed_one_grad * gain_one[:feature_width] * scale_one
            - chunk(residual, n).astype(F32)
            * (scale_one * scale_one * inner_one / model_width)
        )

    grad_gate, grad_up, grad_down = (
        unrolled_sum(own, other, row_scalar, row_count, axis)[None]
        for own, other, axis in zip(own_grads, other_grads, (0, 0, 1))
    )
    grad_out_weight = pair_total(col_share(acc_out.astype(BF16), 1, row_start, link))
    projection_share = pair_total(col_share(acc_projection.astype(BF16), 0, row_start, link))
    grad_query = projection_share[:, :query_width]
    share = projection_share[:, query_width:].astype(BF16)
    shares = rolled(joined(ring_pieces(share), 0, share.shape[0]), -row_place * 2 * head_size, 1)
    shares = shares.astype(F32).reshape(-1, kv_heads, members, 2, head_size).sum(axis=2)
    grad_key = shares[:, :, 0].reshape(-1, kv_heads * head_size)
    grad_value = shares[:, :, 1].reshape(-1, kv_heads * head_size)

    gain_two_full = lax.dynamic_update_slice_in_dim(
        jnp.zeros((model_width,), F32), acc_gain_two, row_start, 0
    )
    router_full = lax.dynamic_update_slice_in_dim(
        jnp.zeros((model_width, experts), F32), acc_router, row_start, 0
    )
    sizes = (model_width, model_width, head_size, head_size, model_width * experts)
    flat = jnp.concatenate(
        [
            rolled(acc_gain_one / gain_one, -row_start),
            gain_two_full,
            acc_query_gain,
            acc_key_gain,
            router_full.reshape(-1),
        ]
    )
    for axis in ("col", "row", "dp"):
        flat = butterfly(flat, axis)
    totals, start = [], 0
    for size in sizes:
        totals.append(flat[start : start + size])
        start += size
    return (
        jnp.concatenate(output_blocks, axis=0),
        jnp.concatenate(input_blocks, axis=0),
        totals[0],
        grad_query,
        grad_key,
        grad_value,
        totals[2],
        totals[3],
        grad_out_weight,
        totals[1],
        totals[4].reshape(model_width, experts),
        grad_gate,
        grad_up,
        grad_down,
    )


def solution(mesh):
    in_specs = (
        P(("dp", "col"), "row"),
        P(("dp", "col")),
        P(("dp", "col"), None),
        P(),
        P("col", "row"),
        P("col", None),
        P("col", None),
        P(),
        P(),
        P("row", "col"),
        P(),
        P(),
        P(("row", "col"), None, None),
        P(("row", "col"), None, None),
        P(("row", "col"), None, None),
        P(("dp", "col"), "row"),
    )
    out_specs = (
        P(("dp", "col"), "row"),
        P(("dp", "col"), "row"),
        P(),
        P("col", "row"),
        P("col", None),
        P("col", None),
        P(),
        P(),
        P("row", "col"),
        P(),
        P(),
        P(("row", "col"), None, None),
        P(("row", "col"), None, None),
        P(("row", "col"), None, None),
    )
    return jax.shard_map(
        per_device, mesh=mesh, in_specs=in_specs, out_specs=out_specs, check_vma=False
    )
```

```python
import functools

import jax
import jax.numpy as jnp
from jax import lax
from jax.experimental import pallas as pl
from jax.experimental.pallas import tpu as pltpu
from jax.sharding import PartitionSpec as P

SEQUENCE_TOKENS = 512
EPSILON = 1e-06
ROPE_BASE = 1000000.0
MASKED = -1e30
LANES = 128
BF16 = jnp.bfloat16
F32 = jnp.float32
NT = (((1,), (1,)), ((), ()))
TN = (((0,), (0,)), ((), ()))

def mm(left, right):
    return jnp.dot(left, right, preferred_element_type=F32)

def mm_nt(left, right):
    return lax.dot_general(left, right, NT, preferred_element_type=F32)

def mm_tn(left, right):
    return lax.dot_general(left, right, (((0,), (0,)), ((), ())), preferred_element_type=F32)

def turn(values, cos_wide, sin_wide):
    return values * cos_wide + pltpu.roll(values, values.shape[1] // 2, 1) * sin_wide

def unit(values):
    return lax.rsqrt(jnp.mean(values * values, axis=1, keepdims=True) + EPSILON)

def sequence_bias(segs_ref, segs_t_ref):
    rows = segs_ref.shape[1]
    before = lax.broadcasted_iota(jnp.int32, (rows, rows), 1) <= lax.broadcasted_iota(jnp.int32, (rows, rows), 0)
    same = segs_t_ref[...] == segs_ref[...]
    return jnp.where(jnp.logical_and(same, before), 0.0, MASKED)

def block_probs(query, key, bias, scale):
    scores = mm_nt(query, key) * scale + bias
    weights = jnp.exp(scores - jnp.max(scores, axis=1, keepdims=True))
    return weights * (1.0 / jnp.sum(weights, axis=1, keepdims=True))

def attention_forward_kernel(scale, q_ref, k_ref, v_ref, segs_ref, segs_t_ref, cos_ref, sin_ref, q_gain_ref, k_gain_ref, out_ref, bias, key, value):
    head = k_ref.shape[1]
    rows = q_ref.shape[0]
    half = rows // 2
    cos_wide, sin_wide = cos_ref[...], sin_ref[...]

    @pl.when(pl.program_id(0) == 0)
    def _():
        bias[...] = sequence_bias(segs_ref, segs_t_ref)
        k_pre = k_ref[...]
        key[...] = turn(k_pre * unit(k_pre) * k_gain_ref[...], cos_wide, sin_wide).astype(BF16)
        value[...] = v_ref[...].astype(BF16)

    for h in range(q_ref.shape[1] // head):
        lanes = slice(h * head, (h + 1) * head)
        q_pre = q_ref[:, lanes]
        query = turn(q_pre * unit(q_pre) * q_gain_ref[...], cos_wide, sin_wide).astype(BF16)
        for part in range(2):
            at, keys = slice(part * half, (part + 1) * half), slice(0, (part + 1) * half)
            probs = block_probs(query[at], key[keys, :], bias[at, keys], scale)
            out_ref[at, lanes] = mm(probs.astype(BF16), value[keys, :]).astype(BF16)

def attention_forward(projected, heads, segs, segs_t, cos_wide, sin_wide, q_gain, k_gain):
    rows = projected.shape[0]
    head = q_gain.shape[1]
    pair = 2 if heads % 2 == 0 else 1
    fixed = lambda *shape: pl.BlockSpec(shape, lambda i: (0,) * len(shape))
    return pl.pallas_call(
        functools.partial(attention_forward_kernel, head ** -0.5),
        grid=(heads // pair,),
        out_shape=jax.ShapeDtypeStruct((rows, heads * head), BF16),
        in_specs=[
            pl.BlockSpec((rows, pair * head), lambda i: (0, i)),
            pl.BlockSpec((rows, head), lambda i: (0, heads)),
            pl.BlockSpec((rows, head), lambda i: (0, heads + 1)),
            fixed(1, rows), fixed(rows, 1), fixed(rows, head), fixed(rows, head), fixed(1, head), fixed(1, head),
        ],
        out_specs=pl.BlockSpec((rows, pair * head), lambda i: (0, i)),
        scratch_shapes=[pltpu.VMEM((rows, rows), F32), pltpu.VMEM((rows, head), BF16), pltpu.VMEM((rows, head), BF16)],
        compiler_params=pltpu.CompilerParams(vmem_limit_bytes=48 << 20),
        cost_estimate=pl.CostEstimate(flops=10000000000, bytes_accessed=10000000, transcendentals=0),
        name="attention_forward",
    )(projected, projected, projected, segs, segs_t, cos_wide, sin_wide, q_gain, k_gain)

def norm_back(values, gain, upstream):
    factor = unit(values)
    weighted = upstream * gain
    inner = jnp.mean(weighted * values, axis=1, keepdims=True)
    return weighted * factor - values * (factor * factor * factor * inner), upstream * values * factor

def attention_backward_kernel(scale, finish, q_ref, k_ref, v_ref, g_ref, segs_ref, segs_t_ref, cos_ref, sin_ref, q_gain_ref, k_gain_ref,
                              out_ref, key_ref, value_ref, inner_ref, gains_ref, bias, key, value, inner):
    head = k_ref.shape[1]
    rows = q_ref.shape[0]
    half = rows // 2
    cos_wide, sin_wide = cos_ref[...], sin_ref[...]
    step, steps = pl.program_id(0), pl.num_programs(0)
    pair = q_ref.shape[1] // head

    @pl.when(step == 0)
    def _():
        bias[...] = sequence_bias(segs_ref, segs_t_ref)
        k_pre = k_ref[...]
        key[...] = turn(k_pre * unit(k_pre) * k_gain_ref[...], cos_wide, sin_wide).astype(BF16)
        value[...] = v_ref[...].astype(BF16)
        key_ref[...] = jnp.zeros_like(key_ref)
        value_ref[...] = jnp.zeros_like(value_ref)
        inner[...] = jnp.zeros_like(inner)
        gains_ref[...] = jnp.zeros_like(gains_ref)

    for h in range(pair):
        lanes = slice(h * head, (h + 1) * head)
        q_pre = q_ref[:, lanes]
        query = turn(q_pre * unit(q_pre) * q_gain_ref[...], cos_wide, sin_wide).astype(BF16)
        grads = []
        for part in range(2):
            at, keys = slice(part * half, (part + 1) * half), slice(0, (part + 1) * half)
            probs = block_probs(query[at], key[keys, :], bias[at, keys], scale)
            upstream = g_ref[at, lanes]
            prob_grad = mm_nt(upstream, value[keys, :])
            score_grad = (probs * (prob_grad - jnp.sum(probs * prob_grad, axis=1, keepdims=True))).astype(BF16)
            grads.append(mm(score_grad, key[keys, :]) * scale)
            key_ref[keys, :] += mm_tn(score_grad, query[at]) * scale
            value_ref[keys, :] += mm_tn(probs.astype(BF16), upstream)
        query_grad = turn(jnp.concatenate(grads, axis=0), cos_wide, -sin_wide)
        q_grad, terms = norm_back(q_pre, q_gain_ref[...], query_grad)
        low = q_grad.astype(BF16)
        out_ref[:, pl.ds(pl.multiple_of((step * pair + h) * head, head), head)] = low
        inner[...] += low.astype(F32) * q_pre
        gains_ref[0:1, :] += jnp.sum(terms, axis=0, keepdims=True)

    @pl.when(step == steps - 1)
    def _():
        total = jnp.sum(inner[...], axis=1, keepdims=True)
        if finish:
            k_pre, v_pre = k_ref[...], v_ref[...]
            k_grad, terms = norm_back(k_pre, k_gain_ref[...], turn(key_ref[...], cos_wide, -sin_wide))
            k_low, v_low = k_grad.astype(BF16), value_ref[...].astype(BF16)
            width = steps * pair * head
            out_ref[:, pl.ds(out_ref.shape[1] - 2 * head, head)] = k_low
            out_ref[:, pl.ds(out_ref.shape[1] - head, head)] = v_low
            gains_ref[1:2, :] = jnp.sum(terms, axis=0, keepdims=True)
            total = total + jnp.sum(k_low.astype(F32) * k_pre + v_low.astype(F32) * v_pre, axis=1, keepdims=True)
        inner_ref[...] = total

def attention_backward(finish, projected, upstream, heads, segs, segs_t, cos_wide, sin_wide, q_gain, k_gain):
    rows = projected.shape[0]
    head = q_gain.shape[1]
    pair = 2 if heads % 2 == 0 else 1
    fixed = lambda *shape: pl.BlockSpec(shape, lambda i: (0,) * len(shape))
    return pl.pallas_call(
        functools.partial(attention_backward_kernel, head ** -0.5, finish),
        grid=(heads // pair,),
        out_shape=[
            jax.ShapeDtypeStruct((rows, (heads + 2) * head), BF16),
            jax.ShapeDtypeStruct((rows, head), F32),
            jax.ShapeDtypeStruct((rows, head), F32),
            jax.ShapeDtypeStruct((rows, 1), F32),
            jax.ShapeDtypeStruct((2, head), F32),
        ],
        in_specs=[
            pl.BlockSpec((rows, pair * head), lambda i: (0, i)),
            pl.BlockSpec((rows, head), lambda i: (0, heads)),
            pl.BlockSpec((rows, head), lambda i: (0, heads + 1)),
            pl.BlockSpec((rows, pair * head), lambda i: (0, i)),
            fixed(1, rows), fixed(rows, 1), fixed(rows, head), fixed(rows, head), fixed(1, head), fixed(1, head),
        ],
        out_specs=[fixed(rows, (heads + 2) * head), fixed(rows, head), fixed(rows, head), fixed(rows, 1), fixed(2, head)],
        scratch_shapes=[pltpu.VMEM((rows, rows), F32), pltpu.VMEM((rows, head), BF16), pltpu.VMEM((rows, head), BF16), pltpu.VMEM((rows, head), F32)],
        compiler_params=pltpu.CompilerParams(vmem_limit_bytes=48 << 20),
        cost_estimate=pl.CostEstimate(flops=20000000000, bytes_accessed=10000000, transcendentals=0),
        name="attention_backward",
    )(projected, projected, projected, upstream, segs, segs_t, cos_wide, sin_wide, q_gain, k_gain)

def norm_kernel(in_ref, gain_ref, out_ref, scale_ref):
    wide = in_ref[...].astype(F32)
    scale = unit(wide)
    scale_ref[...] = scale
    out_ref[...] = (wide * scale * gain_ref[...]).astype(BF16)


def normalized(values, gain):
    rows, width = values.shape
    block = min(128, rows)
    return pl.pallas_call(
        norm_kernel,
        grid=(rows // block,),
        out_shape=[jax.ShapeDtypeStruct((rows, width), BF16), jax.ShapeDtypeStruct((rows, 1), F32)],
        in_specs=[
            pl.BlockSpec((block, width), lambda i: (i, 0)),
            pl.BlockSpec((1, width), lambda i: (0, 0)),
        ],
        out_specs=[
            pl.BlockSpec((block, width), lambda i: (i, 0)),
            pl.BlockSpec((block, 1), lambda i: (i, 0)),
        ],
        compiler_params=pltpu.CompilerParams(vmem_limit_bytes=32 << 20),
        cost_estimate=pl.CostEstimate(flops=2000000000, bytes_accessed=8000000, transcendentals=0),
        name="normalized",
    )(values, gain)


def norm_pieces_kernel(count, scalars_ref, *refs):
    pieces, gain_ref, out_ref, scale_ref = refs[:count], refs[count], refs[count + 1], refs[count + 2]
    width = pieces[0].shape[1]
    total = None
    for piece in pieces:
        wide = piece[...].astype(F32)
        part = jnp.sum(wide * wide, axis=1, keepdims=True)
        total = part if total is None else total + part
    scale = lax.rsqrt(total / (width * count) + EPSILON)
    scale_ref[...] = scale
    for i, piece in enumerate(pieces):
        at = pl.ds(pl.multiple_of((scalars_ref[1] + i) % count * width, width), width)
        out_ref[:, at] = (piece[...].astype(F32) * scale * gain_ref[:, at]).astype(BF16)


def normalized_pieces(pieces, offsets, rows, scalars, gain):
    count = len(pieces)
    width = pieces[0].shape[1]
    block = min(128, rows)
    return pl.pallas_call(
        functools.partial(norm_pieces_kernel, count),
        grid=(rows // block,),
        out_shape=[
            jax.ShapeDtypeStruct((rows, width * count), BF16),
            jax.ShapeDtypeStruct((rows, 1), F32),
        ],
        in_specs=[pl.BlockSpec(memory_space=pltpu.SMEM)]
        + [pl.BlockSpec((block, width), lambda i, o=o: (o // block + i, 0)) for o in offsets]
        + [pl.BlockSpec((1, width * count), lambda i: (0, 0))],
        out_specs=[
            pl.BlockSpec((block, width * count), lambda i: (i, 0)),
            pl.BlockSpec((block, 1), lambda i: (i, 0)),
        ],
        compiler_params=pltpu.CompilerParams(vmem_limit_bytes=32 << 20),
        cost_estimate=pl.CostEstimate(flops=2000000000, bytes_accessed=8000000, transcendentals=0),
        name="normalized_pieces",
    )(scalars, *pieces, gain)


def pair_kernel(first, place, experts, scalars_ref, slots_ref, slots_t_ref, mask_ref, router_ref, *refs):
    refs = list(refs)
    token_in, grad_in = refs[0:2], refs[2:4]
    weights_in = refs[4:7]
    del refs[:7]
    if not first:
        del refs[:5]
    y_out, x_out = refs[0:2], refs[2:4]
    small_out, logits_out, gates_out = refs[4:7]
    kept_out = refs[7:12]
    (token, grad, gate_w, up_w, down_w, y_buf, x_buf, rows_in, rows_grad, rows_dy, rows_u, rows_da, rows_db, in_sem, grad_sem, w_sem, out_sem, kept_sem) = refs[12:]
    capacity = rows_in.shape[0] // 2
    tokens, width = token.shape[1:]
    hidden = gate_w.shape[1]
    load_tok = [pltpu.make_async_copy(token_in[g], token.at[g], in_sem.at[g]) for g in range(2)]
    load_grad = [pltpu.make_async_copy(grad_in[g], grad.at[g], grad_sem.at[g]) for g in range(2)]
    load_w = [
        pltpu.make_async_copy(src, dst, w_sem.at[i])
        for i, (src, dst) in enumerate(zip(weights_in, (gate_w, up_w, down_w)))
    ]
    load_tok[0].start()
    load_grad[0].start()
    for load in load_w:
        load.start()
    load_tok[1].start()
    load_grad[1].start()
    expert = scalars_ref[0]
    stores = []
    wide = min(512, width)
    step = 256 if hidden % 256 == 0 else hidden
    chosen_rows, spreads, gate_cols = [], [], []
    for g in range(2):
        load_tok[g].wait()
        logits = mm(token[g], router_ref[...])
        shifted = logits + mask_ref[g].astype(F32)
        weights = jnp.exp(shifted - jnp.max(shifted, axis=1, keepdims=True))
        gates = weights / jnp.sum(weights, axis=1, keepdims=True)
        if g == 0:
            logits_out[...] = logits
            gates_out[...] = gates
        gates_t = gates.T
        lane = lax.broadcasted_iota(jnp.int32, gates_t.shape, 0)
        gate_row = jnp.sum(jnp.where(lane == expert, gates_t, 0.0), axis=0, keepdims=True)
        chosen = lax.broadcasted_iota(jnp.int32, (capacity, tokens), 0) == slots_ref[g]
        slot_gates = jnp.sum(jnp.where(chosen, gate_row, 0.0), axis=1, keepdims=True)
        pick = jnp.where(chosen, 1.0, 0.0).astype(BF16)
        here = slice(g * capacity, (g + 1) * capacity)
        gate_cols.append(slot_gates)
        load_grad[g].wait()

        def gather(j, _):
            at = pl.ds(pl.multiple_of(j * wide, wide), wide)
            rows_in[here, at] = mm(pick, token[g, :, at]).astype(BF16)
            found = mm(pick, grad[g, :, at])
            rows_grad[here, at] = found.astype(BF16)
            rows_dy[here, at] = (slot_gates * found).astype(BF16)
            return 0

        lax.fori_loop(0, width // wide, gather, 0)
    for load in load_w:
        load.wait()
    slot_gates = jnp.concatenate(gate_cols, axis=0)

    def middle(j, _):
        at = pl.ds(pl.multiple_of(j * step, step), step)
        a = mm(rows_in[...], gate_w[:, at])
        b = mm(rows_in[...], up_w[:, at])
        du = mm_nt(rows_dy[...], down_w[at, :]).astype(BF16).astype(F32)
        sig = 1.0 / (1.0 + jnp.exp(-a))
        silu = a * sig
        rows_u[:, at] = (silu * b).astype(BF16)
        rows_da[:, at] = (du * b * sig * (1.0 + a * (1.0 - sig))).astype(BF16)
        rows_db[:, at] = (du * silu).astype(BF16)
        return 0

    lax.fori_loop(0, hidden // step, middle, 0)
    kept_here = pl.ds(place * 2 * capacity, 2 * capacity)
    for i, kept_rows in enumerate((rows_in, rows_dy, rows_u, rows_da, rows_db)):
        store = pltpu.make_async_copy(kept_rows, kept_out[i].at[kept_here, :], kept_sem.at[i])
        store.start()
        stores.append(store)
    spreads = [
        jnp.where(
            lax.broadcasted_iota(jnp.int32, (tokens, capacity), 1) == slots_t_ref[g], 1.0, 0.0
        ).astype(BF16)
        for g in range(2)
    ]

    def back(j, carry):
        dots, inner = carry
        at = pl.ds(pl.multiple_of(j * wide, wide), wide)
        y = mm(rows_u[...], down_w[:, at]).astype(BF16).astype(F32)
        dots = dots + jnp.sum(rows_grad[:, at].astype(F32) * y, axis=1, keepdims=True)
        low = (slot_gates * y).astype(BF16)
        dx = mm_nt(rows_da[...], gate_w[at, :]) + mm_nt(rows_db[...], up_w[at, :])
        inner = inner + jnp.sum(rows_in[:, at].astype(F32) * dx, axis=1, keepdims=True)
        dx_low = dx.astype(BF16)
        for g in range(2):
            here = slice(g * capacity, (g + 1) * capacity)
            y_buf[g, :, at] = mm(spreads[g], low[here]).astype(BF16)
            x_buf[g, :, at] = mm(spreads[g], dx_low[here]).astype(BF16)
        return dots, inner

    nothing = jnp.zeros((2 * capacity, 1), F32)
    dots, inner = lax.fori_loop(0, width // wide, back, (nothing, nothing))
    for g in range(2):
        here = slice(g * capacity, (g + 1) * capacity)
        chosen = lax.broadcasted_iota(jnp.int32, (capacity, tokens), 0) == slots_ref[g]
        small_row = lax.broadcasted_iota(jnp.int32, small_out.shape[1:], 0)
        dots_row = jnp.sum(jnp.where(chosen, dots[here], 0.0), axis=0, keepdims=True)
        inner_row = jnp.sum(jnp.where(chosen, inner[here], 0.0), axis=0, keepdims=True)
        small_out[g] = jnp.where(small_row == expert, dots_row, 0.0) + jnp.where(
            small_row == experts, inner_row, 0.0
        )
        for i, (buf, out) in enumerate(((x_buf, x_out), (y_buf, y_out))):
            store = pltpu.make_async_copy(buf.at[g], out[g], out_sem.at[i, g])
            store.start()
            stores.append(store)
    for store in stores:
        store.wait()


def expert_pair(
    place, places, capacity, experts, scalars, slots, slots_t, mask, router, tokens, grads, weights, kept
):
    rows, width = tokens[0].shape
    hidden = weights[0].shape[1]
    total = places * 2 * capacity
    anywhere = pl.BlockSpec(memory_space=pl.ANY)
    inside = pl.BlockSpec(memory_space=pltpu.VMEM)
    first = kept is None
    small_rows = (experts + 8) // 8 * 8
    dense = jax.ShapeDtypeStruct((rows, width), BF16)
    kept_shapes = [jax.ShapeDtypeStruct((total, w), BF16) for w in (width, width, hidden, hidden, hidden)]
    flat = jax.ShapeDtypeStruct((rows, router.shape[1]), F32)
    out = pl.pallas_call(
        functools.partial(pair_kernel, first, place, experts),
        out_shape=[dense] * 4 + [jax.ShapeDtypeStruct((2, small_rows, rows), F32), flat, flat] + kept_shapes,
        in_specs=[pl.BlockSpec(memory_space=pltpu.SMEM)] + [inside] * 4 + [anywhere] * (7 if first else 12),
        out_specs=[anywhere] * 4 + [inside] * 3 + [anywhere] * 5,
        input_output_aliases={} if first else {12 + i: 7 + i for i in range(5)},
        scratch_shapes=[
            pltpu.VMEM((2, rows, width), BF16),
            pltpu.VMEM((2, rows, width), BF16),
            pltpu.VMEM((width, hidden), BF16),
            pltpu.VMEM((width, hidden), BF16),
            pltpu.VMEM((hidden, width), BF16),
            pltpu.VMEM((2, rows, width), BF16),
            pltpu.VMEM((2, rows, width), BF16),
            pltpu.VMEM((2 * capacity, width), BF16),
            pltpu.VMEM((2 * capacity, width), BF16),
            pltpu.VMEM((2 * capacity, width), BF16),
            pltpu.VMEM((2 * capacity, hidden), BF16),
            pltpu.VMEM((2 * capacity, hidden), BF16),
            pltpu.VMEM((2 * capacity, hidden), BF16),
            pltpu.SemaphoreType.DMA((2,)),
            pltpu.SemaphoreType.DMA((2,)),
            pltpu.SemaphoreType.DMA((3,)),
            pltpu.SemaphoreType.DMA((2, 2)),
            pltpu.SemaphoreType.DMA((5,)),
        ],
        compiler_params=pltpu.CompilerParams(vmem_limit_bytes=56 << 20),
        cost_estimate=pl.CostEstimate(flops=36000000000, bytes_accessed=10000000, transcendentals=0),
        name="expert_pair",
    )(scalars, slots, slots_t, mask, router, *tokens, *grads, *weights, *([] if first else kept))
    return out


def route_kernel(expert_ref, routes_ref, mask_ref, slots_ref, slots_t_ref):
    rows, top_count = routes_ref.shape[1:]
    routes = routes_ref[0]
    lanes = lax.broadcasted_iota(jnp.int32, (rows, LANES), 1)
    chosen = routes[:, 0:1] == lanes
    for k in range(1, top_count):
        chosen = jnp.logical_or(chosen, routes[:, k : k + 1] == lanes)
    mask_ref[0] = jnp.where(chosen, 0.0, MASKED).astype(BF16)
    below = lax.broadcasted_iota(jnp.int32, (rows, rows), 1) <= lax.broadcasted_iota(
        jnp.int32, (rows, rows), 0
    )
    ones = jnp.where(chosen, 1.0, 0.0)
    ranks = mm(jnp.where(below, 1.0, 0.0).astype(BF16), ones.astype(BF16))
    slots = jnp.where(chosen, ranks - 1.0, -1.0)
    here = lanes == expert_ref[0]
    slots_t_ref[0] = jnp.max(jnp.where(here, slots, -1.0), axis=1, keepdims=True).astype(jnp.int32)
    lane_first = lax.broadcasted_iota(jnp.int32, (LANES, rows), 0)
    slots_ref[0] = jnp.max(
        jnp.where(lane_first == expert_ref[0], slots.T, -1.0), axis=0, keepdims=True
    ).astype(jnp.int32)


def route_tables(scalars, routes):
    blocks, rows, top_count = routes.shape
    return pl.pallas_call(
        route_kernel,
        grid=(blocks,),
        out_shape=[
            jax.ShapeDtypeStruct((blocks, rows, LANES), BF16),
            jax.ShapeDtypeStruct((blocks, 1, rows), jnp.int32),
            jax.ShapeDtypeStruct((blocks, rows, 1), jnp.int32),
        ],
        in_specs=[
            pl.BlockSpec(memory_space=pltpu.SMEM),
            pl.BlockSpec((1, rows, top_count), lambda i: (i, 0, 0)),
        ],
        out_specs=[
            pl.BlockSpec((1, rows, LANES), lambda i: (i, 0, 0)),
            pl.BlockSpec((1, 1, rows), lambda i: (i, 0, 0)),
            pl.BlockSpec((1, rows, 1), lambda i: (i, 0, 0)),
        ],
        compiler_params=pltpu.CompilerParams(vmem_limit_bytes=32 << 20),
        cost_estimate=pl.CostEstimate(flops=1000000000, bytes_accessed=1000000, transcendentals=0),
        name="route_tables",
    )(scalars, routes)


def place_kernel(axis, starts_ref, *refs):
    out = refs[-1]
    for i, piece in enumerate(refs[:-1]):
        width = piece.shape[axis]
        at = pl.ds(pl.multiple_of(starts_ref[i] * width, width), width)
        if axis == 0:
            out[at, :] = piece[...]
        else:
            out[:, at] = piece[...]


def placed(pieces, starts, axis):
    shape = list(pieces[0].shape)
    shape[axis] *= len(pieces)
    inside = pl.BlockSpec(memory_space=pltpu.VMEM)
    return pl.pallas_call(
        functools.partial(place_kernel, axis),
        out_shape=jax.ShapeDtypeStruct(tuple(shape), pieces[0].dtype),
        in_specs=[pl.BlockSpec(memory_space=pltpu.SMEM)] + [inside] * len(pieces),
        out_specs=inside,
        compiler_params=pltpu.CompilerParams(vmem_limit_bytes=32 << 20),
        cost_estimate=pl.CostEstimate(flops=1000000, bytes_accessed=10000000, transcendentals=0),
        name="placed",
    )(starts, *pieces)


def halves_kernel(own_ref, one_ref, two_ref, out_ref):
    early = pl.program_id(0) < pl.num_programs(0) // 2

    @pl.when(early)
    def _():
        out_ref[...] = own_ref[...].astype(F32) + one_ref[...].astype(F32)

    @pl.when(jnp.logical_not(early))
    def _():
        out_ref[...] = own_ref[...].astype(F32) + two_ref[...].astype(F32)


def halves_sum(own, one, two):
    rows, width = own.shape
    half = 2
    block = rows // (2 * half)
    return pl.pallas_call(
        halves_kernel,
        grid=(2 * half,),
        out_shape=jax.ShapeDtypeStruct((rows, width), F32),
        in_specs=[
            pl.BlockSpec((block, width), lambda i: (i, 0)),
            pl.BlockSpec((block, width), lambda i: (jnp.minimum(i, half - 1), 0)),
            pl.BlockSpec((block, width), lambda i: (jnp.maximum(i - half, 0), 0)),
        ],
        out_specs=pl.BlockSpec((block, width), lambda i: (i, 0)),
        compiler_params=pltpu.CompilerParams(vmem_limit_bytes=32 << 20),
        cost_estimate=pl.CostEstimate(flops=4000000000, bytes_accessed=12000000, transcendentals=0),
        name="halves_sum",
    )(own, one, two)


def moved(block, axis, by):
    count = lax.axis_size(axis)
    return lax.ppermute(block, axis, [(i, (i + by) % count) for i in range(count)])


def swapped(block, axis, bit):
    count = lax.axis_size(axis)
    return lax.ppermute(block, axis, [(i, i ^ (1 << bit)) for i in range(count)])


def butterfly(values, axis):
    for bit in range(lax.axis_size(axis).bit_length() - 1):
        values = values + swapped(values, axis, bit)
    return values


def ring_pieces(block):
    count = lax.axis_size("row")
    pieces = [[block]] + [None] * (count - 1)
    from_left = from_right = block
    half = block.shape[0] // 2
    for step in range(1, count // 2):
        from_left = moved(from_left, "row", 1)
        from_right = moved(from_right, "row", -1)
        pieces[count - step] = [from_left]
        pieces[step] = [from_right]
    if count > 1:
        pieces[count // 2] = [
            moved(from_left[:half], "row", 1),
            moved(from_right[half:], "row", -1),
        ]
    return pieces


def chunk_pieces(pieces, number, rows):
    blocks, offsets = [], []
    for piece in pieces:
        tall = piece[0].shape[0]
        if len(piece) == 1:
            blocks.append(piece[0])
            offsets.append(number * rows)
        elif tall >= rows:
            blocks.append(piece[number * rows // tall])
            offsets.append(number * rows % tall)
        else:
            blocks.append(jnp.concatenate(piece, axis=0))
            offsets.append(number * rows)
    return blocks, offsets


def row_gather(block):
    return lax.all_gather(block, "row", axis=block.ndim - 1, tiled=True)


def row_scatter(partial):
    return lax.psum_scatter(partial, "row", scatter_dimension=1, tiled=True).astype(F32)


def after(value, *others):
    return lax.optimization_barrier((value,) + others)[0]


class Link:
    def __init__(self):
        self.last = ()

    def moved(self, block, by):
        block = moved(after(block, *self.last), "col", by)
        self.last = (block,)
        return block


class PairLink:
    def __init__(self):
        self.last = ()

    def swapped(self, block):
        block = swapped(after(block, *self.last), "dp", 0)
        self.last = (block,)
        return block


def col_gather(block, link):
    count = lax.axis_size("col")
    pieces = []
    for step in range(count // 2):
        same = block if step == 0 else link.moved(block, 2 * step)
        pieces += [same, swapped(same, "col", 0)]
    return pieces


def added(*parts):
    total = parts[0].astype(F32)
    for part in parts[1:]:
        total = total + part.astype(F32)
    return total.astype(parts[0].dtype)


def chips_total(totals, link, *others):
    parts = list(totals[0])
    for step in range(1, len(totals)):
        parts.append(after(link.moved(added(*totals[step]), -2 * step), *others))
    return added(*parts)


def col_order():
    count = lax.axis_size("col")
    place = lax.axis_index("col")
    chip, core = place // 2, place % 2
    order = []
    for step in range(count // 2):
        back = (chip - step) % (count // 2) * 2
        order += [back + core, back + 1 - core]
    return order


def col_assemble(block, axis, link):
    return placed(col_gather(block, link), jnp.stack(col_order()).astype(jnp.int32), axis)


def col_share(partial, axis, link):
    count = lax.axis_size("col")
    width = partial.shape[axis] // count
    pieces = [
        lax.dynamic_slice_in_dim(partial, place * width, width, axis)
        for place in col_order()
    ]
    return chips_total(
        [
            (pieces[2 * step], swapped(pieces[2 * step + 1], "col", 0))
            for step in range(count // 2)
        ],
        link,
    )


def positions(segment_ids):
    places = jnp.arange(segment_ids.shape[0], dtype=jnp.int32)
    earlier = jnp.concatenate([segment_ids[:1] - 1, segment_ids[:-1]])
    starts = jnp.logical_or(segment_ids != earlier, places % SEQUENCE_TOKENS == 0)
    opening = lax.cummax(jnp.where(starts, places, 0), axis=0)
    return places - opening


def rotary(places, head_size):
    halfway = head_size // 2
    frequency = ROPE_BASE ** (-2.0 * jnp.arange(halfway, dtype=F32) / head_size)
    angles = places.astype(F32)[:, None] * frequency[None, :]
    cos_part, sin_part = jnp.cos(angles), jnp.sin(angles)
    return (
        jnp.concatenate([cos_part, cos_part], axis=1),
        jnp.concatenate([-sin_part, sin_part], axis=1),
    )


def turn_plain(values, cos_wide, sin_wide):
    return values * cos_wide + jnp.roll(values, values.shape[1] // 2, 1) * sin_wide


def per_device(
    residual,
    segments,
    routes,
    norm_attention,
    query_weight,
    key_projection_matrix,
    value_projection_matrix,
    query_gain,
    key_gain,
    out_weight,
    norm_experts,
    router_weight,
    gate_weight,
    up_weight,
    down_weight,
    grad_output,
):
    row_count = lax.axis_size("row")
    col_count = lax.axis_size("col")
    row_place = lax.axis_index("row")
    col_place = lax.axis_index("col")
    model_width = norm_attention.shape[0]
    feature_width = model_width // row_count
    head_size = query_gain.shape[0]
    heads_here = query_weight.shape[1] // head_size
    query_width = heads_here * head_size
    kv_heads = key_projection_matrix.shape[1] // head_size
    query_group_width = heads_here * row_count // kv_heads
    members = query_group_width // heads_here
    kv_index = row_place * heads_here // query_group_width
    member_place = row_place % members
    share_width = head_size // members
    column_mask = (jnp.arange(head_size, dtype=jnp.int32) // share_width == member_place).astype(
        F32
    )
    experts = gate_weight.shape[0] * row_count * col_count
    expert = row_place * col_count + col_place
    chips = col_count // 2
    token_rows = residual.shape[0]
    rows = SEQUENCE_TOKENS
    chunks = token_rows // rows
    top_count = routes.shape[1]
    capacity = max(2, 5 * rows * top_count // (4 * experts))
    row_start = row_place * feature_width
    labels = jnp.arange(experts, dtype=jnp.int32)
    scalars = jnp.stack([expert, row_place]).astype(jnp.int32)
    key_part = lax.dynamic_slice_in_dim(key_projection_matrix, kv_index * head_size, head_size, 1)
    value_part = lax.dynamic_slice_in_dim(
        value_projection_matrix, kv_index * head_size, head_size, 1
    )

    def chunk(array, number):
        return array[number * rows : (number + 1) * rows]

    link = Link()
    input_pieces = ring_pieces(residual)
    grads_full = [row_gather(chunk(grad_output, n)) for n in range(chunks)]
    projection = col_assemble(
        jnp.concatenate([query_weight, key_part, value_part], axis=1), 0, link
    )
    routes_all = jnp.stack(col_gather(routes, link)).reshape(col_count * chunks, rows, top_count)
    out_full = col_assemble(out_weight, 1, link)
    grads_cols = [None] * chunks
    for n in range(chunks):
        grads_cols[n] = col_gather(grads_full[n], link)
    grads_far = [[g for g in grads_cols[n][2::2]] for n in range(chunks)]

    gain_one = lax.dynamic_slice_in_dim(norm_attention, row_start, feature_width)
    gain_two = lax.dynamic_slice_in_dim(norm_experts, row_start, feature_width)
    router_rows = lax.dynamic_slice_in_dim(router_weight, row_start, feature_width, 0)
    router = jnp.pad(router_weight, ((0, 0), (0, LANES - experts)))
    cos_all, sin_all = rotary(positions(segments), head_size)
    tables = [(chunk(cos_all, n), chunk(sin_all, n)) for n in range(chunks)]
    segs = [(chunk(segments, n)[None, :], chunk(segments, n)[:, None]) for n in range(chunks)]
    head_gains = (query_gain[None, :], key_gain[None, :])
    state = [{} for _ in range(chunks)]

    for n in range(chunks):
        s = state[n]
        s["normed_full"], s["scale_one"] = normalized_pieces(
            *chunk_pieces(input_pieces, n, rows), rows, scalars, norm_attention[None, :]
        )
        normed = s["normed_full"] if n == 0 else after(s["normed_full"], *grads_far[n - 1])
        s["projected"] = mm(normed, projection)
        s["mixed"] = attention_forward(
            s["projected"], heads_here, *segs[n], *tables[n], *head_gains
        )
        partial = mm(s["mixed"], out_full).astype(BF16)
        partial = after(partial, grads_full[n])
        summed = row_scatter(partial)
        if n == chunks - 1:
            summed = after(summed, *grads_far[n])
        s["hidden"] = chunk(residual, n).astype(F32) + summed
    masks, slots, slots_t = (
        table.reshape(col_count, chunks, *table.shape[1:])
        for table in route_tables(scalars, after(routes_all, partial))
    )

    kept = None

    def run_pair(n, place, *others):
        nonlocal kept
        s = state[n]
        two = slice(2 * place, 2 * place + 2)
        found = expert_pair(
            n * chips + place,
            chunks * chips,
            capacity,
            experts,
            scalars,
            slots[two, n],
            slots_t[two, n],
            masks[two, n],
            after(router, *others),
            s["tokens"][two],
            grads_cols[n][two],
            (gate_weight[0], up_weight[0], down_weight[0]),
            kept,
        )
        kept = found[7:]
        for name, same, other in (
            ("y", found[0], found[1]),
            ("x", found[2], found[3]),
            ("small", found[4][0], found[4][1]),
        ):
            other = swapped(other, "col", 0)
            s.setdefault(name, []).append(
                (same, other) if place == 0 else (added(same, other),)
            )
        if place == 0:
            s["logits"], s["gates"] = found[5][:, :experts], found[6][:, :experts]

    def second_norm(n, *others):
        s = state[n]
        hidden_low = s["hidden"].astype(BF16)
        if n == 0:
            hidden_low = after(hidden_low, masks)
        wide = row_gather(hidden_low)
        s["normed_two"], s["scale_two"] = normalized(
            after(wide, *others), norm_experts[None, :]
        )
        own = s["normed_two"]
        s["tokens"] = [own, swapped(own, "col", 0)]
        s["far"] = [link.moved(own, 2 * step) for step in range(1, chips)]

    def far_tokens(n, *others):
        for block in state[n]["far"]:
            same = after(block, *others)
            state[n]["tokens"] += [same, swapped(same, "col", 0)]

    def to_row(n, *others):
        s = state[n]
        s["small"] = butterfly(chips_total(s["small"], link), "row")
        s["total"] = chips_total(s["x"], link, *others)

    second_norm(0)
    for n in range(chunks):
        s = state[n]
        run_pair(n, 0, *([state[n - 1]["x"][-1][0]] if n > 0 else []))
        spacer = s["small"][0][1]
        if n + 1 < chunks:
            second_norm(n + 1, spacer)
            ahead = (state[n + 1]["normed_two"], spacer)
        else:
            ahead = (spacer,)
        far_tokens(n, spacer)
        if n > 0:
            to_row(n - 1)
            ahead += (state[n - 1]["total"],)
        for place in range(1, chips):
            run_pair(n, place, *ahead)
    acc_router = jnp.zeros((feature_width, experts), F32)
    acc_gain_two = jnp.zeros((feature_width,), F32)
    for n in range(chunks):
        s = state[n]
        if n == chunks - 1:
            to_row(n, *([state[n - 1]["hidden_total"]] if n > 0 else []))
        normed_two_grad = row_scatter(s["total"])
        hidden = s["hidden"]
        gate_dots = s["small"][:experts].T
        slot_inner = s["small"][experts]
        pick_grad = s["gates"] * (
            gate_dots - jnp.sum(s["gates"] * gate_dots, axis=1, keepdims=True)
        )
        logit_grad = pick_grad.astype(BF16)
        shard = lax.dynamic_slice_in_dim(s["normed_two"], row_start, feature_width, 1)
        acc_router = acc_router + lax.dot_general(
            shard, logit_grad, TN, preferred_element_type=F32
        )
        normed_two_grad = normed_two_grad + lax.dot_general(
            logit_grad, router_rows, NT, preferred_element_type=F32
        )
        inner_two = slot_inner[:, None] + jnp.sum(
            logit_grad.astype(F32) * s["logits"], axis=1, keepdims=True
        )
        scale_two = s["scale_two"]
        s["hidden_total"] = (
            chunk(grad_output, n).astype(F32)
            + normed_two_grad * gain_two * scale_two
            - hidden * (scale_two * scale_two * inner_two / model_width)
        )
        acc_gain_two = acc_gain_two + jnp.sum(normed_two_grad * hidden * scale_two, axis=0)

    rows_in = after(kept[0], state[-1]["total"])
    rows_u = after(kept[2], state[-1]["total"])
    own_grads = lax.optimization_barrier(
        (
            lax.dot_general(rows_in, kept[3], TN, preferred_element_type=F32).astype(BF16),
            lax.dot_general(rows_in, kept[4], TN, preferred_element_type=F32).astype(BF16),
            lax.dot_general(rows_u, kept[1], TN, preferred_element_type=F32).astype(BF16),
        )
    )
    pair = PairLink()
    halves = [
        pair.swapped(own[half * own.shape[0] // 2 : (half + 1) * own.shape[0] // 2])
        for own in own_grads
        for half in range(2)
    ]
    for n in range(chunks):
        state[n]["mixed_total"] = chips_total(state[n]["y"], link)

    acc_out = acc_query = acc_key = None
    acc_gain_one = jnp.zeros((model_width,), F32)
    acc_query_gain = jnp.zeros((head_size,), F32)
    acc_key_gain = jnp.zeros((head_size,), F32)
    input_blocks = []
    for n in range(chunks):
        s = state[n]
        branch_full = row_gather(s["hidden_total"].astype(BF16))
        if n == chunks - 1:
            branch_full = after(branch_full, halves[0], state[0]["mixed_total"])
        mixed_grad = lax.dot_general(
            branch_full, out_full, NT, preferred_element_type=F32
        ).astype(BF16)
        out_here = lax.dot_general(s["mixed"], branch_full, TN, preferred_element_type=F32)
        acc_out = out_here if n == 0 else acc_out + out_here
        if n == chunks - 1:
            out_share = col_share(acc_out.astype(BF16), 1, link)
        projected_grad, key_grad, value_grad, inner_one, head_terms = attention_backward(
            members == 1, s["projected"], mixed_grad, heads_here, *segs[n], *tables[n], *head_gains
        )
        acc_query_gain = acc_query_gain + head_terms[0]
        if members == 1:
            acc_key_gain = acc_key_gain + head_terms[1]
        else:
            for bit in range(members.bit_length() - 1):
                key_grad = key_grad + swapped(key_grad, "row", bit)
                value_grad = value_grad + swapped(value_grad, "row", bit)
            key_pre = s["projected"][:, query_width : query_width + head_size]
            value_pre = s["projected"][:, query_width + head_size :]
            key_grad, key_terms = norm_back(
                key_pre, head_gains[1], turn_plain(key_grad, tables[n][0], -tables[n][1])
            )
            acc_key_gain = acc_key_gain + column_mask * jnp.sum(key_terms, axis=0)
            key_low = (column_mask * key_grad).astype(BF16)
            value_low = (column_mask * value_grad).astype(BF16)
            projected_grad = jnp.concatenate(
                [projected_grad[:, :query_width], key_low, value_low], axis=1
            )
            inner_one = inner_one + jnp.sum(
                key_low.astype(F32) * key_pre + value_low.astype(F32) * value_pre,
                axis=1,
                keepdims=True,
            )
        key_here = lax.dot_general(
            s["normed_full"], projected_grad[:, query_width:], TN, preferred_element_type=F32
        )
        acc_key = key_here if n == 0 else acc_key + key_here
        partial = lax.dot_general(
            projected_grad, projection, NT, preferred_element_type=F32
        ).astype(BF16)
        s["partial"] = partial
        normed_one_grad = row_scatter(partial)
        inner_one = butterfly(inner_one[:, 0], "row")[:, None]
        acc_gain_one = acc_gain_one + jnp.sum(
            partial.astype(F32) * s["normed_full"].astype(F32), axis=0
        )
        query_here = lax.dot_general(
            s["normed_full"], projected_grad[:, :query_width], TN, preferred_element_type=F32
        )
        acc_query = query_here if n == 0 else acc_query + query_here
        scale_one = s["scale_one"]
        if n == 0:
            normed_one_grad = after(normed_one_grad, halves[1], state[-1]["mixed_total"])
        if n == chunks - 1:
            normed_one_grad = after(normed_one_grad, halves[3])
        input_blocks.append(
            s["hidden_total"]
            + normed_one_grad * gain_one * scale_one
            - chunk(residual, n).astype(F32)
            * (scale_one * scale_one * inner_one / model_width)
        )

    for n in range(chunks):
        s = state[n]
        s["mixture"] = row_scatter(after(s["mixed_total"], state[-1]["partial"]))
    state[0]["mixture"] = after(state[0]["mixture"], halves[4])

    out_other = pair.swapped(out_share)
    key_share = col_share(acc_key.astype(BF16), 0, link)
    key_share = added(key_share, pair.swapped(key_share))
    shares = [jnp.concatenate(piece, axis=0) for piece in ring_pieces(key_share)]
    shares = jnp.concatenate(shares + shares, axis=1)
    shares = lax.dynamic_slice_in_dim(
        shares, (row_count - row_place) * 2 * head_size, row_count * 2 * head_size, 1
    )
    shares = shares.astype(F32).reshape(-1, kv_heads, members, 2, head_size).sum(axis=2)
    grad_key = shares[:, :, 0].reshape(-1, kv_heads * head_size)
    grad_value = shares[:, :, 1].reshape(-1, kv_heads * head_size)
    gain_two_full = lax.dynamic_update_slice_in_dim(
        jnp.zeros((model_width,), F32), acc_gain_two, row_start, 0
    )
    router_full = lax.dynamic_update_slice_in_dim(
        jnp.zeros((model_width, experts), F32), acc_router, row_start, 0
    )
    sizes = (model_width, model_width, head_size, head_size, model_width * experts)
    flat = jnp.concatenate(
        [
            acc_gain_one / norm_attention,
            gain_two_full,
            acc_query_gain,
            acc_key_gain,
            router_full.reshape(-1),
        ]
    )
    for axis in ("col", "row"):
        flat = butterfly(flat, axis)
    flat = flat + pair.swapped(flat)
    totals, start = [], 0
    for size in sizes:
        totals.append(flat[start : start + size])
        start += size
    query_share = col_share(acc_query.astype(BF16), 0, link)
    grad_query = query_share.astype(F32) + pair.swapped(query_share).astype(F32)
    grad_out_weight = out_share.astype(F32) + out_other.astype(F32)
    grad_gate, grad_up, grad_down = (
        halves_sum(own, halves[2 * i], halves[2 * i + 1])[None] for i, own in enumerate(own_grads)
    )
    output_blocks = [(s["hidden"] + s["mixture"]).astype(BF16) for s in state]
    return (
        jnp.concatenate(output_blocks, axis=0),
        jnp.concatenate(input_blocks, axis=0),
        totals[0],
        grad_query,
        grad_key,
        grad_value,
        totals[2],
        totals[3],
        grad_out_weight,
        totals[1],
        totals[4].reshape(model_width, experts),
        grad_gate,
        grad_up,
        grad_down,
    )


def solution(mesh):
    in_specs = (
        P(("dp", "col"), "row"),
        P(("dp", "col")),
        P(("dp", "col"), None),
        P(),
        P("col", "row"),
        P("col", None),
        P("col", None),
        P(),
        P(),
        P("row", "col"),
        P(),
        P(),
        P(("row", "col"), None, None),
        P(("row", "col"), None, None),
        P(("row", "col"), None, None),
        P(("dp", "col"), "row"),
    )
    out_specs = (
        P(("dp", "col"), "row"),
        P(("dp", "col"), "row"),
        P(),
        P("col", "row"),
        P("col", None),
        P("col", None),
        P(),
        P(),
        P("row", "col"),
        P(),
        P(),
        P(("row", "col"), None, None),
        P(("row", "col"), None, None),
        P(("row", "col"), None, None),
    )
    return jax.shard_map(
        per_device, mesh=mesh, in_specs=in_specs, out_specs=out_specs, check_vma=False
    )
```

```python
import functools
import math

import jax
import jax.numpy as jnp
from jax import lax
from jax.experimental import pallas as pl
from jax.experimental.pallas import tpu as pltpu
from jax.sharding import PartitionSpec as P

SEQUENCE_TOKENS = 512
EPSILON = 1e-06
ROPE_BASE = 1000000.0
MASKED = -1e30
LANES = 128
BF16 = jnp.bfloat16
F32 = jnp.float32
NT = (((1,), (1,)), ((), ()))
TN = (((0,), (0,)), ((), ()))

def mm(left, right):
    return jnp.dot(left, right, preferred_element_type=F32)

def mm_nt(left, right):
    return lax.dot_general(left, right, NT, preferred_element_type=F32)

def mm_tn(left, right):
    return lax.dot_general(left, right, (((0,), (0,)), ((), ())), preferred_element_type=F32)

def turn(values, cos_wide, sin_wide):
    return values * cos_wide + pltpu.roll(values, values.shape[1] // 2, 1) * sin_wide

def unit(values):
    return lax.rsqrt(jnp.mean(values * values, axis=1, keepdims=True) + EPSILON)

def sequence_bias(segs_ref, segs_t_ref):
    rows = segs_ref.shape[1]
    before = lax.broadcasted_iota(jnp.int32, (rows, rows), 1) <= lax.broadcasted_iota(jnp.int32, (rows, rows), 0)
    same = segs_t_ref[...] == segs_ref[...]
    return jnp.where(jnp.logical_and(same, before), 0.0, MASKED)

def block_probs(query, key, bias, scale):
    scores = mm_nt(query, key) * scale + bias
    weights = jnp.exp(scores - jnp.max(scores, axis=1, keepdims=True))
    return weights * (1.0 / jnp.sum(weights, axis=1, keepdims=True))

def attention_forward_kernel(scale, q_ref, k_ref, v_ref, segs_ref, segs_t_ref, cos_ref, sin_ref, q_gain_ref, k_gain_ref, out_ref, bias, key, value):
    head = k_ref.shape[1]
    rows = q_ref.shape[0]
    half = rows // 2
    cos_wide, sin_wide = cos_ref[...], sin_ref[...]

    @pl.when(pl.program_id(0) == 0)
    def _():
        bias[...] = sequence_bias(segs_ref, segs_t_ref)
        k_pre = k_ref[...]
        key[...] = turn(k_pre * unit(k_pre) * k_gain_ref[...], cos_wide, sin_wide).astype(BF16)
        value[...] = v_ref[...].astype(BF16)

    for h in range(q_ref.shape[1] // head):
        lanes = slice(h * head, (h + 1) * head)
        q_pre = q_ref[:, lanes]
        query = turn(q_pre * unit(q_pre) * q_gain_ref[...], cos_wide, sin_wide).astype(BF16)
        for part in range(2):
            at, keys = slice(part * half, (part + 1) * half), slice(0, (part + 1) * half)
            probs = block_probs(query[at], key[keys, :], bias[at, keys], scale)
            out_ref[at, lanes] = mm(probs.astype(BF16), value[keys, :]).astype(BF16)

def attention_forward(projected, heads, segs, segs_t, cos_wide, sin_wide, q_gain, k_gain):
    rows = projected.shape[0]
    head = q_gain.shape[1]
    pair = 2 if heads % 2 == 0 else 1
    fixed = lambda *shape: pl.BlockSpec(shape, lambda i: (0,) * len(shape))
    return pl.pallas_call(
        functools.partial(attention_forward_kernel, head ** -0.5),
        grid=(heads // pair,),
        out_shape=jax.ShapeDtypeStruct((rows, heads * head), BF16),
        in_specs=[
            pl.BlockSpec((rows, pair * head), lambda i: (0, i)),
            pl.BlockSpec((rows, head), lambda i: (0, heads)),
            pl.BlockSpec((rows, head), lambda i: (0, heads + 1)),
            fixed(1, rows), fixed(rows, 1), fixed(rows, head), fixed(rows, head), fixed(1, head), fixed(1, head),
        ],
        out_specs=pl.BlockSpec((rows, pair * head), lambda i: (0, i)),
        scratch_shapes=[pltpu.VMEM((rows, rows), F32), pltpu.VMEM((rows, head), BF16), pltpu.VMEM((rows, head), BF16)],
        compiler_params=pltpu.CompilerParams(vmem_limit_bytes=48 << 20),
        cost_estimate=pl.CostEstimate(flops=10000000000, bytes_accessed=10000000, transcendentals=0),
        name="attention_forward",
    )(projected, projected, projected, segs, segs_t, cos_wide, sin_wide, q_gain, k_gain)

def norm_back(values, gain, upstream):
    factor = unit(values)
    weighted = upstream * gain
    inner = jnp.mean(weighted * values, axis=1, keepdims=True)
    return weighted * factor - values * (factor * factor * factor * inner), upstream * values * factor

def attention_backward_kernel(scale, finish, q_ref, k_ref, v_ref, g_ref, segs_ref, segs_t_ref, cos_ref, sin_ref, q_gain_ref, k_gain_ref,
                              out_ref, key_ref, value_ref, inner_ref, gains_ref, bias, key, value, inner):
    head = k_ref.shape[1]
    rows = q_ref.shape[0]
    half = rows // 2
    cos_wide, sin_wide = cos_ref[...], sin_ref[...]
    step, steps = pl.program_id(0), pl.num_programs(0)
    pair = q_ref.shape[1] // head

    @pl.when(step == 0)
    def _():
        bias[...] = sequence_bias(segs_ref, segs_t_ref)
        k_pre = k_ref[...]
        key[...] = turn(k_pre * unit(k_pre) * k_gain_ref[...], cos_wide, sin_wide).astype(BF16)
        value[...] = v_ref[...].astype(BF16)
        key_ref[...] = jnp.zeros_like(key_ref)
        value_ref[...] = jnp.zeros_like(value_ref)
        inner[...] = jnp.zeros_like(inner)
        gains_ref[...] = jnp.zeros_like(gains_ref)

    for h in range(pair):
        lanes = slice(h * head, (h + 1) * head)
        q_pre = q_ref[:, lanes]
        query = turn(q_pre * unit(q_pre) * q_gain_ref[...], cos_wide, sin_wide).astype(BF16)
        grads = []
        for part in range(2):
            at, keys = slice(part * half, (part + 1) * half), slice(0, (part + 1) * half)
            probs = block_probs(query[at], key[keys, :], bias[at, keys], scale)
            upstream = g_ref[at, lanes]
            prob_grad = mm_nt(upstream, value[keys, :])
            score_grad = (probs * (prob_grad - jnp.sum(probs * prob_grad, axis=1, keepdims=True))).astype(BF16)
            grads.append(mm(score_grad, key[keys, :]) * scale)
            key_ref[keys, :] += mm_tn(score_grad, query[at]) * scale
            value_ref[keys, :] += mm_tn(probs.astype(BF16), upstream)
        query_grad = turn(jnp.concatenate(grads, axis=0), cos_wide, -sin_wide)
        q_grad, terms = norm_back(q_pre, q_gain_ref[...], query_grad)
        low = q_grad.astype(BF16)
        out_ref[:, pl.ds(pl.multiple_of((step * pair + h) * head, head), head)] = low
        inner[...] += low.astype(F32) * q_pre
        gains_ref[0:1, :] += jnp.sum(terms, axis=0, keepdims=True)

    @pl.when(step == steps - 1)
    def _():
        total = jnp.sum(inner[...], axis=1, keepdims=True)
        if finish:
            k_pre, v_pre = k_ref[...], v_ref[...]
            k_grad, terms = norm_back(k_pre, k_gain_ref[...], turn(key_ref[...], cos_wide, -sin_wide))
            k_low, v_low = k_grad.astype(BF16), value_ref[...].astype(BF16)
            width = steps * pair * head
            out_ref[:, pl.ds(out_ref.shape[1] - 2 * head, head)] = k_low
            out_ref[:, pl.ds(out_ref.shape[1] - head, head)] = v_low
            gains_ref[1:2, :] = jnp.sum(terms, axis=0, keepdims=True)
            total = total + jnp.sum(k_low.astype(F32) * k_pre + v_low.astype(F32) * v_pre, axis=1, keepdims=True)
        inner_ref[...] = total

def attention_backward(finish, projected, upstream, heads, segs, segs_t, cos_wide, sin_wide, q_gain, k_gain):
    rows = projected.shape[0]
    head = q_gain.shape[1]
    pair = 2 if heads % 2 == 0 else 1
    fixed = lambda *shape: pl.BlockSpec(shape, lambda i: (0,) * len(shape))
    return pl.pallas_call(
        functools.partial(attention_backward_kernel, head ** -0.5, finish),
        grid=(heads // pair,),
        out_shape=[
            jax.ShapeDtypeStruct((rows, (heads + 2) * head), BF16),
            jax.ShapeDtypeStruct((rows, head), F32),
            jax.ShapeDtypeStruct((rows, head), F32),
            jax.ShapeDtypeStruct((rows, 1), F32),
            jax.ShapeDtypeStruct((2, head), F32),
        ],
        in_specs=[
            pl.BlockSpec((rows, pair * head), lambda i: (0, i)),
            pl.BlockSpec((rows, head), lambda i: (0, heads)),
            pl.BlockSpec((rows, head), lambda i: (0, heads + 1)),
            pl.BlockSpec((rows, pair * head), lambda i: (0, i)),
            fixed(1, rows), fixed(rows, 1), fixed(rows, head), fixed(rows, head), fixed(1, head), fixed(1, head),
        ],
        out_specs=[fixed(rows, (heads + 2) * head), fixed(rows, head), fixed(rows, head), fixed(rows, 1), fixed(2, head)],
        scratch_shapes=[pltpu.VMEM((rows, rows), F32), pltpu.VMEM((rows, head), BF16), pltpu.VMEM((rows, head), BF16), pltpu.VMEM((rows, head), F32)],
        compiler_params=pltpu.CompilerParams(vmem_limit_bytes=48 << 20),
        cost_estimate=pl.CostEstimate(flops=20000000000, bytes_accessed=10000000, transcendentals=0),
        name="attention_backward",
    )(projected, projected, projected, upstream, segs, segs_t, cos_wide, sin_wide, q_gain, k_gain)

def norm_kernel(in_ref, gain_ref, out_ref, scale_ref):
    wide = in_ref[...].astype(F32)
    scale = unit(wide)
    scale_ref[...] = scale
    out_ref[...] = (wide * scale * gain_ref[...]).astype(BF16)


def normalized(values, gain):
    rows, width = values.shape
    block = min(128, rows)
    return pl.pallas_call(
        norm_kernel,
        grid=(rows // block,),
        out_shape=[jax.ShapeDtypeStruct((rows, width), BF16), jax.ShapeDtypeStruct((rows, 1), F32)],
        in_specs=[
            pl.BlockSpec((block, width), lambda i: (i, 0)),
            pl.BlockSpec((1, width), lambda i: (0, 0)),
        ],
        out_specs=[
            pl.BlockSpec((block, width), lambda i: (i, 0)),
            pl.BlockSpec((block, 1), lambda i: (i, 0)),
        ],
        compiler_params=pltpu.CompilerParams(vmem_limit_bytes=32 << 20),
        cost_estimate=pl.CostEstimate(flops=2000000000, bytes_accessed=8000000, transcendentals=0),
        name="normalized",
    )(values, gain)


def norm_pieces_kernel(count, scalars_ref, *refs):
    pieces, gain_ref, out_ref, scale_ref = refs[:count], refs[count], refs[count + 1], refs[count + 2]
    width = pieces[0].shape[1]
    total = None
    for piece in pieces:
        wide = piece[...].astype(F32)
        part = jnp.sum(wide * wide, axis=1, keepdims=True)
        total = part if total is None else total + part
    scale = lax.rsqrt(total / (width * count) + EPSILON)
    scale_ref[...] = scale
    for i, piece in enumerate(pieces):
        at = pl.ds(pl.multiple_of((scalars_ref[1] + i) % count * width, width), width)
        out_ref[:, at] = (piece[...].astype(F32) * scale * gain_ref[:, at]).astype(BF16)


def normalized_pieces(pieces, offsets, rows, scalars, gain):
    count = len(pieces)
    width = pieces[0].shape[1]
    block = min(128, rows)
    return pl.pallas_call(
        functools.partial(norm_pieces_kernel, count),
        grid=(rows // block,),
        out_shape=[
            jax.ShapeDtypeStruct((rows, width * count), BF16),
            jax.ShapeDtypeStruct((rows, 1), F32),
        ],
        in_specs=[pl.BlockSpec(memory_space=pltpu.SMEM)]
        + [pl.BlockSpec((block, width), lambda i, o=o: (o // block + i, 0)) for o in offsets]
        + [pl.BlockSpec((1, width * count), lambda i: (0, 0))],
        out_specs=[
            pl.BlockSpec((block, width * count), lambda i: (i, 0)),
            pl.BlockSpec((block, 1), lambda i: (i, 0)),
        ],
        compiler_params=pltpu.CompilerParams(vmem_limit_bytes=32 << 20),
        cost_estimate=pl.CostEstimate(flops=2000000000, bytes_accessed=8000000, transcendentals=0),
        name="normalized_pieces",
    )(scalars, *pieces, gain)


def pair_kernel(first, place, experts, scalars_ref, slots_ref, slots_t_ref, mask_ref, router_ref, *refs):
    refs = list(refs)
    token_in, grad_in = refs[0:2], refs[2:4]
    weights_in = refs[4:7]
    del refs[:7]
    if not first:
        del refs[:5]
    y_out, x_out = refs[0:2], refs[2:4]
    small_out, logits_out, gates_out = refs[4:7]
    kept_out = refs[7:12]
    (token, grad, gate_w, up_w, down_w, y_buf, x_buf, rows_in, rows_grad, rows_u, rows_da, rows_db, in_sem, grad_sem, w_sem, out_sem, kept_sem) = refs[12:]
    capacity = rows_in.shape[0] // 2
    tokens, width = token.shape[1:]
    hidden = gate_w.shape[1]
    load_tok = [pltpu.make_async_copy(token_in[g], token.at[g], in_sem.at[g]) for g in range(2)]
    parts = grad_sem.shape[1]
    strip = width // parts
    load_grad = []
    for g in range(2):
        for d in range(parts):
            there = pl.multiple_of((scalars_ref[1] + d) % parts * strip, strip)
            load_grad.append(
                pltpu.make_async_copy(
                    grad_in[g].at[:, d * strip : (d + 1) * strip],
                    grad.at[g, :, pl.ds(there, strip)],
                    grad_sem.at[g, d],
                )
            )
    load_w = [
        pltpu.make_async_copy(src, dst, w_sem.at[i])
        for i, (src, dst) in enumerate(zip(weights_in, (gate_w, up_w, down_w)))
    ]
    load_tok[0].start()
    for load in load_grad[:parts]:
        load.start()
    for load in load_w:
        load.start()
    load_tok[1].start()
    for load in load_grad[parts:]:
        load.start()
    expert = scalars_ref[0]
    stores = []
    wide = min(512, width)
    step = 256 if hidden % 256 == 0 else hidden
    chosen_rows, spreads, gate_cols = [], [], []
    for g in range(2):
        load_tok[g].wait()
        logits = mm(token[g], router_ref[...])
        shifted = logits + mask_ref[g].astype(F32)
        weights = jnp.exp(shifted - jnp.max(shifted, axis=1, keepdims=True))
        gates = weights / jnp.sum(weights, axis=1, keepdims=True)
        if g == 0:
            logits_out[...] = logits
            gates_out[...] = gates
        gates_t = gates.T
        lane = lax.broadcasted_iota(jnp.int32, gates_t.shape, 0)
        gate_row = jnp.sum(jnp.where(lane == expert, gates_t, 0.0), axis=0, keepdims=True)
        chosen = lax.broadcasted_iota(jnp.int32, (capacity, tokens), 0) == slots_ref[g]
        slot_gates = jnp.sum(jnp.where(chosen, gate_row, 0.0), axis=1, keepdims=True)
        pick = jnp.where(chosen, 1.0, 0.0).astype(BF16)
        here = slice(g * capacity, (g + 1) * capacity)
        gate_cols.append(slot_gates)
        for load in load_grad[g * parts : (g + 1) * parts]:
            load.wait()

        def gather(j, _):
            at = pl.ds(pl.multiple_of(j * wide, wide), wide)
            rows_in[here, at] = mm(pick, token[g, :, at]).astype(BF16)
            rows_grad[here, at] = mm(pick, grad[g, :, at]).astype(BF16)
            return 0

        lax.fori_loop(0, width // wide, gather, 0)
    for load in load_w:
        load.wait()
    slot_gates = jnp.concatenate(gate_cols, axis=0)

    def middle(j, carry):
        dots, inner = carry
        at = pl.ds(pl.multiple_of(j * step, step), step)
        a = mm(rows_in[...], gate_w[:, at])
        b = mm(rows_in[...], up_w[:, at])
        raw = mm_nt(rows_grad[...], down_w[at, :])
        sig = 1.0 / (1.0 + jnp.exp(-a))
        silu = a * sig
        u = (silu * b).astype(BF16).astype(F32)
        dots = dots + jnp.sum(raw * u, axis=1, keepdims=True)
        du = (slot_gates * raw).astype(BF16).astype(F32)
        da = du * b * sig * (1.0 + a * (1.0 - sig))
        db = du * silu
        inner = inner + jnp.sum(da * a + db * b, axis=1, keepdims=True)
        rows_u[:, at] = (slot_gates * u).astype(BF16)
        rows_da[:, at] = da.astype(BF16)
        rows_db[:, at] = db.astype(BF16)
        return dots, inner

    nothing = jnp.zeros((2 * capacity, 1), F32)
    dots, inner = lax.fori_loop(0, hidden // step, middle, (nothing, nothing))
    kept_here = pl.ds(place * 2 * capacity, 2 * capacity)
    for i, kept_rows in enumerate((rows_in, rows_grad, rows_u, rows_da, rows_db)):
        store = pltpu.make_async_copy(kept_rows, kept_out[i].at[kept_here, :], kept_sem.at[i])
        store.start()
        stores.append(store)
    spreads = [
        jnp.where(
            lax.broadcasted_iota(jnp.int32, (tokens, capacity), 1) == slots_t_ref[g], 1.0, 0.0
        ).astype(BF16)
        for g in range(2)
    ]
    for j in range(width // wide):
        at = slice(j * wide, (j + 1) * wide)
        dx = mm_nt(rows_da[...], gate_w[at, :]) + mm_nt(rows_db[...], up_w[at, :])
        y = mm(rows_u[...], down_w[:, at])
        for i, (rows, buf, out) in enumerate(((dx, x_buf, x_out), (y, y_buf, y_out))):
            low = rows.astype(BF16)
            for g in range(2):
                here = slice(g * capacity, (g + 1) * capacity)
                buf[g, :, at] = mm(spreads[g], low[here]).astype(BF16)
                store = pltpu.make_async_copy(
                    buf.at[g, :, at], out[g].at[:, at], out_sem.at[i, g, j]
                )
                store.start()
                stores.append(store)
    small_row = lax.broadcasted_iota(jnp.int32, small_out.shape[1:], 0)
    for g in range(2):
        here = slice(g * capacity, (g + 1) * capacity)
        chosen = lax.broadcasted_iota(jnp.int32, (capacity, tokens), 0) == slots_ref[g]
        dots_row = jnp.sum(jnp.where(chosen, dots[here], 0.0), axis=0, keepdims=True)
        inner_row = jnp.sum(jnp.where(chosen, inner[here], 0.0), axis=0, keepdims=True)
        small_out[g] = jnp.where(small_row == expert, dots_row, 0.0) + jnp.where(
            small_row == experts, inner_row, 0.0
        )
    for store in stores:
        store.wait()


def expert_pair(
    place, places, capacity, experts, scalars, slots, slots_t, mask, router, tokens, grads, weights, kept
):
    rows, width = tokens[0].shape
    hidden = weights[0].shape[1]
    total = places * 2 * capacity
    anywhere = pl.BlockSpec(memory_space=pl.ANY)
    inside = pl.BlockSpec(memory_space=pltpu.VMEM)
    first = kept is None
    parts = lax.axis_size("row")
    small_rows = (experts + 8) // 8 * 8
    dense = jax.ShapeDtypeStruct((rows, width), BF16)
    kept_shapes = [jax.ShapeDtypeStruct((total, w), BF16) for w in (width, width, hidden, hidden, hidden)]
    flat = jax.ShapeDtypeStruct((rows, router.shape[1]), F32)
    out = pl.pallas_call(
        functools.partial(pair_kernel, first, place, experts),
        out_shape=[dense] * 4 + [jax.ShapeDtypeStruct((2, small_rows, rows), F32), flat, flat] + kept_shapes,
        in_specs=[pl.BlockSpec(memory_space=pltpu.SMEM)] + [inside] * 4 + [anywhere] * (7 if first else 12),
        out_specs=[anywhere] * 4 + [inside] * 3 + [anywhere] * 5,
        input_output_aliases={} if first else {12 + i: 7 + i for i in range(5)},
        scratch_shapes=[
            pltpu.VMEM((2, rows, width), BF16),
            pltpu.VMEM((2, rows, width), BF16),
            pltpu.VMEM((width, hidden), BF16),
            pltpu.VMEM((width, hidden), BF16),
            pltpu.VMEM((hidden, width), BF16),
            pltpu.VMEM((2, rows, width), BF16),
            pltpu.VMEM((2, rows, width), BF16),
            pltpu.VMEM((2 * capacity, width), BF16),
            pltpu.VMEM((2 * capacity, width), BF16),
            pltpu.VMEM((2 * capacity, hidden), BF16),
            pltpu.VMEM((2 * capacity, hidden), BF16),
            pltpu.VMEM((2 * capacity, hidden), BF16),
            pltpu.SemaphoreType.DMA((2,)),
            pltpu.SemaphoreType.DMA((2, parts)),
            pltpu.SemaphoreType.DMA((3,)),
            pltpu.SemaphoreType.DMA((2, 2, width // min(512, width))),
            pltpu.SemaphoreType.DMA((5,)),
        ],
        compiler_params=pltpu.CompilerParams(vmem_limit_bytes=56 << 20),
        cost_estimate=pl.CostEstimate(flops=36000000000, bytes_accessed=10000000, transcendentals=0),
        name="expert_pair",
    )(scalars, slots, slots_t, mask, router, *tokens, *grads, *weights, *([] if first else kept))
    return out


def route_kernel(expert_ref, routes_ref, mask_ref, slots_ref, slots_t_ref):
    rows, top_count = routes_ref.shape[1:]
    routes = routes_ref[0]
    lanes = lax.broadcasted_iota(jnp.int32, (rows, LANES), 1)
    chosen = routes[:, 0:1] == lanes
    for k in range(1, top_count):
        chosen = jnp.logical_or(chosen, routes[:, k : k + 1] == lanes)
    mask_ref[0] = jnp.where(chosen, 0.0, MASKED).astype(BF16)
    below = lax.broadcasted_iota(jnp.int32, (rows, rows), 1) <= lax.broadcasted_iota(
        jnp.int32, (rows, rows), 0
    )
    ones = jnp.where(chosen, 1.0, 0.0)
    ranks = mm(jnp.where(below, 1.0, 0.0).astype(BF16), ones.astype(BF16))
    slots = jnp.where(chosen, ranks - 1.0, -1.0)
    here = lanes == expert_ref[0]
    slots_t_ref[0] = jnp.max(jnp.where(here, slots, -1.0), axis=1, keepdims=True).astype(jnp.int32)
    lane_first = lax.broadcasted_iota(jnp.int32, (LANES, rows), 0)
    slots_ref[0] = jnp.max(
        jnp.where(lane_first == expert_ref[0], slots.T, -1.0), axis=0, keepdims=True
    ).astype(jnp.int32)


def route_tables(scalars, routes):
    blocks, rows, top_count = routes.shape
    return pl.pallas_call(
        route_kernel,
        grid=(blocks,),
        out_shape=[
            jax.ShapeDtypeStruct((blocks, rows, LANES), BF16),
            jax.ShapeDtypeStruct((blocks, 1, rows), jnp.int32),
            jax.ShapeDtypeStruct((blocks, rows, 1), jnp.int32),
        ],
        in_specs=[
            pl.BlockSpec(memory_space=pltpu.SMEM),
            pl.BlockSpec((1, rows, top_count), lambda i: (i, 0, 0)),
        ],
        out_specs=[
            pl.BlockSpec((1, rows, LANES), lambda i: (i, 0, 0)),
            pl.BlockSpec((1, 1, rows), lambda i: (i, 0, 0)),
            pl.BlockSpec((1, rows, 1), lambda i: (i, 0, 0)),
        ],
        compiler_params=pltpu.CompilerParams(vmem_limit_bytes=32 << 20),
        cost_estimate=pl.CostEstimate(flops=1000000000, bytes_accessed=1000000, transcendentals=0),
        name="route_tables",
    )(scalars, routes)


def place_kernel(axis, starts_ref, *refs):
    out = refs[-1]
    for i, piece in enumerate(refs[:-1]):
        width = piece.shape[axis]
        at = pl.ds(pl.multiple_of(starts_ref[i] * width, width), width)
        if axis == 0:
            out[at, :] = piece[...]
        else:
            out[:, at] = piece[...]


def placed(pieces, starts, axis):
    shape = list(pieces[0].shape)
    shape[axis] *= len(pieces)
    inside = pl.BlockSpec(memory_space=pltpu.VMEM)
    return pl.pallas_call(
        functools.partial(place_kernel, axis),
        out_shape=jax.ShapeDtypeStruct(tuple(shape), pieces[0].dtype),
        in_specs=[pl.BlockSpec(memory_space=pltpu.SMEM)] + [inside] * len(pieces),
        out_specs=inside,
        compiler_params=pltpu.CompilerParams(vmem_limit_bytes=32 << 20),
        cost_estimate=pl.CostEstimate(flops=1000000, bytes_accessed=10000000, transcendentals=0),
        name="placed",
    )(starts, *pieces)


def pieces_kernel(counts, own_ref, *refs):
    out_ref = refs[-1]
    step, start = pl.program_id(0), 0
    for count, piece in zip(counts, refs[:-1]):

        @pl.when(jnp.logical_and(step >= start, step < start + count))
        def _():
            out_ref[...] = own_ref[...].astype(F32) + piece[...].astype(F32)

        start += count


def pieces_sum(own, pieces):
    rows, width = own.shape
    block = math.gcd(*[piece.shape[0] for piece in pieces])
    counts = [piece.shape[0] // block for piece in pieces]
    specs, start = [pl.BlockSpec((block, width), lambda i: (i, 0))], 0
    for count in counts:
        specs.append(
            pl.BlockSpec(
                (block, width), lambda i, s=start, c=count: (jnp.clip(i - s, 0, c - 1), 0)
            )
        )
        start += count
    return pl.pallas_call(
        functools.partial(pieces_kernel, counts),
        grid=(rows // block,),
        out_shape=jax.ShapeDtypeStruct((rows, width), F32),
        in_specs=specs,
        out_specs=pl.BlockSpec((block, width), lambda i: (i, 0)),
        compiler_params=pltpu.CompilerParams(vmem_limit_bytes=32 << 20),
        cost_estimate=pl.CostEstimate(flops=4000000000, bytes_accessed=12000000, transcendentals=0),
        name="pieces_sum",
    )(own, *pieces)


def grads_kernel(rows_ref, *refs):
    half = len(refs) // 2
    for grad_ref, out_ref in zip(refs[:half], refs[half:]):
        out_ref[...] = mm_tn(rows_ref[...], grad_ref[...]).astype(BF16)


def grads_of(rows_in, *grads):
    count, width = rows_in.shape
    hidden = grads[0].shape[1]
    block = min(512, width)
    return pl.pallas_call(
        grads_kernel,
        grid=(width // block,),
        out_shape=[jax.ShapeDtypeStruct((width, hidden), BF16)] * len(grads),
        in_specs=[pl.BlockSpec((count, block), lambda i: (0, i))]
        + [pl.BlockSpec((count, hidden), lambda i: (0, 0))] * len(grads),
        out_specs=[pl.BlockSpec((block, hidden), lambda i: (i, 0))] * len(grads),
        compiler_params=pltpu.CompilerParams(vmem_limit_bytes=56 << 20),
        cost_estimate=pl.CostEstimate(flops=1000000000, bytes_accessed=1000000, transcendentals=0),
        name="grads_of",
    )(rows_in, *grads)


def grad_of(rows_u, rows_grad):
    count, hidden = rows_u.shape
    width = rows_grad.shape[1]
    block = min(512, width)
    return pl.pallas_call(
        grads_kernel,
        grid=(width // block,),
        out_shape=[jax.ShapeDtypeStruct((hidden, width), BF16)],
        in_specs=[
            pl.BlockSpec((count, hidden), lambda i: (0, 0)),
            pl.BlockSpec((count, block), lambda i: (0, i)),
        ],
        out_specs=[pl.BlockSpec((hidden, block), lambda i: (0, i))],
        compiler_params=pltpu.CompilerParams(vmem_limit_bytes=56 << 20),
        cost_estimate=pl.CostEstimate(flops=1000000000, bytes_accessed=1000000, transcendentals=0),
        name="grad_of",
    )(rows_u, rows_grad)[0]


def moved(block, axis, by):
    count = lax.axis_size(axis)
    return lax.ppermute(block, axis, [(i, (i + by) % count) for i in range(count)])


def swapped(block, axis, bit):
    count = lax.axis_size(axis)
    return lax.ppermute(block, axis, [(i, i ^ (1 << bit)) for i in range(count)])


def butterfly(values, axis):
    for bit in range(lax.axis_size(axis).bit_length() - 1):
        values = values + swapped(values, axis, bit)
    return values


def ring_pieces(block):
    count = lax.axis_size("row")
    pieces = [[block]] + [None] * (count - 1)
    from_left = from_right = block
    half = block.shape[0] // 2
    for step in range(1, count // 2):
        from_left = moved(from_left, "row", 1)
        from_right = moved(from_right, "row", -1)
        pieces[count - step] = [from_left]
        pieces[step] = [from_right]
    if count > 1:
        pieces[count // 2] = [
            moved(from_left[:half], "row", 1),
            moved(from_right[half:], "row", -1),
        ]
    return pieces


def joined(pieces, number, rows):
    blocks = []
    for piece in pieces:
        tall = piece[0].shape[0]
        if len(piece) == 1:
            blocks.append(piece[0][number * rows : (number + 1) * rows])
        elif tall >= rows:
            start = number * rows % tall
            blocks.append(piece[number * rows // tall][start : start + rows])
        else:
            whole = jnp.concatenate(piece, axis=0)
            blocks.append(whole[number * rows : (number + 1) * rows])
    return jnp.concatenate(blocks, axis=1)


def row_gather(block):
    return lax.all_gather(block, "row", axis=block.ndim - 1, tiled=True)


def row_scatter(partial):
    return lax.psum_scatter(partial, "row", scatter_dimension=1, tiled=True).astype(F32)


def after(value, *others):
    return lax.optimization_barrier((value,) + others)[0]


class Link:
    def __init__(self):
        self.last = ()

    def moved(self, block, by):
        block = moved(after(block, *self.last), "col", by)
        self.last = (block,)
        return block


class PairLink:
    def __init__(self):
        self.last = ()

    def swapped(self, block):
        block = swapped(after(block, *self.last), "dp", 0)
        self.last = (block,)
        return block


def col_gather(block, link):
    count = lax.axis_size("col")
    pieces = []
    for step in range(count // 2):
        same = block if step == 0 else link.moved(block, 2 * step)
        pieces += [same, swapped(same, "col", 0)]
    return pieces


def added(*parts):
    total = parts[0].astype(F32)
    for part in parts[1:]:
        total = total + part.astype(F32)
    return total.astype(parts[0].dtype)


def chips_total(totals, link, *others):
    parts = list(totals[0])
    for step in range(1, len(totals)):
        parts.append(after(link.moved(added(*totals[step]), -2 * step), *others))
    return added(*parts)


def col_order():
    count = lax.axis_size("col")
    place = lax.axis_index("col")
    chip, core = place // 2, place % 2
    order = []
    for step in range(count // 2):
        back = (chip - step) % (count // 2) * 2
        order += [back + core, back + 1 - core]
    return order


def col_assemble(block, axis, link):
    return placed(col_gather(block, link), jnp.stack(col_order()).astype(jnp.int32), axis)


def col_share(partial, axis, link):
    count = lax.axis_size("col")
    width = partial.shape[axis] // count
    pieces = [
        lax.dynamic_slice_in_dim(partial, place * width, width, axis)
        for place in col_order()
    ]
    return chips_total(
        [
            (pieces[2 * step], swapped(pieces[2 * step + 1], "col", 0))
            for step in range(count // 2)
        ],
        link,
    )


def positions(segment_ids):
    places = jnp.arange(segment_ids.shape[0], dtype=jnp.int32)
    earlier = jnp.concatenate([segment_ids[:1] - 1, segment_ids[:-1]])
    starts = jnp.logical_or(segment_ids != earlier, places % SEQUENCE_TOKENS == 0)
    opening = lax.cummax(jnp.where(starts, places, 0), axis=0)
    return places - opening


def rotary(places, head_size):
    halfway = head_size // 2
    frequency = ROPE_BASE ** (-2.0 * jnp.arange(halfway, dtype=F32) / head_size)
    angles = places.astype(F32)[:, None] * frequency[None, :]
    cos_part, sin_part = jnp.cos(angles), jnp.sin(angles)
    return (
        jnp.concatenate([cos_part, cos_part], axis=1),
        jnp.concatenate([-sin_part, sin_part], axis=1),
    )


def turn_plain(values, cos_wide, sin_wide):
    return values * cos_wide + jnp.roll(values, values.shape[1] // 2, 1) * sin_wide


def per_device(
    residual,
    segments,
    routes,
    norm_attention,
    query_weight,
    key_projection_matrix,
    value_projection_matrix,
    query_gain,
    key_gain,
    out_weight,
    norm_experts,
    router_weight,
    gate_weight,
    up_weight,
    down_weight,
    grad_output,
):
    row_count = lax.axis_size("row")
    col_count = lax.axis_size("col")
    row_place = lax.axis_index("row")
    col_place = lax.axis_index("col")
    model_width = norm_attention.shape[0]
    feature_width = model_width // row_count
    head_size = query_gain.shape[0]
    heads_here = query_weight.shape[1] // head_size
    query_width = heads_here * head_size
    kv_heads = key_projection_matrix.shape[1] // head_size
    query_group_width = heads_here * row_count // kv_heads
    members = query_group_width // heads_here
    kv_index = row_place * heads_here // query_group_width
    member_place = row_place % members
    share_width = head_size // members
    column_mask = (jnp.arange(head_size, dtype=jnp.int32) // share_width == member_place).astype(
        F32
    )
    experts = gate_weight.shape[0] * row_count * col_count
    expert = row_place * col_count + col_place
    chips = col_count // 2
    token_rows = residual.shape[0]
    rows = SEQUENCE_TOKENS
    chunks = token_rows // rows
    top_count = routes.shape[1]
    capacity = max(2, 5 * rows * top_count // (4 * experts))
    row_start = row_place * feature_width
    labels = jnp.arange(experts, dtype=jnp.int32)
    scalars = jnp.stack([expert, row_place]).astype(jnp.int32)
    key_part = lax.dynamic_slice_in_dim(key_projection_matrix, kv_index * head_size, head_size, 1)
    value_part = lax.dynamic_slice_in_dim(
        value_projection_matrix, kv_index * head_size, head_size, 1
    )

    def chunk(array, number):
        return array[number * rows : (number + 1) * rows]

    link = Link()
    inputs_full = [row_gather(chunk(residual, n)) for n in range(chunks)]
    projection = col_assemble(
        jnp.concatenate([query_weight, key_part, value_part], axis=1), 0, link
    )
    routes_all = jnp.stack(col_gather(routes, link)).reshape(col_count * chunks, rows, top_count)
    out_full = col_assemble(out_weight, 1, link)
    grads_cols = [None] * chunks
    grad_pieces = ring_pieces(grad_output)
    grads_near = [piece[0] for piece in grad_pieces[1:] if len(piece) == 1]
    grads_middle = [block for piece in grad_pieces if len(piece) > 1 for block in piece]
    for n in range(chunks):
        grads_cols[n] = col_gather(joined(grad_pieces, n, rows), link)
    grads_far = [[g for g in grads_cols[n][2::2]] for n in range(chunks)]

    gain_one = lax.dynamic_slice_in_dim(norm_attention, row_start, feature_width)
    gain_two = lax.dynamic_slice_in_dim(norm_experts, row_start, feature_width)
    router_rows = lax.dynamic_slice_in_dim(router_weight, row_start, feature_width, 0)
    router = jnp.pad(router_weight, ((0, 0), (0, LANES - experts)))
    cos_all, sin_all = rotary(positions(segments), head_size)
    tables = [(chunk(cos_all, n), chunk(sin_all, n)) for n in range(chunks)]
    segs = [(chunk(segments, n)[None, :], chunk(segments, n)[:, None]) for n in range(chunks)]
    head_gains = (query_gain[None, :], key_gain[None, :])
    state = [{} for _ in range(chunks)]

    for n in range(chunks):
        s = state[n]
        s["normed_full"], s["scale_one"] = normalized(inputs_full[n], norm_attention[None, :])
        normed = s["normed_full"] if n == 0 else after(s["normed_full"], *grads_near)
        s["projected"] = mm(normed, projection)
        s["mixed"] = attention_forward(
            s["projected"], heads_here, *segs[n], *tables[n], *head_gains
        )
        partial = mm(s["mixed"], out_full).astype(BF16)
        s["mixed_out"] = partial
    masks, slots, slots_t = (
        table.reshape(col_count, chunks, *table.shape[1:])
        for table in route_tables(scalars, after(routes_all, partial))
    )

    kept = None

    def run_pair(n, place, *others):
        nonlocal kept
        s = state[n]
        two = slice(2 * place, 2 * place + 2)
        found = expert_pair(
            n * chips + place,
            chunks * chips,
            capacity,
            experts,
            scalars,
            slots[two, n],
            slots_t[two, n],
            masks[two, n],
            after(router, *others),
            s["tokens"][two],
            grads_cols[n][two],
            (gate_weight[0], up_weight[0], down_weight[0]),
            kept,
        )
        kept = found[7:]
        for name, same, other in (
            ("y", found[0], found[1]),
            ("x", found[2], found[3]),
            ("small", found[4][0], found[4][1]),
        ):
            other = swapped(other, "col", 0)
            s.setdefault(name, []).append(
                (same, other) if place == 0 else (added(same, other),)
            )
        if place == 0:
            s["logits"], s["gates"] = found[5][:, :experts], found[6][:, :experts]

    def hidden_of(n, ready, *others):
        s = state[n]
        summed = row_scatter(after(s["mixed_out"], *ready))
        s["hidden"] = chunk(residual, n).astype(F32) + after(summed, *others)
        s["wide"] = row_gather(after(s["hidden"].astype(BF16), masks))

    def second_norm(n, *others):
        s = state[n]
        s["normed_two"], s["scale_two"] = normalized(
            after(s["wide"], *others), norm_experts[None, :]
        )
        own = s["normed_two"]
        s["tokens"] = [own, swapped(own, "col", 0)]
        s["far"] = [link.moved(own, 2 * step) for step in range(1, chips)]

    def far_tokens(n, *others):
        for block in state[n]["far"]:
            same = after(block, *others)
            state[n]["tokens"] += [same, swapped(same, "col", 0)]

    def to_row(n, *others):
        s = state[n]
        s["small"] = butterfly(chips_total(s["small"], link), "row")
        s["total"] = chips_total(s["x"], link, *others)

    hidden_of(0, (), *grads_middle)
    second_norm(0, *grads_far[0], *grads_far[-1])
    for n in range(chunks):
        s = state[n]
        run_pair(n, 0, *([x[0] for x in state[n - 1]["x"][1:]] if n > 0 else []))
        spacer = s["small"][0][1]
        far_tokens(n, spacer)
        if n + 1 < chunks:
            hidden_of(n + 1, (s["wide"],), spacer)
        for place in range(1, chips):
            run_pair(n, place, spacer)
        if n > 0:
            to_row(n - 1, s["small"][-1][0])
        if n + 1 < chunks:
            second_norm(n + 1, s["small"][-1][0])
    pair = PairLink()
    own_grads, other_grads = [], []

    def expert_grads():
        grad_down = grad_of(kept[2], kept[1])
        grad_gate, grad_up = grads_of(after(kept[0], grad_down), kept[3], kept[4])
        own_grads.extend((grad_gate, grad_up, grad_down))
        wide, deep = grad_gate.shape[0], grad_down.shape[0]
        first, middle = wide // 8, wide // 2
        cuts = [(0, 0, first), (2, 0, deep // 2), (2, deep // 2, deep), (0, first, middle)]
        cuts += [(0, middle, wide), (1, 0, wide // 2), (1, wide // 2, wide)]
        for i, low, high in cuts:
            other_grads.append(pair.swapped(own_grads[i][low:high]))
        return other_grads[:1]

    acc_router = jnp.zeros((feature_width, experts), F32)
    acc_gain_two = jnp.zeros((feature_width,), F32)
    for n in range(chunks):
        s = state[n]
        if n == chunks - 1:
            to_row(n, *expert_grads())
        normed_two_grad = row_scatter(s["total"])
        hidden = s["hidden"]
        gate_dots = s["small"][:experts].T
        slot_inner = s["small"][experts]
        pick_grad = s["gates"] * (
            gate_dots - jnp.sum(s["gates"] * gate_dots, axis=1, keepdims=True)
        )
        logit_grad = pick_grad.astype(BF16)
        shard = lax.dynamic_slice_in_dim(s["normed_two"], row_start, feature_width, 1)
        acc_router = acc_router + lax.dot_general(
            shard, logit_grad, TN, preferred_element_type=F32
        )
        normed_two_grad = normed_two_grad + lax.dot_general(
            logit_grad, router_rows, NT, preferred_element_type=F32
        )
        inner_two = slot_inner[:, None] + jnp.sum(
            logit_grad.astype(F32) * s["logits"], axis=1, keepdims=True
        )
        scale_two = s["scale_two"]
        s["hidden_total"] = (
            chunk(grad_output, n).astype(F32)
            + normed_two_grad * gain_two * scale_two
            - hidden * (scale_two * scale_two * inner_two / model_width)
        )
        s["branch_full"] = row_gather(s["hidden_total"].astype(BF16))
        acc_gain_two = acc_gain_two + jnp.sum(normed_two_grad * hidden * scale_two, axis=0)

    for n in range(chunks):
        state[n]["mixed_total"] = chips_total(state[n]["y"], link)

    acc_out = acc_query = acc_key = None
    acc_gain_one = jnp.zeros((model_width,), F32)
    acc_query_gain = jnp.zeros((head_size,), F32)
    acc_key_gain = jnp.zeros((head_size,), F32)
    input_blocks = []
    for n in range(chunks):
        s = state[n]
        branch_full = s["branch_full"]
        if n == chunks - 1:
            branch_full = after(branch_full, other_grads[1], state[0]["mixed_total"])
        mixed_grad = lax.dot_general(
            branch_full, out_full, NT, preferred_element_type=F32
        ).astype(BF16)
        out_here = lax.dot_general(s["mixed"], branch_full, TN, preferred_element_type=F32)
        acc_out = out_here if n == 0 else acc_out + out_here
        if n == chunks - 1:
            out_share = col_share(acc_out.astype(BF16), 1, link)
        projected_grad, key_grad, value_grad, inner_one, head_terms = attention_backward(
            members == 1, s["projected"], mixed_grad, heads_here, *segs[n], *tables[n], *head_gains
        )
        acc_query_gain = acc_query_gain + head_terms[0]
        if members == 1:
            acc_key_gain = acc_key_gain + head_terms[1]
        else:
            for bit in range(members.bit_length() - 1):
                key_grad = key_grad + swapped(key_grad, "row", bit)
                value_grad = value_grad + swapped(value_grad, "row", bit)
            key_pre = s["projected"][:, query_width : query_width + head_size]
            value_pre = s["projected"][:, query_width + head_size :]
            key_grad, key_terms = norm_back(
                key_pre, head_gains[1], turn_plain(key_grad, tables[n][0], -tables[n][1])
            )
            acc_key_gain = acc_key_gain + column_mask * jnp.sum(key_terms, axis=0)
            key_low = (column_mask * key_grad).astype(BF16)
            value_low = (column_mask * value_grad).astype(BF16)
            projected_grad = jnp.concatenate(
                [projected_grad[:, :query_width], key_low, value_low], axis=1
            )
            inner_one = inner_one + jnp.sum(
                key_low.astype(F32) * key_pre + value_low.astype(F32) * value_pre,
                axis=1,
                keepdims=True,
            )
        key_here = lax.dot_general(
            s["normed_full"], projected_grad[:, query_width:], TN, preferred_element_type=F32
        )
        acc_key = key_here if n == 0 else acc_key + key_here
        partial = lax.dot_general(
            projected_grad, projection, NT, preferred_element_type=F32
        ).astype(BF16)
        s["partial"] = partial
        normed_one_grad = row_scatter(partial)
        inner_one = butterfly(inner_one[:, 0], "row")[:, None]
        acc_gain_one = acc_gain_one + jnp.sum(
            partial.astype(F32) * s["normed_full"].astype(F32), axis=0
        )
        query_here = lax.dot_general(
            s["normed_full"], projected_grad[:, :query_width], TN, preferred_element_type=F32
        )
        acc_query = query_here if n == 0 else acc_query + query_here
        scale_one = s["scale_one"]
        if n == 0:
            normed_one_grad = after(normed_one_grad, other_grads[2], other_grads[3], state[-1]["mixed_total"])
        if n == chunks - 1:
            normed_one_grad = after(normed_one_grad, other_grads[4])
        input_blocks.append(
            s["hidden_total"]
            + normed_one_grad * gain_one * scale_one
            - chunk(residual, n).astype(F32)
            * (scale_one * scale_one * inner_one / model_width)
        )

    key_share = col_share(acc_key.astype(BF16), 0, link)
    query_share = col_share(acc_query.astype(BF16), 0, link)
    for n in range(chunks):
        s = state[n]
        s["mixture"] = row_scatter(after(s["mixed_total"], state[-1]["partial"]))
    state[0]["mixture"] = after(state[0]["mixture"], *other_grads, out_share, key_share)
    out_other = pair.swapped(out_share)
    key_share = added(key_share, pair.swapped(key_share))
    shares = [jnp.concatenate(piece, axis=0) for piece in ring_pieces(key_share)]
    query_other = pair.swapped(query_share)
    state[-1]["mixture"] = after(
        state[-1]["mixture"], out_other, query_share, shares[1], shares[-1]
    )
    shares = jnp.concatenate(shares + shares, axis=1)
    shares = lax.dynamic_slice_in_dim(
        shares, (row_count - row_place) * 2 * head_size, row_count * 2 * head_size, 1
    )
    shares = shares.astype(F32).reshape(-1, kv_heads, members, 2, head_size).sum(axis=2)
    grad_key = shares[:, :, 0].reshape(-1, kv_heads * head_size)
    grad_value = shares[:, :, 1].reshape(-1, kv_heads * head_size)
    gain_two_full = lax.dynamic_update_slice_in_dim(
        jnp.zeros((model_width,), F32), acc_gain_two, row_start, 0
    )
    router_full = lax.dynamic_update_slice_in_dim(
        jnp.zeros((model_width, experts), F32), acc_router, row_start, 0
    )
    sizes = (model_width, model_width, head_size, head_size, model_width * experts)
    flat = jnp.concatenate(
        [
            acc_gain_one / norm_attention,
            gain_two_full,
            acc_query_gain,
            acc_key_gain,
            router_full.reshape(-1),
        ]
    )
    for axis in ("col", "row"):
        flat = butterfly(flat, axis)
    flat = after(flat, *[s["mixture"] for s in state])
    flat = flat + pair.swapped(flat)
    totals, start = [], 0
    for size in sizes:
        totals.append(flat[start : start + size])
        start += size
    grad_query = query_share.astype(F32) + query_other.astype(F32)
    grad_out_weight = out_share.astype(F32) + out_other.astype(F32)
    grad_gate, grad_up, grad_down = (
        pieces_sum(own, [other_grads[j] for j in parts])[None]
        for own, parts in zip(own_grads, ((0, 3, 4), (5, 6), (1, 2)))
    )
    output_blocks = [(s["hidden"] + s["mixture"]).astype(BF16) for s in state]
    return (
        jnp.concatenate(output_blocks, axis=0),
        jnp.concatenate(input_blocks, axis=0),
        totals[0],
        grad_query,
        grad_key,
        grad_value,
        totals[2],
        totals[3],
        grad_out_weight,
        totals[1],
        totals[4].reshape(model_width, experts),
        grad_gate,
        grad_up,
        grad_down,
    )


def solution(mesh):
    in_specs = (
        P(("dp", "col"), "row"),
        P(("dp", "col")),
        P(("dp", "col"), None),
        P(),
        P("col", "row"),
        P("col", None),
        P("col", None),
        P(),
        P(),
        P("row", "col"),
        P(),
        P(),
        P(("row", "col"), None, None),
        P(("row", "col"), None, None),
        P(("row", "col"), None, None),
        P(("dp", "col"), "row"),
    )
    out_specs = (
        P(("dp", "col"), "row"),
        P(("dp", "col"), "row"),
        P(),
        P("col", "row"),
        P("col", None),
        P("col", None),
        P(),
        P(),
        P("row", "col"),
        P(),
        P(),
        P(("row", "col"), None, None),
        P(("row", "col"), None, None),
        P(("row", "col"), None, None),
    )
    return jax.shard_map(
        per_device, mesh=mesh, in_specs=in_specs, out_specs=out_specs, check_vma=False
    )
```

```python
import functools
import math

import jax
import jax.numpy as jnp
from jax import lax
from jax.experimental import pallas as pl
from jax.experimental.pallas import tpu as pltpu
from jax.sharding import PartitionSpec as P

SEQUENCE_TOKENS = 512
EPSILON = 1e-06
ROPE_BASE = 1000000.0
MASKED = -1e30
LANES = 128
BF16 = jnp.bfloat16
F32 = jnp.float32
NT = (((1,), (1,)), ((), ()))
TN = (((0,), (0,)), ((), ()))

def mm(left, right):
    return jnp.dot(left, right, preferred_element_type=F32)

def mm_nt(left, right):
    return lax.dot_general(left, right, NT, preferred_element_type=F32)

def mm_tn(left, right):
    return lax.dot_general(left, right, (((0,), (0,)), ((), ())), preferred_element_type=F32)

def turn(values, cos_wide, sin_wide):
    return values * cos_wide + pltpu.roll(values, values.shape[1] // 2, 1) * sin_wide

def unit(values):
    return lax.rsqrt(jnp.mean(values * values, axis=1, keepdims=True) + EPSILON)

def sequence_bias(segs_ref, segs_t_ref):
    rows = segs_ref.shape[1]
    before = lax.broadcasted_iota(jnp.int32, (rows, rows), 1) <= lax.broadcasted_iota(jnp.int32, (rows, rows), 0)
    same = segs_t_ref[...] == segs_ref[...]
    return jnp.where(jnp.logical_and(same, before), 0.0, MASKED)

def block_probs(query, key, bias, scale):
    scores = mm_nt(query, key) * scale + bias
    weights = jnp.exp(scores - jnp.max(scores, axis=1, keepdims=True))
    return weights * (1.0 / jnp.sum(weights, axis=1, keepdims=True))

def attention_forward_kernel(scale, q_ref, k_ref, v_ref, segs_ref, segs_t_ref, cos_ref, sin_ref, q_gain_ref, k_gain_ref, out_ref, bias, key, value):
    head = k_ref.shape[1]
    rows = q_ref.shape[0]
    half = rows // 2
    cos_wide, sin_wide = cos_ref[...], sin_ref[...]

    @pl.when(pl.program_id(0) == 0)
    def _():
        bias[...] = sequence_bias(segs_ref, segs_t_ref)
        k_pre = k_ref[...]
        key[...] = turn(k_pre * unit(k_pre) * k_gain_ref[...], cos_wide, sin_wide).astype(BF16)
        value[...] = v_ref[...].astype(BF16)

    for h in range(q_ref.shape[1] // head):
        lanes = slice(h * head, (h + 1) * head)
        q_pre = q_ref[:, lanes]
        query = turn(q_pre * unit(q_pre) * q_gain_ref[...], cos_wide, sin_wide).astype(BF16)
        for part in range(2):
            at, keys = slice(part * half, (part + 1) * half), slice(0, (part + 1) * half)
            probs = block_probs(query[at], key[keys, :], bias[at, keys], scale)
            out_ref[at, lanes] = mm(probs.astype(BF16), value[keys, :]).astype(BF16)

def attention_forward(projected, heads, segs, segs_t, cos_wide, sin_wide, q_gain, k_gain):
    rows = projected.shape[0]
    head = q_gain.shape[1]
    pair = 2 if heads % 2 == 0 else 1
    fixed = lambda *shape: pl.BlockSpec(shape, lambda i: (0,) * len(shape))
    return pl.pallas_call(
        functools.partial(attention_forward_kernel, head ** -0.5),
        grid=(heads // pair,),
        out_shape=jax.ShapeDtypeStruct((rows, heads * head), BF16),
        in_specs=[
            pl.BlockSpec((rows, pair * head), lambda i: (0, i)),
            pl.BlockSpec((rows, head), lambda i: (0, heads)),
            pl.BlockSpec((rows, head), lambda i: (0, heads + 1)),
            fixed(1, rows), fixed(rows, 1), fixed(rows, head), fixed(rows, head), fixed(1, head), fixed(1, head),
        ],
        out_specs=pl.BlockSpec((rows, pair * head), lambda i: (0, i)),
        scratch_shapes=[pltpu.VMEM((rows, rows), F32), pltpu.VMEM((rows, head), BF16), pltpu.VMEM((rows, head), BF16)],
        compiler_params=pltpu.CompilerParams(vmem_limit_bytes=48 << 20),
        cost_estimate=pl.CostEstimate(flops=10000000000, bytes_accessed=10000000, transcendentals=0),
        name="attention_forward",
    )(projected, projected, projected, segs, segs_t, cos_wide, sin_wide, q_gain, k_gain)

def norm_back(values, gain, upstream):
    factor = unit(values)
    weighted = upstream * gain
    inner = jnp.mean(weighted * values, axis=1, keepdims=True)
    return weighted * factor - values * (factor * factor * factor * inner), upstream * values * factor

def attention_backward_kernel(scale, finish, q_ref, k_ref, v_ref, g_ref, segs_ref, segs_t_ref, cos_ref, sin_ref, q_gain_ref, k_gain_ref,
                              out_ref, key_ref, value_ref, inner_ref, gains_ref, bias, key, value, inner):
    head = k_ref.shape[1]
    rows = q_ref.shape[0]
    half = rows // 2
    cos_wide, sin_wide = cos_ref[...], sin_ref[...]
    step, steps = pl.program_id(0), pl.num_programs(0)
    pair = q_ref.shape[1] // head

    @pl.when(step == 0)
    def _():
        bias[...] = sequence_bias(segs_ref, segs_t_ref)
        k_pre = k_ref[...]
        key[...] = turn(k_pre * unit(k_pre) * k_gain_ref[...], cos_wide, sin_wide).astype(BF16)
        value[...] = v_ref[...].astype(BF16)
        key_ref[...] = jnp.zeros_like(key_ref)
        value_ref[...] = jnp.zeros_like(value_ref)
        inner[...] = jnp.zeros_like(inner)
        gains_ref[...] = jnp.zeros_like(gains_ref)

    for h in range(pair):
        lanes = slice(h * head, (h + 1) * head)
        q_pre = q_ref[:, lanes]
        query = turn(q_pre * unit(q_pre) * q_gain_ref[...], cos_wide, sin_wide).astype(BF16)
        grads = []
        for part in range(2):
            at, keys = slice(part * half, (part + 1) * half), slice(0, (part + 1) * half)
            probs = block_probs(query[at], key[keys, :], bias[at, keys], scale)
            upstream = g_ref[at, lanes]
            prob_grad = mm_nt(upstream, value[keys, :])
            score_grad = (probs * (prob_grad - jnp.sum(probs * prob_grad, axis=1, keepdims=True))).astype(BF16)
            grads.append(mm(score_grad, key[keys, :]) * scale)
            key_ref[keys, :] += mm_tn(score_grad, query[at]) * scale
            value_ref[keys, :] += mm_tn(probs.astype(BF16), upstream)
        query_grad = turn(jnp.concatenate(grads, axis=0), cos_wide, -sin_wide)
        q_grad, terms = norm_back(q_pre, q_gain_ref[...], query_grad)
        low = q_grad.astype(BF16)
        out_ref[:, pl.ds(pl.multiple_of((step * pair + h) * head, head), head)] = low
        inner[...] += low.astype(F32) * q_pre
        gains_ref[0:1, :] += jnp.sum(terms, axis=0, keepdims=True)

    @pl.when(step == steps - 1)
    def _():
        total = jnp.sum(inner[...], axis=1, keepdims=True)
        if finish:
            k_pre, v_pre = k_ref[...], v_ref[...]
            k_grad, terms = norm_back(k_pre, k_gain_ref[...], turn(key_ref[...], cos_wide, -sin_wide))
            k_low, v_low = k_grad.astype(BF16), value_ref[...].astype(BF16)
            width = steps * pair * head
            out_ref[:, pl.ds(out_ref.shape[1] - 2 * head, head)] = k_low
            out_ref[:, pl.ds(out_ref.shape[1] - head, head)] = v_low
            gains_ref[1:2, :] = jnp.sum(terms, axis=0, keepdims=True)
            total = total + jnp.sum(k_low.astype(F32) * k_pre + v_low.astype(F32) * v_pre, axis=1, keepdims=True)
        inner_ref[...] = total

def attention_backward(finish, projected, upstream, heads, segs, segs_t, cos_wide, sin_wide, q_gain, k_gain):
    rows = projected.shape[0]
    head = q_gain.shape[1]
    pair = 2 if heads % 2 == 0 else 1
    fixed = lambda *shape: pl.BlockSpec(shape, lambda i: (0,) * len(shape))
    return pl.pallas_call(
        functools.partial(attention_backward_kernel, head ** -0.5, finish),
        grid=(heads // pair,),
        out_shape=[
            jax.ShapeDtypeStruct((rows, (heads + 2) * head), BF16),
            jax.ShapeDtypeStruct((rows, head), F32),
            jax.ShapeDtypeStruct((rows, head), F32),
            jax.ShapeDtypeStruct((rows, 1), F32),
            jax.ShapeDtypeStruct((2, head), F32),
        ],
        in_specs=[
            pl.BlockSpec((rows, pair * head), lambda i: (0, i)),
            pl.BlockSpec((rows, head), lambda i: (0, heads)),
            pl.BlockSpec((rows, head), lambda i: (0, heads + 1)),
            pl.BlockSpec((rows, pair * head), lambda i: (0, i)),
            fixed(1, rows), fixed(rows, 1), fixed(rows, head), fixed(rows, head), fixed(1, head), fixed(1, head),
        ],
        out_specs=[fixed(rows, (heads + 2) * head), fixed(rows, head), fixed(rows, head), fixed(rows, 1), fixed(2, head)],
        scratch_shapes=[pltpu.VMEM((rows, rows), F32), pltpu.VMEM((rows, head), BF16), pltpu.VMEM((rows, head), BF16), pltpu.VMEM((rows, head), F32)],
        compiler_params=pltpu.CompilerParams(vmem_limit_bytes=48 << 20),
        cost_estimate=pl.CostEstimate(flops=20000000000, bytes_accessed=10000000, transcendentals=0),
        name="attention_backward",
    )(projected, projected, projected, upstream, segs, segs_t, cos_wide, sin_wide, q_gain, k_gain)

def norm_kernel(in_ref, gain_ref, out_ref, scale_ref):
    wide = in_ref[...].astype(F32)
    scale = unit(wide)
    scale_ref[...] = scale
    out_ref[...] = (wide * scale * gain_ref[...]).astype(BF16)


def normalized(values, gain):
    rows, width = values.shape
    block = min(128, rows)
    return pl.pallas_call(
        norm_kernel,
        grid=(rows // block,),
        out_shape=[jax.ShapeDtypeStruct((rows, width), BF16), jax.ShapeDtypeStruct((rows, 1), F32)],
        in_specs=[
            pl.BlockSpec((block, width), lambda i: (i, 0)),
            pl.BlockSpec((1, width), lambda i: (0, 0)),
        ],
        out_specs=[
            pl.BlockSpec((block, width), lambda i: (i, 0)),
            pl.BlockSpec((block, 1), lambda i: (i, 0)),
        ],
        compiler_params=pltpu.CompilerParams(vmem_limit_bytes=32 << 20),
        cost_estimate=pl.CostEstimate(flops=2000000000, bytes_accessed=8000000, transcendentals=0),
        name="normalized",
    )(values, gain)


def norm_pieces_kernel(count, scalars_ref, *refs):
    pieces, gain_ref, out_ref, scale_ref = refs[:count], refs[count], refs[count + 1], refs[count + 2]
    width = pieces[0].shape[1]
    total = None
    for piece in pieces:
        wide = piece[...].astype(F32)
        part = jnp.sum(wide * wide, axis=1, keepdims=True)
        total = part if total is None else total + part
    scale = lax.rsqrt(total / (width * count) + EPSILON)
    scale_ref[...] = scale
    for i, piece in enumerate(pieces):
        at = pl.ds(pl.multiple_of((scalars_ref[1] + i) % count * width, width), width)
        out_ref[:, at] = (piece[...].astype(F32) * scale * gain_ref[:, at]).astype(BF16)


def normalized_pieces(pieces, offsets, rows, scalars, gain):
    count = len(pieces)
    width = pieces[0].shape[1]
    block = min(128, rows)
    return pl.pallas_call(
        functools.partial(norm_pieces_kernel, count),
        grid=(rows // block,),
        out_shape=[
            jax.ShapeDtypeStruct((rows, width * count), BF16),
            jax.ShapeDtypeStruct((rows, 1), F32),
        ],
        in_specs=[pl.BlockSpec(memory_space=pltpu.SMEM)]
        + [pl.BlockSpec((block, width), lambda i, o=o: (o // block + i, 0)) for o in offsets]
        + [pl.BlockSpec((1, width * count), lambda i: (0, 0))],
        out_specs=[
            pl.BlockSpec((block, width * count), lambda i: (i, 0)),
            pl.BlockSpec((block, 1), lambda i: (i, 0)),
        ],
        compiler_params=pltpu.CompilerParams(vmem_limit_bytes=32 << 20),
        cost_estimate=pl.CostEstimate(flops=2000000000, bytes_accessed=8000000, transcendentals=0),
        name="normalized_pieces",
    )(scalars, *pieces, gain)


def pair_kernel(first, place, experts, scalars_ref, slots_ref, slots_t_ref, mask_ref, router_ref, *refs):
    refs = list(refs)
    token_in, grad_in = refs[0:2], refs[2:4]
    weights_in = refs[4:7]
    del refs[:7]
    if not first:
        del refs[:5]
    y_out, x_out = refs[0:2], refs[2:4]
    small_out, logits_out, gates_out = refs[4:7]
    kept_out = refs[7:12]
    (token, grad, gate_w, up_w, down_w, y_buf, x_buf, rows_in, rows_grad, rows_u, rows_da, rows_db, in_sem, grad_sem, w_sem, out_sem, kept_sem) = refs[12:]
    capacity = rows_in.shape[0] // 2
    tokens, width = token.shape[1:]
    hidden = gate_w.shape[1]
    load_tok = [pltpu.make_async_copy(token_in[g], token.at[g], in_sem.at[g]) for g in range(2)]
    parts = grad_sem.shape[1]
    strip = width // parts
    load_grad = []
    for g in range(2):
        for d in range(parts):
            there = pl.multiple_of((scalars_ref[1] + d) % parts * strip, strip)
            load_grad.append(
                pltpu.make_async_copy(
                    grad_in[g].at[:, d * strip : (d + 1) * strip],
                    grad.at[g, :, pl.ds(there, strip)],
                    grad_sem.at[g, d],
                )
            )
    load_w = [
        pltpu.make_async_copy(src, dst, w_sem.at[i])
        for i, (src, dst) in enumerate(zip(weights_in, (gate_w, up_w, down_w)))
    ]
    load_tok[0].start()
    for load in load_grad[:parts]:
        load.start()
    for load in load_w:
        load.start()
    load_tok[1].start()
    for load in load_grad[parts:]:
        load.start()
    expert = scalars_ref[0]
    stores = []
    wide = min(512, width)
    step = 256 if hidden % 256 == 0 else hidden
    chosen_rows, spreads, gate_cols = [], [], []
    for g in range(2):
        load_tok[g].wait()
        logits = mm(token[g], router_ref[...])
        shifted = logits + mask_ref[g].astype(F32)
        weights = jnp.exp(shifted - jnp.max(shifted, axis=1, keepdims=True))
        gates = weights / jnp.sum(weights, axis=1, keepdims=True)
        if g == 0:
            logits_out[...] = logits
            gates_out[...] = gates
        gates_t = gates.T
        lane = lax.broadcasted_iota(jnp.int32, gates_t.shape, 0)
        gate_row = jnp.sum(jnp.where(lane == expert, gates_t, 0.0), axis=0, keepdims=True)
        chosen = lax.broadcasted_iota(jnp.int32, (capacity, tokens), 0) == slots_ref[g]
        slot_gates = jnp.sum(jnp.where(chosen, gate_row, 0.0), axis=1, keepdims=True)
        pick = jnp.where(chosen, 1.0, 0.0).astype(BF16)
        here = slice(g * capacity, (g + 1) * capacity)
        gate_cols.append(slot_gates)
        for load in load_grad[g * parts : (g + 1) * parts]:
            load.wait()

        def gather(j, _):
            at = pl.ds(pl.multiple_of(j * wide, wide), wide)
            rows_in[here, at] = mm(pick, token[g, :, at]).astype(BF16)
            rows_grad[here, at] = mm(pick, grad[g, :, at]).astype(BF16)
            return 0

        lax.fori_loop(0, width // wide, gather, 0)
    for load in load_w:
        load.wait()
    slot_gates = jnp.concatenate(gate_cols, axis=0)

    def middle(j, carry):
        dots, inner = carry
        at = pl.ds(pl.multiple_of(j * step, step), step)
        a = mm(rows_in[...], gate_w[:, at])
        b = mm(rows_in[...], up_w[:, at])
        raw = mm_nt(rows_grad[...], down_w[at, :])
        sig = 1.0 / (1.0 + jnp.exp(-a))
        silu = a * sig
        u = (silu * b).astype(BF16).astype(F32)
        dots = dots + jnp.sum(raw * u, axis=1, keepdims=True)
        du = (slot_gates * raw).astype(BF16).astype(F32)
        da = du * b * sig * (1.0 + a * (1.0 - sig))
        db = du * silu
        inner = inner + jnp.sum(da * a + db * b, axis=1, keepdims=True)
        rows_u[:, at] = (slot_gates * u).astype(BF16)
        rows_da[:, at] = da.astype(BF16)
        rows_db[:, at] = db.astype(BF16)
        return dots, inner

    nothing = jnp.zeros((2 * capacity, 1), F32)
    dots, inner = lax.fori_loop(0, hidden // step, middle, (nothing, nothing))
    kept_here = pl.ds(place * 2 * capacity, 2 * capacity)
    for i, kept_rows in enumerate((rows_in, rows_grad, rows_u, rows_da, rows_db)):
        store = pltpu.make_async_copy(kept_rows, kept_out[i].at[kept_here, :], kept_sem.at[i])
        store.start()
        stores.append(store)
    spreads = [
        jnp.where(
            lax.broadcasted_iota(jnp.int32, (tokens, capacity), 1) == slots_t_ref[g], 1.0, 0.0
        ).astype(BF16)
        for g in range(2)
    ]
    for j in range(width // wide):
        at = slice(j * wide, (j + 1) * wide)
        dx = mm_nt(rows_da[...], gate_w[at, :]) + mm_nt(rows_db[...], up_w[at, :])
        y = mm(rows_u[...], down_w[:, at])
        for i, (rows, buf, out) in enumerate(((dx, x_buf, x_out), (y, y_buf, y_out))):
            low = rows.astype(BF16)
            for g in range(2):
                here = slice(g * capacity, (g + 1) * capacity)
                buf[g, :, at] = mm(spreads[g], low[here]).astype(BF16)
                store = pltpu.make_async_copy(
                    buf.at[g, :, at], out[g].at[:, at], out_sem.at[i, g, j]
                )
                store.start()
                stores.append(store)
    small_row = lax.broadcasted_iota(jnp.int32, small_out.shape[1:], 0)
    for g in range(2):
        here = slice(g * capacity, (g + 1) * capacity)
        chosen = lax.broadcasted_iota(jnp.int32, (capacity, tokens), 0) == slots_ref[g]
        dots_row = jnp.sum(jnp.where(chosen, dots[here], 0.0), axis=0, keepdims=True)
        inner_row = jnp.sum(jnp.where(chosen, inner[here], 0.0), axis=0, keepdims=True)
        small_out[g] = jnp.where(small_row == expert, dots_row, 0.0) + jnp.where(
            small_row == experts, inner_row, 0.0
        )
    for store in stores:
        store.wait()


def expert_pair(
    place, places, capacity, experts, scalars, slots, slots_t, mask, router, tokens, grads, weights, kept
):
    rows, width = tokens[0].shape
    hidden = weights[0].shape[1]
    total = places * 2 * capacity
    anywhere = pl.BlockSpec(memory_space=pl.ANY)
    inside = pl.BlockSpec(memory_space=pltpu.VMEM)
    first = kept is None
    parts = lax.axis_size("row")
    small_rows = (experts + 8) // 8 * 8
    dense = jax.ShapeDtypeStruct((rows, width), BF16)
    kept_shapes = [jax.ShapeDtypeStruct((total, w), BF16) for w in (width, width, hidden, hidden, hidden)]
    flat = jax.ShapeDtypeStruct((rows, router.shape[1]), F32)
    out = pl.pallas_call(
        functools.partial(pair_kernel, first, place, experts),
        out_shape=[dense] * 4 + [jax.ShapeDtypeStruct((2, small_rows, rows), F32), flat, flat] + kept_shapes,
        in_specs=[pl.BlockSpec(memory_space=pltpu.SMEM)] + [inside] * 4 + [anywhere] * (7 if first else 12),
        out_specs=[anywhere] * 4 + [inside] * 3 + [anywhere] * 5,
        input_output_aliases={} if first else {12 + i: 7 + i for i in range(5)},
        scratch_shapes=[
            pltpu.VMEM((2, rows, width), BF16),
            pltpu.VMEM((2, rows, width), BF16),
            pltpu.VMEM((width, hidden), BF16),
            pltpu.VMEM((width, hidden), BF16),
            pltpu.VMEM((hidden, width), BF16),
            pltpu.VMEM((2, rows, width), BF16),
            pltpu.VMEM((2, rows, width), BF16),
            pltpu.VMEM((2 * capacity, width), BF16),
            pltpu.VMEM((2 * capacity, width), BF16),
            pltpu.VMEM((2 * capacity, hidden), BF16),
            pltpu.VMEM((2 * capacity, hidden), BF16),
            pltpu.VMEM((2 * capacity, hidden), BF16),
            pltpu.SemaphoreType.DMA((2,)),
            pltpu.SemaphoreType.DMA((2, parts)),
            pltpu.SemaphoreType.DMA((3,)),
            pltpu.SemaphoreType.DMA((2, 2, width // min(512, width))),
            pltpu.SemaphoreType.DMA((5,)),
        ],
        compiler_params=pltpu.CompilerParams(vmem_limit_bytes=56 << 20),
        cost_estimate=pl.CostEstimate(flops=36000000000, bytes_accessed=10000000, transcendentals=0),
        name="expert_pair",
    )(scalars, slots, slots_t, mask, router, *tokens, *grads, *weights, *([] if first else kept))
    return out


def route_kernel(expert_ref, routes_ref, mask_ref, slots_ref, slots_t_ref):
    rows, top_count = routes_ref.shape[1:]
    routes = routes_ref[0]
    lanes = lax.broadcasted_iota(jnp.int32, (rows, LANES), 1)
    chosen = routes[:, 0:1] == lanes
    for k in range(1, top_count):
        chosen = jnp.logical_or(chosen, routes[:, k : k + 1] == lanes)
    mask_ref[0] = jnp.where(chosen, 0.0, MASKED).astype(BF16)
    below = lax.broadcasted_iota(jnp.int32, (rows, rows), 1) <= lax.broadcasted_iota(
        jnp.int32, (rows, rows), 0
    )
    ones = jnp.where(chosen, 1.0, 0.0)
    ranks = mm(jnp.where(below, 1.0, 0.0).astype(BF16), ones.astype(BF16))
    slots = jnp.where(chosen, ranks - 1.0, -1.0)
    here = lanes == expert_ref[0]
    slots_t_ref[0] = jnp.max(jnp.where(here, slots, -1.0), axis=1, keepdims=True).astype(jnp.int32)
    lane_first = lax.broadcasted_iota(jnp.int32, (LANES, rows), 0)
    slots_ref[0] = jnp.max(
        jnp.where(lane_first == expert_ref[0], slots.T, -1.0), axis=0, keepdims=True
    ).astype(jnp.int32)


def route_tables(scalars, routes):
    blocks, rows, top_count = routes.shape
    return pl.pallas_call(
        route_kernel,
        grid=(blocks,),
        out_shape=[
            jax.ShapeDtypeStruct((blocks, rows, LANES), BF16),
            jax.ShapeDtypeStruct((blocks, 1, rows), jnp.int32),
            jax.ShapeDtypeStruct((blocks, rows, 1), jnp.int32),
        ],
        in_specs=[
            pl.BlockSpec(memory_space=pltpu.SMEM),
            pl.BlockSpec((1, rows, top_count), lambda i: (i, 0, 0)),
        ],
        out_specs=[
            pl.BlockSpec((1, rows, LANES), lambda i: (i, 0, 0)),
            pl.BlockSpec((1, 1, rows), lambda i: (i, 0, 0)),
            pl.BlockSpec((1, rows, 1), lambda i: (i, 0, 0)),
        ],
        compiler_params=pltpu.CompilerParams(vmem_limit_bytes=32 << 20),
        cost_estimate=pl.CostEstimate(flops=1000000000, bytes_accessed=1000000, transcendentals=0),
        name="route_tables",
    )(scalars, routes)


def place_kernel(axis, starts_ref, *refs):
    out = refs[-1]
    for i, piece in enumerate(refs[:-1]):
        width = piece.shape[axis]
        at = pl.ds(pl.multiple_of(starts_ref[i] * width, width), width)
        if axis == 0:
            out[at, :] = piece[...]
        else:
            out[:, at] = piece[...]


def placed(pieces, starts, axis):
    shape = list(pieces[0].shape)
    shape[axis] *= len(pieces)
    inside = pl.BlockSpec(memory_space=pltpu.VMEM)
    return pl.pallas_call(
        functools.partial(place_kernel, axis),
        out_shape=jax.ShapeDtypeStruct(tuple(shape), pieces[0].dtype),
        in_specs=[pl.BlockSpec(memory_space=pltpu.SMEM)] + [inside] * len(pieces),
        out_specs=inside,
        compiler_params=pltpu.CompilerParams(vmem_limit_bytes=32 << 20),
        cost_estimate=pl.CostEstimate(flops=1000000, bytes_accessed=10000000, transcendentals=0),
        name="placed",
    )(starts, *pieces)


def pieces_kernel(counts, own_ref, *refs):
    out_ref = refs[-1]
    step, start = pl.program_id(0), 0
    for count, piece in zip(counts, refs[:-1]):

        @pl.when(jnp.logical_and(step >= start, step < start + count))
        def _():
            out_ref[...] = own_ref[...].astype(F32) + piece[...].astype(F32)

        start += count


def pieces_sum(own, pieces):
    rows, width = own.shape
    block = math.gcd(*[piece.shape[0] for piece in pieces])
    counts = [piece.shape[0] // block for piece in pieces]
    specs, start = [pl.BlockSpec((block, width), lambda i: (i, 0))], 0
    for count in counts:
        specs.append(
            pl.BlockSpec(
                (block, width), lambda i, s=start, c=count: (jnp.clip(i - s, 0, c - 1), 0)
            )
        )
        start += count
    return pl.pallas_call(
        functools.partial(pieces_kernel, counts),
        grid=(rows // block,),
        out_shape=jax.ShapeDtypeStruct((rows, width), F32),
        in_specs=specs,
        out_specs=pl.BlockSpec((block, width), lambda i: (i, 0)),
        compiler_params=pltpu.CompilerParams(vmem_limit_bytes=32 << 20),
        cost_estimate=pl.CostEstimate(flops=4000000000, bytes_accessed=12000000, transcendentals=0),
        name="pieces_sum",
    )(own, *pieces)


def grads_kernel(rows_ref, *refs):
    half = len(refs) // 2
    for grad_ref, out_ref in zip(refs[:half], refs[half:]):
        out_ref[...] = mm_tn(rows_ref[...], grad_ref[...]).astype(BF16)


def grads_of(rows_in, *grads):
    count, width = rows_in.shape
    hidden = grads[0].shape[1]
    block = min(512, width)
    return pl.pallas_call(
        grads_kernel,
        grid=(width // block,),
        out_shape=[jax.ShapeDtypeStruct((width, hidden), BF16)] * len(grads),
        in_specs=[pl.BlockSpec((count, block), lambda i: (0, i))]
        + [pl.BlockSpec((count, hidden), lambda i: (0, 0))] * len(grads),
        out_specs=[pl.BlockSpec((block, hidden), lambda i: (i, 0))] * len(grads),
        compiler_params=pltpu.CompilerParams(vmem_limit_bytes=56 << 20),
        cost_estimate=pl.CostEstimate(flops=1000000000, bytes_accessed=1000000, transcendentals=0),
        name="grads_of",
    )(rows_in, *grads)


def grad_of(rows_u, rows_grad):
    count, hidden = rows_u.shape
    width = rows_grad.shape[1]
    block = min(512, width)
    return pl.pallas_call(
        grads_kernel,
        grid=(width // block,),
        out_shape=[jax.ShapeDtypeStruct((hidden, width), BF16)],
        in_specs=[
            pl.BlockSpec((count, hidden), lambda i: (0, 0)),
            pl.BlockSpec((count, block), lambda i: (0, i)),
        ],
        out_specs=[pl.BlockSpec((hidden, block), lambda i: (0, i))],
        compiler_params=pltpu.CompilerParams(vmem_limit_bytes=56 << 20),
        cost_estimate=pl.CostEstimate(flops=1000000000, bytes_accessed=1000000, transcendentals=0),
        name="grad_of",
    )(rows_u, rows_grad)[0]


def moved(block, axis, by):
    count = lax.axis_size(axis)
    return lax.ppermute(block, axis, [(i, (i + by) % count) for i in range(count)])


def swapped(block, axis, bit):
    count = lax.axis_size(axis)
    return lax.ppermute(block, axis, [(i, i ^ (1 << bit)) for i in range(count)])


def butterfly(values, axis):
    for bit in range(lax.axis_size(axis).bit_length() - 1):
        values = values + swapped(values, axis, bit)
    return values


def ring_pieces(block):
    count = lax.axis_size("row")
    pieces = [[block]] + [None] * (count - 1)
    from_left = from_right = block
    half = block.shape[0] // 2
    for step in range(1, count // 2):
        from_left = moved(from_left, "row", 1)
        from_right = moved(from_right, "row", -1)
        pieces[count - step] = [from_left]
        pieces[step] = [from_right]
    if count > 1:
        pieces[count // 2] = [
            moved(from_left[:half], "row", 1),
            moved(from_right[half:], "row", -1),
        ]
    return pieces


def joined(pieces, number, rows):
    blocks = []
    for piece in pieces:
        tall = piece[0].shape[0]
        if len(piece) == 1:
            blocks.append(piece[0][number * rows : (number + 1) * rows])
        elif tall >= rows:
            start = number * rows % tall
            blocks.append(piece[number * rows // tall][start : start + rows])
        else:
            whole = jnp.concatenate(piece, axis=0)
            blocks.append(whole[number * rows : (number + 1) * rows])
    return jnp.concatenate(blocks, axis=1)


def row_gather(block):
    return lax.all_gather(block, "row", axis=block.ndim - 1, tiled=True)


def row_scatter(partial):
    return lax.psum_scatter(partial, "row", scatter_dimension=1, tiled=True)


def after(value, *others):
    return lax.optimization_barrier((value,) + others)[0]


class Link:
    def __init__(self):
        self.last = ()

    def moved(self, block, by):
        block = moved(after(block, *self.last), "col", by)
        self.last = (block,)
        return block


class PairLink:
    def __init__(self):
        self.last = ()

    def swapped(self, block):
        block = swapped(after(block, *self.last), "dp", 0)
        self.last = (block,)
        return block


def col_gather(block, link):
    count = lax.axis_size("col")
    pieces = []
    for step in range(count // 2):
        same = block if step == 0 else link.moved(block, 2 * step)
        pieces += [same, swapped(same, "col", 0)]
    return pieces


def added(*parts):
    total = parts[0].astype(F32)
    for part in parts[1:]:
        total = total + part.astype(F32)
    return total.astype(parts[0].dtype)


def chips_total(totals, link, *others):
    parts = list(totals[0])
    for step in range(1, len(totals)):
        parts.append(after(link.moved(added(*totals[step]), -2 * step), *others))
    return added(*parts)


def col_order():
    count = lax.axis_size("col")
    place = lax.axis_index("col")
    chip, core = place // 2, place % 2
    order = []
    for step in range(count // 2):
        back = (chip - step) % (count // 2) * 2
        order += [back + core, back + 1 - core]
    return order


def col_assemble(block, axis, link):
    return placed(col_gather(block, link), jnp.stack(col_order()).astype(jnp.int32), axis)


def col_share(partial, axis, link):
    count = lax.axis_size("col")
    width = partial.shape[axis] // count
    pieces = [
        lax.dynamic_slice_in_dim(partial, place * width, width, axis)
        for place in col_order()
    ]
    return chips_total(
        [
            (pieces[2 * step], swapped(pieces[2 * step + 1], "col", 0))
            for step in range(count // 2)
        ],
        link,
    )


def positions(segment_ids):
    places = jnp.arange(segment_ids.shape[0], dtype=jnp.int32)
    earlier = jnp.concatenate([segment_ids[:1] - 1, segment_ids[:-1]])
    starts = jnp.logical_or(segment_ids != earlier, places % SEQUENCE_TOKENS == 0)
    opening = lax.cummax(jnp.where(starts, places, 0), axis=0)
    return places - opening


def rotary(places, head_size):
    halfway = head_size // 2
    frequency = ROPE_BASE ** (-2.0 * jnp.arange(halfway, dtype=F32) / head_size)
    angles = places.astype(F32)[:, None] * frequency[None, :]
    cos_part, sin_part = jnp.cos(angles), jnp.sin(angles)
    return (
        jnp.concatenate([cos_part, cos_part], axis=1),
        jnp.concatenate([-sin_part, sin_part], axis=1),
    )


def turn_plain(values, cos_wide, sin_wide):
    return values * cos_wide + jnp.roll(values, values.shape[1] // 2, 1) * sin_wide


def per_device(
    residual,
    segments,
    routes,
    norm_attention,
    query_weight,
    key_projection_matrix,
    value_projection_matrix,
    query_gain,
    key_gain,
    out_weight,
    norm_experts,
    router_weight,
    gate_weight,
    up_weight,
    down_weight,
    grad_output,
):
    row_count = lax.axis_size("row")
    col_count = lax.axis_size("col")
    row_place = lax.axis_index("row")
    col_place = lax.axis_index("col")
    model_width = norm_attention.shape[0]
    feature_width = model_width // row_count
    head_size = query_gain.shape[0]
    heads_here = query_weight.shape[1] // head_size
    query_width = heads_here * head_size
    kv_heads = key_projection_matrix.shape[1] // head_size
    query_group_width = heads_here * row_count // kv_heads
    members = query_group_width // heads_here
    kv_index = row_place * heads_here // query_group_width
    member_place = row_place % members
    share_width = head_size // members
    column_mask = (jnp.arange(head_size, dtype=jnp.int32) // share_width == member_place).astype(
        F32
    )
    experts = gate_weight.shape[0] * row_count * col_count
    expert = row_place * col_count + col_place
    chips = col_count // 2
    token_rows = residual.shape[0]
    rows = SEQUENCE_TOKENS
    chunks = token_rows // rows
    top_count = routes.shape[1]
    capacity = max(2, 5 * rows * top_count // (4 * experts))
    row_start = row_place * feature_width
    labels = jnp.arange(experts, dtype=jnp.int32)
    scalars = jnp.stack([expert, row_place]).astype(jnp.int32)
    key_part = lax.dynamic_slice_in_dim(key_projection_matrix, kv_index * head_size, head_size, 1)
    value_part = lax.dynamic_slice_in_dim(
        value_projection_matrix, kv_index * head_size, head_size, 1
    )

    def chunk(array, number):
        return array[number * rows : (number + 1) * rows]

    link = Link()
    inputs_full = [row_gather(chunk(residual, n)) for n in range(chunks)]
    projection = col_assemble(
        jnp.concatenate([query_weight, key_part, value_part], axis=1), 0, link
    )
    routes_all = jnp.stack(col_gather(routes, link)).reshape(col_count * chunks, rows, top_count)
    out_full = col_assemble(out_weight, 1, link)
    grads_cols = [None] * chunks
    grad_pieces = ring_pieces(grad_output)
    grads_near = [piece[0] for piece in grad_pieces[1:] if len(piece) == 1]
    grads_middle = [block for piece in grad_pieces if len(piece) > 1 for block in piece]
    for n in range(chunks):
        grads_cols[n] = col_gather(joined(grad_pieces, n, rows), link)
    grads_far = [[g for g in grads_cols[n][2::2]] for n in range(chunks)]

    gain_one = lax.dynamic_slice_in_dim(norm_attention, row_start, feature_width)
    gain_two = lax.dynamic_slice_in_dim(norm_experts, row_start, feature_width)
    router_rows = lax.dynamic_slice_in_dim(router_weight, row_start, feature_width, 0)
    router = jnp.pad(router_weight, ((0, 0), (0, LANES - experts)))
    cos_all, sin_all = rotary(positions(segments), head_size)
    tables = [(chunk(cos_all, n), chunk(sin_all, n)) for n in range(chunks)]
    segs = [(chunk(segments, n)[None, :], chunk(segments, n)[:, None]) for n in range(chunks)]
    head_gains = (query_gain[None, :], key_gain[None, :])
    state = [{} for _ in range(chunks)]

    for n in range(chunks):
        s = state[n]
        s["normed_full"], s["scale_one"] = normalized(inputs_full[n], norm_attention[None, :])
        normed = s["normed_full"] if n == 0 else after(s["normed_full"], *grads_near)
        s["projected"] = mm(normed, projection)
        s["mixed"] = attention_forward(
            s["projected"], heads_here, *segs[n], *tables[n], *head_gains
        )
        partial = mm(s["mixed"], out_full).astype(BF16)
        s["mixed_out"] = partial
    masks, slots, slots_t = (
        table.reshape(col_count, chunks, *table.shape[1:])
        for table in route_tables(scalars, after(routes_all, partial))
    )

    kept = None

    def run_pair(n, place, *others):
        nonlocal kept
        s = state[n]
        two = slice(2 * place, 2 * place + 2)
        found = expert_pair(
            n * chips + place,
            chunks * chips,
            capacity,
            experts,
            scalars,
            slots[two, n],
            slots_t[two, n],
            masks[two, n],
            after(router, *others),
            s["tokens"][two],
            grads_cols[n][two],
            (gate_weight[0], up_weight[0], down_weight[0]),
            kept,
        )
        kept = found[7:]
        for name, same, other in (
            ("y", found[0], found[1]),
            ("x", found[2], found[3]),
            ("small", found[4][0], found[4][1]),
        ):
            other = swapped(other, "col", 0)
            s.setdefault(name, []).append(
                (same, other) if place == 0 else (added(same, other),)
            )
        if place == 0:
            s["logits"], s["gates"] = found[5][:, :experts], found[6][:, :experts]

    def hidden_of(n, ready, *others):
        s = state[n]
        summed = row_scatter(after(s["mixed_out"], *ready))
        s["hidden"] = chunk(residual, n).astype(F32) + after(summed, *others).astype(F32)
        s["wide"] = row_gather(after(s["hidden"].astype(BF16), masks))

    def second_norm(n, *others):
        s = state[n]
        s["normed_two"], s["scale_two"] = normalized(
            after(s["wide"], *others), norm_experts[None, :]
        )
        own = s["normed_two"]
        s["tokens"] = [own, swapped(own, "col", 0)]
        s["far"] = [link.moved(own, 2 * step) for step in range(1, chips)]

    def far_tokens(n, *others):
        for block in state[n]["far"]:
            same = after(block, *others)
            state[n]["tokens"] += [same, swapped(same, "col", 0)]

    def to_row(n, *others):
        s = state[n]
        s["small"] = butterfly(chips_total(s["small"], link), "row")
        s["total"] = chips_total(s["x"], link, *others)

    hidden_of(0, (), *grads_middle)
    second_norm(0, *grads_far[0], *grads_far[-1])
    for n in range(chunks):
        s = state[n]
        run_pair(n, 0, *([x[0] for x in state[n - 1]["x"][1:]] if n > 0 else []))
        spacer = s["small"][0][1]
        far_tokens(n, spacer)
        if n + 1 < chunks:
            hidden_of(n + 1, (s["wide"],), spacer)
        for place in range(1, chips):
            run_pair(n, place, spacer)
        if n > 0:
            to_row(n - 1, s["small"][-1][0])
        if n + 1 < chunks:
            second_norm(n + 1, s["small"][-1][0])
    pair = PairLink()
    own_grads, other_grads = [], []

    def expert_grads():
        grad_down = grad_of(kept[2], kept[1])
        grad_gate, grad_up = grads_of(after(kept[0], grad_down), kept[3], kept[4])
        own_grads.extend((grad_gate, grad_up, grad_down))
        wide, deep = grad_gate.shape[0], grad_down.shape[0]
        first, middle = wide // 8, wide // 2
        cuts = [(0, 0, first), (2, 0, deep // 2), (2, deep // 2, deep), (0, first, middle)]
        cuts += [(0, middle, wide), (1, 0, wide // 2), (1, wide // 2, wide)]
        for i, low, high in cuts:
            other_grads.append(pair.swapped(own_grads[i][low:high]))
        return other_grads[:1]

    acc_router = jnp.zeros((feature_width, experts), F32)
    acc_gain_two = jnp.zeros((feature_width,), F32)
    for n in range(chunks):
        s = state[n]
        if n == chunks - 1:
            to_row(n, *expert_grads())
        normed_two_grad = row_scatter(s["total"])
        hidden = s["hidden"]
        gate_dots = s["small"][:experts].T
        slot_inner = s["small"][experts]
        pick_grad = s["gates"] * (
            gate_dots - jnp.sum(s["gates"] * gate_dots, axis=1, keepdims=True)
        )
        logit_grad = pick_grad.astype(BF16)
        shard = lax.dynamic_slice_in_dim(s["normed_two"], row_start, feature_width, 1)
        acc_router = acc_router + lax.dot_general(
            shard, logit_grad, TN, preferred_element_type=F32
        )
        normed_two_grad = normed_two_grad.astype(F32) + lax.dot_general(
            logit_grad, router_rows, NT, preferred_element_type=F32
        )
        inner_two = slot_inner[:, None] + jnp.sum(
            logit_grad.astype(F32) * s["logits"], axis=1, keepdims=True
        )
        scale_two = s["scale_two"]
        s["hidden_total"] = (
            chunk(grad_output, n).astype(F32)
            + normed_two_grad * gain_two * scale_two
            - hidden * (scale_two * scale_two * inner_two / model_width)
        )
        s["branch_full"] = row_gather(s["hidden_total"].astype(BF16))
        acc_gain_two = acc_gain_two + jnp.sum(normed_two_grad * hidden * scale_two, axis=0)

    for n in range(chunks):
        state[n]["mixed_total"] = chips_total(state[n]["y"], link)

    acc_out = acc_query = acc_key = None
    acc_gain_one = jnp.zeros((model_width,), F32)
    acc_query_gain = jnp.zeros((head_size,), F32)
    acc_key_gain = jnp.zeros((head_size,), F32)
    input_blocks = []
    for n in range(chunks):
        s = state[n]
        branch_full = s["branch_full"]
        if n == chunks - 1:
            branch_full = after(branch_full, other_grads[1], state[0]["mixed_total"])
        mixed_grad = lax.dot_general(
            branch_full, out_full, NT, preferred_element_type=F32
        ).astype(BF16)
        out_here = lax.dot_general(s["mixed"], branch_full, TN, preferred_element_type=F32)
        acc_out = out_here if n == 0 else acc_out + out_here
        if n == chunks - 1:
            out_share = col_share(acc_out.astype(BF16), 1, link)
        projected_grad, key_grad, value_grad, inner_one, head_terms = attention_backward(
            members == 1, s["projected"], mixed_grad, heads_here, *segs[n], *tables[n], *head_gains
        )
        acc_query_gain = acc_query_gain + head_terms[0]
        if members == 1:
            acc_key_gain = acc_key_gain + head_terms[1]
        else:
            for bit in range(members.bit_length() - 1):
                key_grad = key_grad + swapped(key_grad, "row", bit)
                value_grad = value_grad + swapped(value_grad, "row", bit)
            key_pre = s["projected"][:, query_width : query_width + head_size]
            value_pre = s["projected"][:, query_width + head_size :]
            key_grad, key_terms = norm_back(
                key_pre, head_gains[1], turn_plain(key_grad, tables[n][0], -tables[n][1])
            )
            acc_key_gain = acc_key_gain + column_mask * jnp.sum(key_terms, axis=0)
            key_low = (column_mask * key_grad).astype(BF16)
            value_low = (column_mask * value_grad).astype(BF16)
            projected_grad = jnp.concatenate(
                [projected_grad[:, :query_width], key_low, value_low], axis=1
            )
            inner_one = inner_one + jnp.sum(
                key_low.astype(F32) * key_pre + value_low.astype(F32) * value_pre,
                axis=1,
                keepdims=True,
            )
        key_here = lax.dot_general(
            s["normed_full"], projected_grad[:, query_width:], TN, preferred_element_type=F32
        )
        acc_key = key_here if n == 0 else acc_key + key_here
        partial = lax.dot_general(
            projected_grad, projection, NT, preferred_element_type=F32
        ).astype(BF16)
        s["partial"] = partial
        normed_one_grad = row_scatter(partial)
        inner_one = butterfly(inner_one[:, 0], "row")[:, None]
        acc_gain_one = acc_gain_one + jnp.sum(
            partial.astype(F32) * s["normed_full"].astype(F32), axis=0
        )
        query_here = lax.dot_general(
            s["normed_full"], projected_grad[:, :query_width], TN, preferred_element_type=F32
        )
        acc_query = query_here if n == 0 else acc_query + query_here
        scale_one = s["scale_one"]
        if n == 0:
            normed_one_grad = after(normed_one_grad, other_grads[2], other_grads[3], state[-1]["mixed_total"])
        if n == chunks - 1:
            normed_one_grad = after(normed_one_grad, other_grads[4])
        input_blocks.append(
            s["hidden_total"]
            + normed_one_grad.astype(F32) * gain_one * scale_one
            - chunk(residual, n).astype(F32)
            * (scale_one * scale_one * inner_one / model_width)
        )

    key_share = col_share(acc_key.astype(BF16), 0, link)
    query_share = col_share(acc_query.astype(BF16), 0, link)
    for n in range(chunks):
        s = state[n]
        s["mixture"] = row_scatter(after(s["mixed_total"], state[-1]["partial"]))
    state[0]["mixture"] = after(state[0]["mixture"], *other_grads, out_share, key_share)
    out_other = pair.swapped(out_share)
    key_share = added(key_share, pair.swapped(key_share))
    shares = [jnp.concatenate(piece, axis=0) for piece in ring_pieces(key_share)]
    query_other = pair.swapped(query_share)
    state[-1]["mixture"] = after(
        state[-1]["mixture"], out_other, query_share, shares[1], shares[-1]
    )
    shares = jnp.concatenate(shares + shares, axis=1)
    shares = lax.dynamic_slice_in_dim(
        shares, (row_count - row_place) * 2 * head_size, row_count * 2 * head_size, 1
    )
    shares = shares.astype(F32).reshape(-1, kv_heads, members, 2, head_size).sum(axis=2)
    grad_key = shares[:, :, 0].reshape(-1, kv_heads * head_size)
    grad_value = shares[:, :, 1].reshape(-1, kv_heads * head_size)
    gain_two_full = lax.dynamic_update_slice_in_dim(
        jnp.zeros((model_width,), F32), acc_gain_two, row_start, 0
    )
    router_full = lax.dynamic_update_slice_in_dim(
        jnp.zeros((model_width, experts), F32), acc_router, row_start, 0
    )
    sizes = (model_width, model_width, head_size, head_size, model_width * experts)
    flat = jnp.concatenate(
        [
            acc_gain_one / norm_attention,
            gain_two_full,
            acc_query_gain,
            acc_key_gain,
            router_full.reshape(-1),
        ]
    )
    for axis in ("col", "row"):
        flat = butterfly(flat, axis)
    flat = after(flat, *[s["mixture"] for s in state])
    flat = flat + pair.swapped(flat)
    totals, start = [], 0
    for size in sizes:
        totals.append(flat[start : start + size])
        start += size
    grad_query = query_share.astype(F32) + query_other.astype(F32)
    grad_out_weight = out_share.astype(F32) + out_other.astype(F32)
    grad_gate, grad_up, grad_down = (
        pieces_sum(own, [other_grads[j] for j in parts])[None]
        for own, parts in zip(own_grads, ((0, 3, 4), (5, 6), (1, 2)))
    )
    output_blocks = [(s["hidden"] + s["mixture"].astype(F32)).astype(BF16) for s in state]
    return (
        jnp.concatenate(output_blocks, axis=0),
        jnp.concatenate(input_blocks, axis=0),
        totals[0],
        grad_query,
        grad_key,
        grad_value,
        totals[2],
        totals[3],
        grad_out_weight,
        totals[1],
        totals[4].reshape(model_width, experts),
        grad_gate,
        grad_up,
        grad_down,
    )


def solution(mesh):
    in_specs = (
        P(("dp", "col"), "row"),
        P(("dp", "col")),
        P(("dp", "col"), None),
        P(),
        P("col", "row"),
        P("col", None),
        P("col", None),
        P(),
        P(),
        P("row", "col"),
        P(),
        P(),
        P(("row", "col"), None, None),
        P(("row", "col"), None, None),
        P(("row", "col"), None, None),
        P(("dp", "col"), "row"),
    )
    out_specs = (
        P(("dp", "col"), "row"),
        P(("dp", "col"), "row"),
        P(),
        P("col", "row"),
        P("col", None),
        P("col", None),
        P(),
        P(),
        P("row", "col"),
        P(),
        P(),
        P(("row", "col"), None, None),
        P(("row", "col"), None, None),
        P(("row", "col"), None, None),
    )
    return jax.shard_map(
        per_device, mesh=mesh, in_specs=in_specs, out_specs=out_specs, check_vma=False
    )
```

```python
import functools
import math

import jax
import jax.numpy as jnp
from jax import lax
from jax.experimental import pallas as pl
from jax.experimental.pallas import tpu as pltpu
from jax.sharding import PartitionSpec as P

SEQUENCE_TOKENS = 512
EPSILON = 1e-06
ROPE_BASE = 1000000.0
MASKED = -1e30
LANES = 128
BF16 = jnp.bfloat16
F32 = jnp.float32
NT = (((1,), (1,)), ((), ()))
TN = (((0,), (0,)), ((), ()))

def mm(left, right):
    return jnp.dot(left, right, preferred_element_type=F32)

def mm_nt(left, right):
    return lax.dot_general(left, right, NT, preferred_element_type=F32)

def mm_tn(left, right):
    return lax.dot_general(left, right, (((0,), (0,)), ((), ())), preferred_element_type=F32)

def turn(values, cos_wide, sin_wide):
    return values * cos_wide + pltpu.roll(values, values.shape[1] // 2, 1) * sin_wide

def unit(values):
    return lax.rsqrt(jnp.mean(values * values, axis=1, keepdims=True) + EPSILON)

def sequence_bias(segs_ref, segs_t_ref):
    rows = segs_ref.shape[1]
    before = lax.broadcasted_iota(jnp.int32, (rows, rows), 1) <= lax.broadcasted_iota(jnp.int32, (rows, rows), 0)
    same = segs_t_ref[...] == segs_ref[...]
    return jnp.where(jnp.logical_and(same, before), 0.0, MASKED)

def block_probs(query, key, bias, scale):
    scores = mm_nt(query, key) * scale + bias
    weights = jnp.exp(scores - jnp.max(scores, axis=1, keepdims=True))
    return weights * (1.0 / jnp.sum(weights, axis=1, keepdims=True))

def attention_forward_kernel(scale, q_ref, k_ref, v_ref, segs_ref, segs_t_ref, cos_ref, sin_ref, q_gain_ref, k_gain_ref, out_ref, bias, key, value):
    head = k_ref.shape[1]
    rows = q_ref.shape[0]
    half = rows // 2
    cos_wide, sin_wide = cos_ref[...], sin_ref[...]

    @pl.when(pl.program_id(0) == 0)
    def _():
        bias[...] = sequence_bias(segs_ref, segs_t_ref)
        k_pre = k_ref[...]
        key[...] = turn(k_pre * unit(k_pre) * k_gain_ref[...], cos_wide, sin_wide).astype(BF16)
        value[...] = v_ref[...].astype(BF16)

    for h in range(q_ref.shape[1] // head):
        lanes = slice(h * head, (h + 1) * head)
        q_pre = q_ref[:, lanes]
        query = turn(q_pre * unit(q_pre) * q_gain_ref[...], cos_wide, sin_wide).astype(BF16)
        for part in range(2):
            at, keys = slice(part * half, (part + 1) * half), slice(0, (part + 1) * half)
            probs = block_probs(query[at], key[keys, :], bias[at, keys], scale)
            out_ref[at, lanes] = mm(probs.astype(BF16), value[keys, :]).astype(BF16)

def attention_forward(projected, heads, segs, segs_t, cos_wide, sin_wide, q_gain, k_gain):
    rows = projected.shape[0]
    head = q_gain.shape[1]
    pair = 2 if heads % 2 == 0 else 1
    fixed = lambda *shape: pl.BlockSpec(shape, lambda i: (0,) * len(shape))
    return pl.pallas_call(
        functools.partial(attention_forward_kernel, head ** -0.5),
        grid=(heads // pair,),
        out_shape=jax.ShapeDtypeStruct((rows, heads * head), BF16),
        in_specs=[
            pl.BlockSpec((rows, pair * head), lambda i: (0, i)),
            pl.BlockSpec((rows, head), lambda i: (0, heads)),
            pl.BlockSpec((rows, head), lambda i: (0, heads + 1)),
            fixed(1, rows), fixed(rows, 1), fixed(rows, head), fixed(rows, head), fixed(1, head), fixed(1, head),
        ],
        out_specs=pl.BlockSpec((rows, pair * head), lambda i: (0, i)),
        scratch_shapes=[pltpu.VMEM((rows, rows), F32), pltpu.VMEM((rows, head), BF16), pltpu.VMEM((rows, head), BF16)],
        compiler_params=pltpu.CompilerParams(vmem_limit_bytes=48 << 20),
        cost_estimate=pl.CostEstimate(flops=10000000000, bytes_accessed=10000000, transcendentals=0),
        name="attention_forward",
    )(projected, projected, projected, segs, segs_t, cos_wide, sin_wide, q_gain, k_gain)

def norm_back(values, gain, upstream):
    factor = unit(values)
    weighted = upstream * gain
    inner = jnp.mean(weighted * values, axis=1, keepdims=True)
    return weighted * factor - values * (factor * factor * factor * inner), upstream * values * factor

def attention_backward_kernel(scale, finish, q_ref, k_ref, v_ref, g_ref, segs_ref, segs_t_ref, cos_ref, sin_ref, q_gain_ref, k_gain_ref,
                              out_ref, key_ref, value_ref, inner_ref, gains_ref, bias, key, value, inner):
    head = k_ref.shape[1]
    rows = q_ref.shape[0]
    half = rows // 2
    cos_wide, sin_wide = cos_ref[...], sin_ref[...]
    step, steps = pl.program_id(0), pl.num_programs(0)
    pair = q_ref.shape[1] // head

    @pl.when(step == 0)
    def _():
        bias[...] = sequence_bias(segs_ref, segs_t_ref)
        k_pre = k_ref[...]
        key[...] = turn(k_pre * unit(k_pre) * k_gain_ref[...], cos_wide, sin_wide).astype(BF16)
        value[...] = v_ref[...].astype(BF16)
        key_ref[...] = jnp.zeros_like(key_ref)
        value_ref[...] = jnp.zeros_like(value_ref)
        inner[...] = jnp.zeros_like(inner)
        gains_ref[...] = jnp.zeros_like(gains_ref)

    for h in range(pair):
        lanes = slice(h * head, (h + 1) * head)
        q_pre = q_ref[:, lanes]
        query = turn(q_pre * unit(q_pre) * q_gain_ref[...], cos_wide, sin_wide).astype(BF16)
        grads = []
        for part in range(2):
            at, keys = slice(part * half, (part + 1) * half), slice(0, (part + 1) * half)
            probs = block_probs(query[at], key[keys, :], bias[at, keys], scale)
            upstream = g_ref[at, lanes]
            prob_grad = mm_nt(upstream, value[keys, :])
            score_grad = (probs * (prob_grad - jnp.sum(probs * prob_grad, axis=1, keepdims=True))).astype(BF16)
            grads.append(mm(score_grad, key[keys, :]) * scale)
            key_ref[keys, :] += mm_tn(score_grad, query[at]) * scale
            value_ref[keys, :] += mm_tn(probs.astype(BF16), upstream)
        query_grad = turn(jnp.concatenate(grads, axis=0), cos_wide, -sin_wide)
        q_grad, terms = norm_back(q_pre, q_gain_ref[...], query_grad)
        low = q_grad.astype(BF16)
        out_ref[:, pl.ds(pl.multiple_of((step * pair + h) * head, head), head)] = low
        inner[...] += low.astype(F32) * q_pre
        gains_ref[0:1, :] += jnp.sum(terms, axis=0, keepdims=True)

    @pl.when(step == steps - 1)
    def _():
        total = jnp.sum(inner[...], axis=1, keepdims=True)
        if finish:
            k_pre, v_pre = k_ref[...], v_ref[...]
            k_grad, terms = norm_back(k_pre, k_gain_ref[...], turn(key_ref[...], cos_wide, -sin_wide))
            k_low, v_low = k_grad.astype(BF16), value_ref[...].astype(BF16)
            width = steps * pair * head
            out_ref[:, pl.ds(out_ref.shape[1] - 2 * head, head)] = k_low
            out_ref[:, pl.ds(out_ref.shape[1] - head, head)] = v_low
            gains_ref[1:2, :] = jnp.sum(terms, axis=0, keepdims=True)
            total = total + jnp.sum(k_low.astype(F32) * k_pre + v_low.astype(F32) * v_pre, axis=1, keepdims=True)
        inner_ref[...] = total

def attention_backward(finish, projected, upstream, heads, segs, segs_t, cos_wide, sin_wide, q_gain, k_gain):
    rows = projected.shape[0]
    head = q_gain.shape[1]
    pair = 2 if heads % 2 == 0 else 1
    fixed = lambda *shape: pl.BlockSpec(shape, lambda i: (0,) * len(shape))
    return pl.pallas_call(
        functools.partial(attention_backward_kernel, head ** -0.5, finish),
        grid=(heads // pair,),
        out_shape=[
            jax.ShapeDtypeStruct((rows, (heads + 2) * head), BF16),
            jax.ShapeDtypeStruct((rows, head), F32),
            jax.ShapeDtypeStruct((rows, head), F32),
            jax.ShapeDtypeStruct((rows, 1), F32),
            jax.ShapeDtypeStruct((2, head), F32),
        ],
        in_specs=[
            pl.BlockSpec((rows, pair * head), lambda i: (0, i)),
            pl.BlockSpec((rows, head), lambda i: (0, heads)),
            pl.BlockSpec((rows, head), lambda i: (0, heads + 1)),
            pl.BlockSpec((rows, pair * head), lambda i: (0, i)),
            fixed(1, rows), fixed(rows, 1), fixed(rows, head), fixed(rows, head), fixed(1, head), fixed(1, head),
        ],
        out_specs=[fixed(rows, (heads + 2) * head), fixed(rows, head), fixed(rows, head), fixed(rows, 1), fixed(2, head)],
        scratch_shapes=[pltpu.VMEM((rows, rows), F32), pltpu.VMEM((rows, head), BF16), pltpu.VMEM((rows, head), BF16), pltpu.VMEM((rows, head), F32)],
        compiler_params=pltpu.CompilerParams(vmem_limit_bytes=48 << 20),
        cost_estimate=pl.CostEstimate(flops=20000000000, bytes_accessed=10000000, transcendentals=0),
        name="attention_backward",
    )(projected, projected, projected, upstream, segs, segs_t, cos_wide, sin_wide, q_gain, k_gain)

def norm_kernel(in_ref, gain_ref, out_ref, scale_ref):
    wide = in_ref[...].astype(F32)
    scale = unit(wide)
    scale_ref[...] = scale
    out_ref[...] = (wide * scale * gain_ref[...]).astype(BF16)


def normalized(values, gain):
    rows, width = values.shape
    block = min(128, rows)
    return pl.pallas_call(
        norm_kernel,
        grid=(rows // block,),
        out_shape=[jax.ShapeDtypeStruct((rows, width), BF16), jax.ShapeDtypeStruct((rows, 1), F32)],
        in_specs=[
            pl.BlockSpec((block, width), lambda i: (i, 0)),
            pl.BlockSpec((1, width), lambda i: (0, 0)),
        ],
        out_specs=[
            pl.BlockSpec((block, width), lambda i: (i, 0)),
            pl.BlockSpec((block, 1), lambda i: (i, 0)),
        ],
        compiler_params=pltpu.CompilerParams(vmem_limit_bytes=32 << 20),
        cost_estimate=pl.CostEstimate(flops=2000000000, bytes_accessed=8000000, transcendentals=0),
        name="normalized",
    )(values, gain)


def norm_pieces_kernel(count, scalars_ref, *refs):
    pieces, gain_ref, out_ref, scale_ref = refs[:count], refs[count], refs[count + 1], refs[count + 2]
    width = pieces[0].shape[1]
    total = None
    for piece in pieces:
        wide = piece[...].astype(F32)
        part = jnp.sum(wide * wide, axis=1, keepdims=True)
        total = part if total is None else total + part
    scale = lax.rsqrt(total / (width * count) + EPSILON)
    scale_ref[...] = scale
    for i, piece in enumerate(pieces):
        at = pl.ds(pl.multiple_of((scalars_ref[1] + i) % count * width, width), width)
        out_ref[:, at] = (piece[...].astype(F32) * scale * gain_ref[:, at]).astype(BF16)


def normalized_pieces(pieces, offsets, rows, scalars, gain):
    count = len(pieces)
    width = pieces[0].shape[1]
    block = min(128, rows)
    return pl.pallas_call(
        functools.partial(norm_pieces_kernel, count),
        grid=(rows // block,),
        out_shape=[
            jax.ShapeDtypeStruct((rows, width * count), BF16),
            jax.ShapeDtypeStruct((rows, 1), F32),
        ],
        in_specs=[pl.BlockSpec(memory_space=pltpu.SMEM)]
        + [pl.BlockSpec((block, width), lambda i, o=o: (o // block + i, 0)) for o in offsets]
        + [pl.BlockSpec((1, width * count), lambda i: (0, 0))],
        out_specs=[
            pl.BlockSpec((block, width * count), lambda i: (i, 0)),
            pl.BlockSpec((block, 1), lambda i: (i, 0)),
        ],
        compiler_params=pltpu.CompilerParams(vmem_limit_bytes=32 << 20),
        cost_estimate=pl.CostEstimate(flops=2000000000, bytes_accessed=8000000, transcendentals=0),
        name="normalized_pieces",
    )(scalars, *pieces, gain)


def pair_kernel(first, place, experts, scalars_ref, slots_ref, slots_t_ref, mask_ref, router_ref, *refs):
    refs = list(refs)
    token_in, grad_in = refs[0:2], refs[2:4]
    weights_in = refs[4:7]
    del refs[:7]
    if not first:
        del refs[:5]
    y_out, x_out = refs[0:2], refs[2:4]
    small_out, logits_out, gates_out = refs[4:7]
    kept_out = refs[7:12]
    (token, grad, gate_w, up_w, down_w, y_buf, x_buf, rows_in, rows_grad, rows_u, rows_da, rows_db, in_sem, grad_sem, w_sem, out_sem, kept_sem) = refs[12:]
    capacity = rows_in.shape[0] // 2
    tokens, width = token.shape[1:]
    hidden = gate_w.shape[1]
    load_tok = [pltpu.make_async_copy(token_in[g], token.at[g], in_sem.at[g]) for g in range(2)]
    parts = grad_sem.shape[1]
    strip = width // parts
    load_grad = []
    for g in range(2):
        for d in range(parts):
            there = pl.multiple_of((scalars_ref[1] + d) % parts * strip, strip)
            load_grad.append(
                pltpu.make_async_copy(
                    grad_in[g].at[:, d * strip : (d + 1) * strip],
                    grad.at[g, :, pl.ds(there, strip)],
                    grad_sem.at[g, d],
                )
            )
    load_w = [
        pltpu.make_async_copy(src, dst, w_sem.at[i])
        for i, (src, dst) in enumerate(zip(weights_in, (gate_w, up_w, down_w)))
    ]
    load_tok[0].start()
    for load in load_grad[:parts]:
        load.start()
    load_tok[1].start()
    for load in load_grad[parts:]:
        load.start()
    for load in load_w:
        load.start()
    expert = scalars_ref[0]
    stores = []
    wide = min(512, width)
    step = 256 if hidden % 256 == 0 else hidden
    chosen_rows, spreads, gate_cols = [], [], []
    for g in range(2):
        load_tok[g].wait()
        logits = mm(token[g], router_ref[...])
        shifted = logits + mask_ref[g].astype(F32)
        weights = jnp.exp(shifted - jnp.max(shifted, axis=1, keepdims=True))
        gates = weights / jnp.sum(weights, axis=1, keepdims=True)
        if g == 0:
            logits_out[...] = logits
            gates_out[...] = gates
        gates_t = gates.T
        lane = lax.broadcasted_iota(jnp.int32, gates_t.shape, 0)
        gate_row = jnp.sum(jnp.where(lane == expert, gates_t, 0.0), axis=0, keepdims=True)
        chosen = lax.broadcasted_iota(jnp.int32, (capacity, tokens), 0) == slots_ref[g]
        slot_gates = jnp.sum(jnp.where(chosen, gate_row, 0.0), axis=1, keepdims=True)
        pick = jnp.where(chosen, 1.0, 0.0).astype(BF16)
        here = slice(g * capacity, (g + 1) * capacity)
        gate_cols.append(slot_gates)
        for load in load_grad[g * parts : (g + 1) * parts]:
            load.wait()

        def gather(j, _):
            at = pl.ds(pl.multiple_of(j * wide, wide), wide)
            rows_in[here, at] = mm(pick, token[g, :, at]).astype(BF16)
            rows_grad[here, at] = mm(pick, grad[g, :, at]).astype(BF16)
            return 0

        lax.fori_loop(0, width // wide, gather, 0)
    for load in load_w:
        load.wait()
    slot_gates = jnp.concatenate(gate_cols, axis=0)

    def middle(j, carry):
        dots, inner = carry
        at = pl.ds(pl.multiple_of(j * step, step), step)
        a = mm(rows_in[...], gate_w[:, at])
        b = mm(rows_in[...], up_w[:, at])
        raw = mm_nt(rows_grad[...], down_w[at, :])
        sig = 1.0 / (1.0 + jnp.exp(-a))
        silu = a * sig
        u = (silu * b).astype(BF16).astype(F32)
        dots = dots + jnp.sum(raw * u, axis=1, keepdims=True)
        du = (slot_gates * raw).astype(BF16).astype(F32)
        da = du * b * sig * (1.0 + a * (1.0 - sig))
        db = du * silu
        inner = inner + jnp.sum(da * a + db * b, axis=1, keepdims=True)
        rows_u[:, at] = (slot_gates * u).astype(BF16)
        rows_da[:, at] = da.astype(BF16)
        rows_db[:, at] = db.astype(BF16)
        return dots, inner

    nothing = jnp.zeros((2 * capacity, 1), F32)
    dots, inner = lax.fori_loop(0, hidden // step, middle, (nothing, nothing))
    kept_here = pl.ds(place * 2 * capacity, 2 * capacity)
    for i, kept_rows in enumerate((rows_in, rows_grad, rows_u, rows_da, rows_db)):
        store = pltpu.make_async_copy(kept_rows, kept_out[i].at[kept_here, :], kept_sem.at[i])
        store.start()
        stores.append(store)
    spreads = [
        jnp.where(
            lax.broadcasted_iota(jnp.int32, (tokens, capacity), 1) == slots_t_ref[g], 1.0, 0.0
        ).astype(BF16)
        for g in range(2)
    ]
    for j in range(width // wide):
        at = slice(j * wide, (j + 1) * wide)
        dx = mm_nt(rows_da[...], gate_w[at, :]) + mm_nt(rows_db[...], up_w[at, :])
        y = mm(rows_u[...], down_w[:, at])
        for i, (rows, buf, out) in enumerate(((dx, x_buf, x_out), (y, y_buf, y_out))):
            low = rows.astype(BF16)
            for g in range(2):
                here = slice(g * capacity, (g + 1) * capacity)
                buf[g, :, at] = mm(spreads[g], low[here]).astype(BF16)
                store = pltpu.make_async_copy(
                    buf.at[g, :, at], out[g].at[:, at], out_sem.at[i, g, j]
                )
                store.start()
                stores.append(store)
    small_row = lax.broadcasted_iota(jnp.int32, small_out.shape[1:], 0)
    for g in range(2):
        here = slice(g * capacity, (g + 1) * capacity)
        chosen = lax.broadcasted_iota(jnp.int32, (capacity, tokens), 0) == slots_ref[g]
        dots_row = jnp.sum(jnp.where(chosen, dots[here], 0.0), axis=0, keepdims=True)
        inner_row = jnp.sum(jnp.where(chosen, inner[here], 0.0), axis=0, keepdims=True)
        small_out[g] = jnp.where(small_row == expert, dots_row, 0.0) + jnp.where(
            small_row == experts, inner_row, 0.0
        )
    for store in stores:
        store.wait()


def expert_pair(
    place, places, capacity, experts, scalars, slots, slots_t, mask, router, tokens, grads, weights, kept
):
    rows, width = tokens[0].shape
    hidden = weights[0].shape[1]
    total = places * 2 * capacity
    anywhere = pl.BlockSpec(memory_space=pl.ANY)
    inside = pl.BlockSpec(memory_space=pltpu.VMEM)
    first = kept is None
    parts = lax.axis_size("row")
    small_rows = (experts + 8) // 8 * 8
    dense = jax.ShapeDtypeStruct((rows, width), BF16)
    kept_shapes = [jax.ShapeDtypeStruct((total, w), BF16) for w in (width, width, hidden, hidden, hidden)]
    flat = jax.ShapeDtypeStruct((rows, router.shape[1]), F32)
    out = pl.pallas_call(
        functools.partial(pair_kernel, first, place, experts),
        out_shape=[dense] * 4 + [jax.ShapeDtypeStruct((2, small_rows, rows), F32), flat, flat] + kept_shapes,
        in_specs=[pl.BlockSpec(memory_space=pltpu.SMEM)] + [inside] * 4 + [anywhere] * (7 if first else 12),
        out_specs=[anywhere] * 4 + [inside] * 3 + [anywhere] * 5,
        input_output_aliases={} if first else {12 + i: 7 + i for i in range(5)},
        scratch_shapes=[
            pltpu.VMEM((2, rows, width), BF16),
            pltpu.VMEM((2, rows, width), BF16),
            pltpu.VMEM((width, hidden), BF16),
            pltpu.VMEM((width, hidden), BF16),
            pltpu.VMEM((hidden, width), BF16),
            pltpu.VMEM((2, rows, width), BF16),
            pltpu.VMEM((2, rows, width), BF16),
            pltpu.VMEM((2 * capacity, width), BF16),
            pltpu.VMEM((2 * capacity, width), BF16),
            pltpu.VMEM((2 * capacity, hidden), BF16),
            pltpu.VMEM((2 * capacity, hidden), BF16),
            pltpu.VMEM((2 * capacity, hidden), BF16),
            pltpu.SemaphoreType.DMA((2,)),
            pltpu.SemaphoreType.DMA((2, parts)),
            pltpu.SemaphoreType.DMA((3,)),
            pltpu.SemaphoreType.DMA((2, 2, width // min(512, width))),
            pltpu.SemaphoreType.DMA((5,)),
        ],
        compiler_params=pltpu.CompilerParams(vmem_limit_bytes=56 << 20),
        cost_estimate=pl.CostEstimate(flops=36000000000, bytes_accessed=10000000, transcendentals=0),
        name="expert_pair",
    )(scalars, slots, slots_t, mask, router, *tokens, *grads, *weights, *([] if first else kept))
    return out


def route_kernel(expert_ref, routes_ref, mask_ref, slots_ref, slots_t_ref):
    rows, top_count = routes_ref.shape[1:]
    routes = routes_ref[0]
    lanes = lax.broadcasted_iota(jnp.int32, (rows, LANES), 1)
    chosen = routes[:, 0:1] == lanes
    for k in range(1, top_count):
        chosen = jnp.logical_or(chosen, routes[:, k : k + 1] == lanes)
    mask_ref[0] = jnp.where(chosen, 0.0, MASKED).astype(BF16)
    below = lax.broadcasted_iota(jnp.int32, (rows, rows), 1) <= lax.broadcasted_iota(
        jnp.int32, (rows, rows), 0
    )
    ones = jnp.where(chosen, 1.0, 0.0)
    ranks = mm(jnp.where(below, 1.0, 0.0).astype(BF16), ones.astype(BF16))
    slots = jnp.where(chosen, ranks - 1.0, -1.0)
    here = lanes == expert_ref[0]
    slots_t_ref[0] = jnp.max(jnp.where(here, slots, -1.0), axis=1, keepdims=True).astype(jnp.int32)
    lane_first = lax.broadcasted_iota(jnp.int32, (LANES, rows), 0)
    slots_ref[0] = jnp.max(
        jnp.where(lane_first == expert_ref[0], slots.T, -1.0), axis=0, keepdims=True
    ).astype(jnp.int32)


def route_tables(scalars, routes):
    blocks, rows, top_count = routes.shape
    return pl.pallas_call(
        route_kernel,
        grid=(blocks,),
        out_shape=[
            jax.ShapeDtypeStruct((blocks, rows, LANES), BF16),
            jax.ShapeDtypeStruct((blocks, 1, rows), jnp.int32),
            jax.ShapeDtypeStruct((blocks, rows, 1), jnp.int32),
        ],
        in_specs=[
            pl.BlockSpec(memory_space=pltpu.SMEM),
            pl.BlockSpec((1, rows, top_count), lambda i: (i, 0, 0)),
        ],
        out_specs=[
            pl.BlockSpec((1, rows, LANES), lambda i: (i, 0, 0)),
            pl.BlockSpec((1, 1, rows), lambda i: (i, 0, 0)),
            pl.BlockSpec((1, rows, 1), lambda i: (i, 0, 0)),
        ],
        compiler_params=pltpu.CompilerParams(vmem_limit_bytes=32 << 20),
        cost_estimate=pl.CostEstimate(flops=1000000000, bytes_accessed=1000000, transcendentals=0),
        name="route_tables",
    )(scalars, routes)


def place_kernel(axis, starts_ref, *refs):
    out = refs[-1]
    for i, piece in enumerate(refs[:-1]):
        width = piece.shape[axis]
        at = pl.ds(pl.multiple_of(starts_ref[i] * width, width), width)
        if axis == 0:
            out[at, :] = piece[...]
        else:
            out[:, at] = piece[...]


def placed(pieces, starts, axis):
    shape = list(pieces[0].shape)
    shape[axis] *= len(pieces)
    inside = pl.BlockSpec(memory_space=pltpu.VMEM)
    return pl.pallas_call(
        functools.partial(place_kernel, axis),
        out_shape=jax.ShapeDtypeStruct(tuple(shape), pieces[0].dtype),
        in_specs=[pl.BlockSpec(memory_space=pltpu.SMEM)] + [inside] * len(pieces),
        out_specs=inside,
        compiler_params=pltpu.CompilerParams(vmem_limit_bytes=32 << 20),
        cost_estimate=pl.CostEstimate(flops=1000000, bytes_accessed=10000000, transcendentals=0),
        name="placed",
    )(starts, *pieces)


def pieces_kernel(counts, own_ref, *refs):
    out_ref = refs[-1]
    step, start = pl.program_id(0), 0
    for count, piece in zip(counts, refs[:-1]):

        @pl.when(jnp.logical_and(step >= start, step < start + count))
        def _():
            out_ref[...] = own_ref[...].astype(F32) + piece[...].astype(F32)

        start += count


def pieces_sum(own, pieces):
    rows, width = own.shape
    block = math.gcd(*[piece.shape[0] for piece in pieces])
    counts = [piece.shape[0] // block for piece in pieces]
    specs, start = [pl.BlockSpec((block, width), lambda i: (i, 0))], 0
    for count in counts:
        specs.append(
            pl.BlockSpec(
                (block, width), lambda i, s=start, c=count: (jnp.clip(i - s, 0, c - 1), 0)
            )
        )
        start += count
    return pl.pallas_call(
        functools.partial(pieces_kernel, counts),
        grid=(rows // block,),
        out_shape=jax.ShapeDtypeStruct((rows, width), F32),
        in_specs=specs,
        out_specs=pl.BlockSpec((block, width), lambda i: (i, 0)),
        compiler_params=pltpu.CompilerParams(vmem_limit_bytes=32 << 20),
        cost_estimate=pl.CostEstimate(flops=4000000000, bytes_accessed=12000000, transcendentals=0),
        name="pieces_sum",
    )(own, *pieces)


def grads_kernel(rows_ref, *refs):
    half = len(refs) // 2
    for grad_ref, out_ref in zip(refs[:half], refs[half:]):
        out_ref[...] = mm_tn(rows_ref[...], grad_ref[...]).astype(BF16)


def grads_of(rows_in, *grads):
    count, width = rows_in.shape
    hidden = grads[0].shape[1]
    block = min(512, width)
    return pl.pallas_call(
        grads_kernel,
        grid=(width // block,),
        out_shape=[jax.ShapeDtypeStruct((width, hidden), BF16)] * len(grads),
        in_specs=[pl.BlockSpec((count, block), lambda i: (0, i))]
        + [pl.BlockSpec((count, hidden), lambda i: (0, 0))] * len(grads),
        out_specs=[pl.BlockSpec((block, hidden), lambda i: (i, 0))] * len(grads),
        compiler_params=pltpu.CompilerParams(vmem_limit_bytes=56 << 20),
        cost_estimate=pl.CostEstimate(flops=1000000000, bytes_accessed=1000000, transcendentals=0),
        name="grads_of",
    )(rows_in, *grads)


def grad_of(rows_u, rows_grad):
    count, hidden = rows_u.shape
    width = rows_grad.shape[1]
    block = min(512, width)
    return pl.pallas_call(
        grads_kernel,
        grid=(width // block,),
        out_shape=[jax.ShapeDtypeStruct((hidden, width), BF16)],
        in_specs=[
            pl.BlockSpec((count, hidden), lambda i: (0, 0)),
            pl.BlockSpec((count, block), lambda i: (0, i)),
        ],
        out_specs=[pl.BlockSpec((hidden, block), lambda i: (0, i))],
        compiler_params=pltpu.CompilerParams(vmem_limit_bytes=56 << 20),
        cost_estimate=pl.CostEstimate(flops=1000000000, bytes_accessed=1000000, transcendentals=0),
        name="grad_of",
    )(rows_u, rows_grad)[0]


def moved(block, axis, by):
    count = lax.axis_size(axis)
    return lax.ppermute(block, axis, [(i, (i + by) % count) for i in range(count)])


def swapped(block, axis, bit):
    count = lax.axis_size(axis)
    return lax.ppermute(block, axis, [(i, i ^ (1 << bit)) for i in range(count)])


def butterfly(values, axis):
    for bit in range(lax.axis_size(axis).bit_length() - 1):
        values = values + swapped(values, axis, bit)
    return values


def ring_pieces(block):
    count = lax.axis_size("row")
    pieces = [[block]] + [None] * (count - 1)
    from_left = from_right = block
    half = block.shape[0] // 2
    for step in range(1, count // 2):
        from_left = moved(from_left, "row", 1)
        from_right = moved(from_right, "row", -1)
        pieces[count - step] = [from_left]
        pieces[step] = [from_right]
    if count > 1:
        pieces[count // 2] = [
            moved(from_left[:half], "row", 1),
            moved(from_right[half:], "row", -1),
        ]
    return pieces


def joined(pieces, number, rows):
    blocks = []
    for piece in pieces:
        tall = piece[0].shape[0]
        if len(piece) == 1:
            blocks.append(piece[0][number * rows : (number + 1) * rows])
        elif tall >= rows:
            start = number * rows % tall
            blocks.append(piece[number * rows // tall][start : start + rows])
        else:
            whole = jnp.concatenate(piece, axis=0)
            blocks.append(whole[number * rows : (number + 1) * rows])
    return jnp.concatenate(blocks, axis=1)


def row_gather(block):
    return lax.all_gather(block, "row", axis=block.ndim - 1, tiled=True)


def row_scatter(partial):
    return lax.psum_scatter(partial, "row", scatter_dimension=1, tiled=True)


def after(value, *others):
    return lax.optimization_barrier((value,) + others)[0]


class Link:
    def __init__(self):
        self.last = ()

    def moved(self, block, by):
        block = moved(after(block, *self.last), "col", by)
        self.last = (block,)
        return block


class PairLink:
    def __init__(self):
        self.last = ()

    def swapped(self, block):
        block = swapped(after(block, *self.last), "dp", 0)
        self.last = (block,)
        return block


def col_gather(block, link):
    count = lax.axis_size("col")
    pieces = []
    for step in range(count // 2):
        same = block if step == 0 else link.moved(block, 2 * step)
        pieces += [same, swapped(same, "col", 0)]
    return pieces


def added(*parts):
    total = parts[0].astype(F32)
    for part in parts[1:]:
        total = total + part.astype(F32)
    return total.astype(parts[0].dtype)


def chips_total(totals, link, *others):
    parts = list(totals[0])
    for step in range(1, len(totals)):
        parts.append(after(link.moved(added(*totals[step]), -2 * step), *others))
    return added(*parts)


def col_order():
    count = lax.axis_size("col")
    place = lax.axis_index("col")
    chip, core = place // 2, place % 2
    order = []
    for step in range(count // 2):
        back = (chip - step) % (count // 2) * 2
        order += [back + core, back + 1 - core]
    return order


def col_assemble(block, axis, link):
    return placed(col_gather(block, link), jnp.stack(col_order()).astype(jnp.int32), axis)


def col_share(partial, axis, link):
    count = lax.axis_size("col")
    width = partial.shape[axis] // count
    pieces = [
        lax.dynamic_slice_in_dim(partial, place * width, width, axis)
        for place in col_order()
    ]
    return chips_total(
        [
            (pieces[2 * step], swapped(pieces[2 * step + 1], "col", 0))
            for step in range(count // 2)
        ],
        link,
    )


def positions(segment_ids):
    places = jnp.arange(segment_ids.shape[0], dtype=jnp.int32)
    earlier = jnp.concatenate([segment_ids[:1] - 1, segment_ids[:-1]])
    starts = jnp.logical_or(segment_ids != earlier, places % SEQUENCE_TOKENS == 0)
    opening = lax.cummax(jnp.where(starts, places, 0), axis=0)
    return places - opening


def rotary(places, head_size):
    halfway = head_size // 2
    frequency = ROPE_BASE ** (-2.0 * jnp.arange(halfway, dtype=F32) / head_size)
    angles = places.astype(F32)[:, None] * frequency[None, :]
    cos_part, sin_part = jnp.cos(angles), jnp.sin(angles)
    return (
        jnp.concatenate([cos_part, cos_part], axis=1),
        jnp.concatenate([-sin_part, sin_part], axis=1),
    )


def turn_plain(values, cos_wide, sin_wide):
    return values * cos_wide + jnp.roll(values, values.shape[1] // 2, 1) * sin_wide


def per_device(
    residual,
    segments,
    routes,
    norm_attention,
    query_weight,
    key_projection_matrix,
    value_projection_matrix,
    query_gain,
    key_gain,
    out_weight,
    norm_experts,
    router_weight,
    gate_weight,
    up_weight,
    down_weight,
    grad_output,
):
    row_count = lax.axis_size("row")
    col_count = lax.axis_size("col")
    row_place = lax.axis_index("row")
    col_place = lax.axis_index("col")
    model_width = norm_attention.shape[0]
    feature_width = model_width // row_count
    head_size = query_gain.shape[0]
    heads_here = query_weight.shape[1] // head_size
    query_width = heads_here * head_size
    kv_heads = key_projection_matrix.shape[1] // head_size
    query_group_width = heads_here * row_count // kv_heads
    members = query_group_width // heads_here
    kv_index = row_place * heads_here // query_group_width
    member_place = row_place % members
    share_width = head_size // members
    column_mask = (jnp.arange(head_size, dtype=jnp.int32) // share_width == member_place).astype(
        F32
    )
    experts = gate_weight.shape[0] * row_count * col_count
    expert = row_place * col_count + col_place
    chips = col_count // 2
    token_rows = residual.shape[0]
    rows = SEQUENCE_TOKENS
    chunks = token_rows // rows
    top_count = routes.shape[1]
    capacity = max(2, 5 * rows * top_count // (4 * experts))
    row_start = row_place * feature_width
    labels = jnp.arange(experts, dtype=jnp.int32)
    scalars = jnp.stack([expert, row_place]).astype(jnp.int32)
    key_part = lax.dynamic_slice_in_dim(key_projection_matrix, kv_index * head_size, head_size, 1)
    value_part = lax.dynamic_slice_in_dim(
        value_projection_matrix, kv_index * head_size, head_size, 1
    )

    def chunk(array, number):
        return array[number * rows : (number + 1) * rows]

    link = Link()
    inputs_full = [row_gather(chunk(residual, n)) for n in range(chunks)]
    projection = col_assemble(
        jnp.concatenate([query_weight, key_part, value_part], axis=1), 0, link
    )
    routes_all = jnp.stack(col_gather(routes, link)).reshape(col_count * chunks, rows, top_count)
    out_full = col_assemble(out_weight, 1, link)
    grads_cols = [None] * chunks
    grad_pieces = ring_pieces(grad_output)
    grads_near = [piece[0] for piece in grad_pieces[1:] if len(piece) == 1]
    grads_middle = [block for piece in grad_pieces if len(piece) > 1 for block in piece]
    for n in range(chunks):
        grads_cols[n] = col_gather(joined(grad_pieces, n, rows), link)
    grads_far = [[g for g in grads_cols[n][2::2]] for n in range(chunks)]

    gain_one = lax.dynamic_slice_in_dim(norm_attention, row_start, feature_width)
    gain_two = lax.dynamic_slice_in_dim(norm_experts, row_start, feature_width)
    router_rows = lax.dynamic_slice_in_dim(router_weight, row_start, feature_width, 0)
    router = jnp.pad(router_weight, ((0, 0), (0, LANES - experts)))
    cos_all, sin_all = rotary(positions(segments), head_size)
    tables = [(chunk(cos_all, n), chunk(sin_all, n)) for n in range(chunks)]
    segs = [(chunk(segments, n)[None, :], chunk(segments, n)[:, None]) for n in range(chunks)]
    head_gains = (query_gain[None, :], key_gain[None, :])
    state = [{} for _ in range(chunks)]

    for n in range(chunks):
        s = state[n]
        s["normed_full"], s["scale_one"] = normalized(inputs_full[n], norm_attention[None, :])
        normed = s["normed_full"] if n == 0 else after(s["normed_full"], *grads_near)
        s["projected"] = mm(normed, projection)
        s["mixed"] = attention_forward(
            s["projected"], heads_here, *segs[n], *tables[n], *head_gains
        )
        partial = mm(s["mixed"], out_full).astype(BF16)
        s["mixed_out"] = partial
    masks, slots, slots_t = (
        table.reshape(col_count, chunks, *table.shape[1:])
        for table in route_tables(scalars, after(routes_all, partial))
    )

    kept = None

    def run_pair(n, place, *others):
        nonlocal kept
        s = state[n]
        two = slice(2 * place, 2 * place + 2)
        found = expert_pair(
            n * chips + place,
            chunks * chips,
            capacity,
            experts,
            scalars,
            slots[two, n],
            slots_t[two, n],
            masks[two, n],
            after(router, *others),
            s["tokens"][two],
            grads_cols[n][two],
            (gate_weight[0], up_weight[0], down_weight[0]),
            kept,
        )
        kept = found[7:]
        for name, same, other in (
            ("y", found[0], found[1]),
            ("x", found[2], found[3]),
            ("small", found[4][0], found[4][1]),
        ):
            other = swapped(other, "col", 0)
            s.setdefault(name, []).append(
                (same, other) if place == 0 else (added(same, other),)
            )
        if place == 0:
            s["logits"], s["gates"] = found[5][:, :experts], found[6][:, :experts]

    def hidden_of(n, ready, *others):
        s = state[n]
        summed = row_scatter(after(s["mixed_out"], *ready))
        s["hidden"] = chunk(residual, n).astype(F32) + after(summed, *others).astype(F32)
        s["wide"] = row_gather(after(s["hidden"].astype(BF16), masks))

    def second_norm(n, *others):
        s = state[n]
        s["normed_two"], s["scale_two"] = normalized(
            after(s["wide"], *others), norm_experts[None, :]
        )
        own = s["normed_two"]
        s["tokens"] = [own, swapped(own, "col", 0)]
        s["far"] = [link.moved(own, 2 * step) for step in range(1, chips)]

    def far_tokens(n, *others):
        for block in state[n]["far"]:
            same = after(block, *others)
            state[n]["tokens"] += [same, swapped(same, "col", 0)]

    def to_row(n, *others):
        s = state[n]
        s["small"] = butterfly(chips_total(s["small"], link), "row")
        s["total"] = chips_total(s["x"], link, *others)

    hidden_of(0, (), *grads_middle)
    second_norm(0, *grads_far[0], *grads_far[-1])
    for n in range(chunks):
        s = state[n]
        run_pair(n, 0, *([x[0] for x in state[n - 1]["x"][1:]] if n > 0 else []))
        spacer = s["small"][0][1]
        far_tokens(n, spacer)
        if n + 1 < chunks:
            hidden_of(n + 1, (s["wide"],), spacer)
        for place in range(1, chips):
            run_pair(n, place, spacer)
        if n > 0:
            to_row(n - 1, s["small"][-1][0])
        if n + 1 < chunks:
            second_norm(n + 1, s["small"][-1][0])
    pair = PairLink()
    own_grads, other_grads = [], []

    def expert_grads():
        grad_down = grad_of(kept[2], kept[1])
        grad_gate, grad_up = grads_of(after(kept[0], grad_down), kept[3], kept[4])
        own_grads.extend((grad_gate, grad_up, grad_down))
        wide, deep = grad_gate.shape[0], grad_down.shape[0]
        first, middle = wide // 8, wide // 2
        cuts = [(0, 0, first), (2, 0, deep // 2), (2, deep // 2, deep), (0, first, middle)]
        cuts += [(0, middle, wide), (1, 0, wide // 2), (1, wide // 2, wide)]
        for i, low, high in cuts:
            other_grads.append(pair.swapped(own_grads[i][low:high]))
        return other_grads[:1]

    acc_router = jnp.zeros((feature_width, experts), F32)
    acc_gain_two = jnp.zeros((feature_width,), F32)
    for n in range(chunks):
        s = state[n]
        if n == chunks - 1:
            to_row(n, *expert_grads())
        normed_two_grad = row_scatter(s["total"])
        hidden = s["hidden"]
        gate_dots = s["small"][:experts].T
        slot_inner = s["small"][experts]
        pick_grad = s["gates"] * (
            gate_dots - jnp.sum(s["gates"] * gate_dots, axis=1, keepdims=True)
        )
        logit_grad = pick_grad.astype(BF16)
        shard = lax.dynamic_slice_in_dim(s["normed_two"], row_start, feature_width, 1)
        acc_router = acc_router + lax.dot_general(
            shard, logit_grad, TN, preferred_element_type=F32
        )
        normed_two_grad = normed_two_grad.astype(F32) + lax.dot_general(
            logit_grad, router_rows, NT, preferred_element_type=F32
        )
        inner_two = slot_inner[:, None] + jnp.sum(
            logit_grad.astype(F32) * s["logits"], axis=1, keepdims=True
        )
        scale_two = s["scale_two"]
        s["hidden_total"] = (
            chunk(grad_output, n).astype(F32)
            + normed_two_grad * gain_two * scale_two
            - hidden * (scale_two * scale_two * inner_two / model_width)
        )
        s["branch_full"] = row_gather(s["hidden_total"].astype(BF16))
        acc_gain_two = acc_gain_two + jnp.sum(normed_two_grad * hidden * scale_two, axis=0)

    for n in range(chunks):
        state[n]["mixed_total"] = chips_total(state[n]["y"], link)

    acc_out = acc_query = acc_key = None
    acc_gain_one = jnp.zeros((model_width,), F32)
    acc_query_gain = jnp.zeros((head_size,), F32)
    acc_key_gain = jnp.zeros((head_size,), F32)
    input_blocks = []
    for n in range(chunks):
        s = state[n]
        branch_full = s["branch_full"]
        if n == chunks - 1:
            branch_full = after(branch_full, other_grads[1], state[0]["mixed_total"])
        mixed_grad = lax.dot_general(
            branch_full, out_full, NT, preferred_element_type=F32
        ).astype(BF16)
        out_here = lax.dot_general(s["mixed"], branch_full, TN, preferred_element_type=F32)
        acc_out = out_here if n == 0 else acc_out + out_here
        if n == chunks - 1:
            out_share = col_share(acc_out.astype(BF16), 1, link)
        projected_grad, key_grad, value_grad, inner_one, head_terms = attention_backward(
            members == 1, s["projected"], mixed_grad, heads_here, *segs[n], *tables[n], *head_gains
        )
        acc_query_gain = acc_query_gain + head_terms[0]
        if members == 1:
            acc_key_gain = acc_key_gain + head_terms[1]
        else:
            for bit in range(members.bit_length() - 1):
                key_grad = key_grad + swapped(key_grad, "row", bit)
                value_grad = value_grad + swapped(value_grad, "row", bit)
            key_pre = s["projected"][:, query_width : query_width + head_size]
            value_pre = s["projected"][:, query_width + head_size :]
            key_grad, key_terms = norm_back(
                key_pre, head_gains[1], turn_plain(key_grad, tables[n][0], -tables[n][1])
            )
            acc_key_gain = acc_key_gain + column_mask * jnp.sum(key_terms, axis=0)
            key_low = (column_mask * key_grad).astype(BF16)
            value_low = (column_mask * value_grad).astype(BF16)
            projected_grad = jnp.concatenate(
                [projected_grad[:, :query_width], key_low, value_low], axis=1
            )
            inner_one = inner_one + jnp.sum(
                key_low.astype(F32) * key_pre + value_low.astype(F32) * value_pre,
                axis=1,
                keepdims=True,
            )
        key_here = lax.dot_general(
            s["normed_full"], projected_grad[:, query_width:], TN, preferred_element_type=F32
        )
        acc_key = key_here if n == 0 else acc_key + key_here
        partial = lax.dot_general(
            projected_grad, projection, NT, preferred_element_type=F32
        ).astype(BF16)
        s["partial"] = partial
        normed_one_grad = row_scatter(partial)
        inner_one = butterfly(inner_one[:, 0], "row")[:, None]
        acc_gain_one = acc_gain_one + jnp.sum(
            partial.astype(F32) * s["normed_full"].astype(F32), axis=0
        )
        query_here = lax.dot_general(
            s["normed_full"], projected_grad[:, :query_width], TN, preferred_element_type=F32
        )
        acc_query = query_here if n == 0 else acc_query + query_here
        scale_one = s["scale_one"]
        if n == 0:
            normed_one_grad = after(normed_one_grad, other_grads[2], other_grads[3], state[-1]["mixed_total"])
        if n == chunks - 1:
            normed_one_grad = after(normed_one_grad, other_grads[4])
        input_blocks.append(
            s["hidden_total"]
            + normed_one_grad.astype(F32) * gain_one * scale_one
            - chunk(residual, n).astype(F32)
            * (scale_one * scale_one * inner_one / model_width)
        )

    key_share = col_share(acc_key.astype(BF16), 0, link)
    query_share = col_share(acc_query.astype(BF16), 0, link)
    for n in range(chunks):
        s = state[n]
        s["mixture"] = row_scatter(after(s["mixed_total"], state[-1]["partial"]))
    state[0]["mixture"] = after(state[0]["mixture"], *other_grads, out_share, key_share)
    out_other = pair.swapped(out_share)
    key_share = added(key_share, pair.swapped(key_share))
    shares = [jnp.concatenate(piece, axis=0) for piece in ring_pieces(key_share)]
    query_other = pair.swapped(query_share)
    state[-1]["mixture"] = after(
        state[-1]["mixture"], out_other, query_share, shares[1], shares[-1]
    )
    shares = jnp.concatenate(shares + shares, axis=1)
    shares = lax.dynamic_slice_in_dim(
        shares, (row_count - row_place) * 2 * head_size, row_count * 2 * head_size, 1
    )
    shares = shares.astype(F32).reshape(-1, kv_heads, members, 2, head_size).sum(axis=2)
    grad_key = shares[:, :, 0].reshape(-1, kv_heads * head_size)
    grad_value = shares[:, :, 1].reshape(-1, kv_heads * head_size)
    gain_two_full = lax.dynamic_update_slice_in_dim(
        jnp.zeros((model_width,), F32), acc_gain_two, row_start, 0
    )
    router_full = lax.dynamic_update_slice_in_dim(
        jnp.zeros((model_width, experts), F32), acc_router, row_start, 0
    )
    sizes = (model_width, model_width, head_size, head_size, model_width * experts)
    flat = jnp.concatenate(
        [
            acc_gain_one / norm_attention,
            gain_two_full,
            acc_query_gain,
            acc_key_gain,
            router_full.reshape(-1),
        ]
    )
    for axis in ("col", "row"):
        flat = butterfly(flat, axis)
    flat = after(flat, *[s["mixture"] for s in state])
    flat = flat + pair.swapped(flat)
    totals, start = [], 0
    for size in sizes:
        totals.append(flat[start : start + size])
        start += size
    grad_query = query_share.astype(F32) + query_other.astype(F32)
    grad_out_weight = out_share.astype(F32) + out_other.astype(F32)
    grad_gate, grad_up, grad_down = (
        pieces_sum(own, [other_grads[j] for j in parts])[None]
        for own, parts in zip(own_grads, ((0, 3, 4), (5, 6), (1, 2)))
    )
    output_blocks = [(s["hidden"] + s["mixture"].astype(F32)).astype(BF16) for s in state]
    return (
        jnp.concatenate(output_blocks, axis=0),
        jnp.concatenate(input_blocks, axis=0),
        totals[0],
        grad_query,
        grad_key,
        grad_value,
        totals[2],
        totals[3],
        grad_out_weight,
        totals[1],
        totals[4].reshape(model_width, experts),
        grad_gate,
        grad_up,
        grad_down,
    )


def solution(mesh):
    in_specs = (
        P(("dp", "col"), "row"),
        P(("dp", "col")),
        P(("dp", "col"), None),
        P(),
        P("col", "row"),
        P("col", None),
        P("col", None),
        P(),
        P(),
        P("row", "col"),
        P(),
        P(),
        P(("row", "col"), None, None),
        P(("row", "col"), None, None),
        P(("row", "col"), None, None),
        P(("dp", "col"), "row"),
    )
    out_specs = (
        P(("dp", "col"), "row"),
        P(("dp", "col"), "row"),
        P(),
        P("col", "row"),
        P("col", None),
        P("col", None),
        P(),
        P(),
        P("row", "col"),
        P(),
        P(),
        P(("row", "col"), None, None),
        P(("row", "col"), None, None),
        P(("row", "col"), None, None),
    )
    return jax.shard_map(
        per_device, mesh=mesh, in_specs=in_specs, out_specs=out_specs, check_vma=False
    )
```
